32 devices in a mesh: dp: 8 (over y, x, core), tensor: 2 (over z_hi), seq: 2 (over z_lo).
Axes of the slice: x: 2, y: 2, z: 4 (z_hi: 2, z_lo: 2; z = z_hi * 2 + z_lo), core: 2. Of those that a mesh axis runs over, the one named last changes fastest.
Arguments:
- frames: bfloat16 [8, 1500, 768], P('dp', 'seq'), may hold values from -6 to 6
- languages: int32 [8], P('dp'), may hold values from 0 to 98
- present: int32 [8], P('dp'), may hold values 0 or 1
- lang_table: bfloat16 [99, 768], replicated, may hold values from -3 to 3
- norm1_gain: bfloat16 [768], replicated, may hold values from 0.099609375 to 1.8984375
- norm1_shift: bfloat16 [768], replicated, may hold values from -2 to 2
- qkv_weight: bfloat16 [3, 768, 768], P(None, None, 'tensor'), may hold values from -0.3125 to 0.3125
- qkv_bias: bfloat16 [2, 768], P(None, 'tensor'), may hold values from -2 to 2
- out_weight: bfloat16 [768, 768], P('tensor'), may hold values from -0.625 to 0.625
- out_bias: bfloat16 [768], replicated, may hold values from -2 to 2
- norm2_gain: bfloat16 [768], replicated, may hold values from 0.099609375 to 1.8984375
- norm2_shift: bfloat16 [768], replicated, may hold values from -2 to 2
- up_weight: bfloat16 [768, 3072], P(None, 'tensor'), may hold values from -0.21875 to 0.21875
- up_bias: bfloat16 [3072], P('tensor'), may hold values from -3 to 3
- down_weight: bfloat16 [3072, 768], P('tensor'), may hold values from -0.15625 to 0.15625
- down_bias: bfloat16 [768], replicated, may hold values from -2 to 2
- grad_out: bfloat16 [8, 1500, 768], P('dp', 'seq'), may hold values from -6 to 6
Outputs:
- output: bfloat16 [8, 1500, 768], P('dp', 'seq')
- grad_frames: bfloat16 [8, 1500, 768], P('dp', 'seq')
- grad_lang_table: float32 [99, 768], replicated
- grad_norm1_gain: float32 [768], replicated
- grad_norm1_shift: float32 [768], replicated
- grad_qkv_weight: float32 [3, 768, 768], P(None, None, 'tensor')
- grad_qkv_bias: float32 [2, 768], P(None, 'tensor')
- grad_out_weight: float32 [768, 768], P('tensor')
- grad_out_bias: float32 [768], replicated
- grad_norm2_gain: float32 [768], replicated
- grad_norm2_shift: float32 [768], replicated
- grad_up_weight: float32 [768, 3072], P(None, 'tensor')
- grad_up_bias: float32 [3072], P('tensor')
- grad_down_weight: float32 [3072, 768], P('tensor')
- grad_down_bias: float32 [768], replicated
The draws below stay inside these ranges and needn't reach their ends.
Inputs may be any that keep to these rules, and one draw needn't show every extreme that they name: `languages`: a language group per clip slot, of 99. `present`: padded slots carry 0.
All inputs are finite; a program needn't handle non-finite values. No bound on the sum of `present` on one device may be relied on, other than what follows from the above.
Results may differ from the reference program's by a relative error of at most 0.013.
The reference program's roundings to bfloat16 on the way count: a program that leaves them out, or rounds other values in their place, can miss the bound.
Values may be sent and summed in bfloat16 or wider, within the bound.
A program may use at most 256 MiB of HBM per device.

```python
import jax
import jax.numpy as jnp
from jax import lax

D = 768
HEADS = 12
HEAD = 64
FF = 3072
FRAMES = 1500
LANGS = 99
CLIPS = 8


def set_ends(drawn, rng, smallest, high):
    shape = drawn.shape
    index_at = [jax.random.randint(jax.random.fold_in(rng, axis), (), 0, shape[axis]) for axis in range(len(shape))]
    drawn = drawn.at[tuple(index_at)].set(smallest)
    longest = shape.index(max(shape))
    index_at[longest] = (index_at[longest] + 1) % shape[longest]
    return drawn.at[tuple(index_at)].set(high)


def block_scale(key, shape, shards, smallest, top_value):
    def one(dim, blocks):
        steps = jax.random.uniform(jax.random.fold_in(jax.random.fold_in(key, 6), dim), (blocks,), jnp.float32, smallest / len(shards), top_value / len(shards))
        return jnp.repeat(jnp.exp(steps), shape[dim] // blocks).reshape((-1,) + (1,) * (len(shape) - dim - 1))

    loudness = one(*shards[0])
    for cut in shards[1:]:
        loudness = loudness * one(*cut)
    return loudness


def gaussian(rng, extent, deviation, most, split=(), dtype=jnp.bfloat16):
    factor_of = block_scale(rng, extent, split, -0.22, 0.18) if split else 1.0
    values = jax.random.normal(rng, extent, jnp.float32) * deviation * factor_of
    return jnp.minimum(jnp.maximum(values, -most), most).astype(dtype)


def setup_inputs(seed: int = 0) -> dict:
    streams_of = jax.random.split(jax.random.key(seed), 18)
    return {
        "frames": gaussian(streams_of[0], (CLIPS, FRAMES, D), 1.0, 6.0, ((0, 8), (1, 2))),
        "languages": set_ends(jax.random.randint(streams_of[1], (CLIPS,), 0, LANGS), jax.random.fold_in(streams_of[1], 1), 0, LANGS - 1).astype(jnp.int32),
        "present": set_ends((jax.random.randint(streams_of[2], (CLIPS,), 0, 3) < 2).astype(jnp.int32), jax.random.fold_in(streams_of[2], 1), 0, 1),
        "lang_table": gaussian(streams_of[3], (LANGS, D), 0.5, 3.0),
        "norm1_gain": jnp.clip(1.0 + 0.18 * jax.random.normal(streams_of[4], (D,), jnp.float32), 0.099609375, 1.8984375).astype(jnp.bfloat16),
        "norm1_shift": gaussian(streams_of[5], (D,), 0.3, 2.0),
        "qkv_weight": gaussian(streams_of[6], (3, D, D), (D // 2) ** -0.5, 0.3125, ((2, 2),)),
        "qkv_bias": gaussian(streams_of[7], (2, D), 0.3, 2.0, ((1, 2),)),
        "out_weight": gaussian(streams_of[8], (D, D), (D // 8) ** -0.5, 0.625, ((0, 2),)),
        "out_bias": gaussian(streams_of[9], (D,), 0.3, 2.0),
        "norm2_gain": jnp.clip(1.0 + 0.18 * jax.random.normal(streams_of[10], (D,), jnp.float32), 0.099609375, 1.8984375).astype(jnp.bfloat16),
        "norm2_shift": gaussian(streams_of[11], (D,), 0.3, 2.0),
        "up_weight": gaussian(streams_of[12], (D, FF), D ** -0.5, 0.21875, ((1, 2),)),
        "up_bias": gaussian(streams_of[13], (FF,), 0.5, 3.0, ((0, 2),)),
        "down_weight": gaussian(streams_of[14], (FF, D), (FF // 2) ** -0.5, 0.15625, ((0, 2),)),
        "down_bias": gaussian(streams_of[15], (D,), 0.3, 2.0),
        "grad_out": gaussian(streams_of[16], (CLIPS, FRAMES, D), 1.0, 6.0, ((0, 8), (1, 2))),
    }


@jax.custom_vjp
def low(v):
    return lax.optimization_barrier(v.astype(jnp.bfloat16)).astype(jnp.float32)

@jax.custom_vjp
def low_back(v):
    return v

def low_keep(v):
    return (low(v), None)

def low_pass(kept, grad):
    return (grad,)

def back_keep(v):
    return (v, None)

def back_low(kept, grad):
    return (low(grad),)
low.defvjp(low_keep, low_pass)
low_back.defvjp(back_keep, back_low)

def matmul(left, right):
    return jnp.dot(left, right, precision=lax.Precision.HIGHEST)

def layer_norm(inputs, scales, shifts):
    row_mean = lax.optimization_barrier(jnp.mean(inputs, axis=-1, keepdims=True))
    centred = inputs - row_mean
    variance = lax.optimization_barrier(jnp.mean(centred * centred, axis=-1, keepdims=True))
    return centred * lax.rsqrt(variance + 1e-05) * scales + shifts

def clip_forward(params, table_f32, clip_rows, language, keep_mask):
    gain_one, shift_one, qkv_w, qkv_b, out_w, out_b, gain_two, shift_two, up_w, up_b, down_w, down_b = params
    stream = clip_rows + table_f32[language][None, :]
    normed1 = low(layer_norm(stream, gain_one, shift_one))
    queries = low_back(low((matmul(normed1, qkv_w[0]) + qkv_b[0]) * 0.125))
    key_rows = low_back(low(matmul(normed1, qkv_w[1])))
    values = low_back(low(matmul(normed1, qkv_w[2]) + qkv_b[1]))
    query_heads = queries.reshape(FRAMES, HEADS, HEAD)
    key_heads = key_rows.reshape(FRAMES, HEADS, HEAD)
    value_heads = values.reshape(FRAMES, HEADS, HEAD)
    scores = low_back(jnp.einsum('qhd,khd->hqk', query_heads, key_heads, precision=lax.Precision.HIGHEST))
    weights = jax.nn.softmax(scores, axis=-1)
    mixed_heads = jnp.einsum('hqk,khd->qhd', low(weights), value_heads, precision=lax.Precision.HIGHEST)
    mixed_heads = low_back(low(mixed_heads.reshape(FRAMES, D)))
    hidden1 = stream + low_back(matmul(mixed_heads, out_w)) + out_b
    normed2 = low(layer_norm(hidden1, gain_two, shift_two))
    pre_act = low_back(matmul(normed2, up_w) + up_b)
    activation = low(jax.nn.gelu(pre_act, approximate=False))
    return keep_mask * (hidden1 + matmul(activation, down_w) + down_b)

def reference(frames, languages, present, lang_table, norm1_gain, norm1_shift, qkv_weight, qkv_bias, out_weight, out_bias, norm2_gain, norm2_shift, up_weight, up_bias, down_weight, down_bias, grad_out):
    params = tuple((item.astype(jnp.float32) for item in (norm1_gain, norm1_shift, qkv_weight, qkv_bias, out_weight, out_bias, norm2_gain, norm2_shift, up_weight, up_bias, down_weight, down_bias)))
    table_f32 = lang_table.astype(jnp.float32)

    def clip_step(totals, clip_item):
        clip_rows, language, keep_mask, cotangent = clip_item

        def runner(weight_set, table_in, rows_in):
            return clip_forward(weight_set, table_in, rows_in, language, keep_mask)
        result, pullback = jax.vjp(runner, params, table_f32, clip_rows.astype(jnp.float32))
        grad_params, grad_table, grad_rows = pullback(cotangent.astype(jnp.float32))
        totals = jax.tree.map(jnp.add, totals, (grad_params, grad_table))
        return (totals, (result.astype(jnp.bfloat16), grad_rows.astype(jnp.bfloat16)))
    zero_sums = jax.tree.map(jnp.zeros_like, (params, table_f32))
    totals, (output, grad_frames) = lax.scan(clip_step, zero_sums, (frames, languages, present.astype(jnp.float32), grad_out))
    grad_params, grad_table = totals
    return (output, grad_frames, grad_table, grad_params[0], grad_params[1], grad_params[2], grad_params[3], grad_params[4], grad_params[5], grad_params[6], grad_params[7], grad_params[8], grad_params[9], grad_params[10], grad_params[11])
```

```python
import jax
import jax.numpy as jnp
from jax import lax
from jax.sharding import PartitionSpec as P

HEAD = 64
EPSILON = 1e-05
QUERY_SCALE = 0.125
AXES = ("dp", "tensor", "seq")
F32 = jnp.float32
BF16 = jnp.bfloat16


class Grid:
    def __init__(self, mesh):
        self.dp, self.tp, self.sp = (mesh.shape[name] for name in AXES)
        self.pairs = self.dp // 2

    def send(self, value, target):
        moves = []
        for d in range(self.dp):
            for t in range(self.tp):
                for s in range(self.sp):
                    to = target(d, t, s)
                    if to is not None:
                        moves.append((self.flat(d, t, s), self.flat(*to)))
        return lax.ppermute(value, AXES, moves)

    def flat(self, d, t, s):
        return (d * self.tp + t) * self.sp + s

    def levels(self):
        d, s = lax.axis_index("dp"), lax.axis_index("seq")
        steps = [(lambda d, t, s: (d, t, s ^ 1), s)]
        bit = 2
        while bit < self.dp:
            steps.append((lambda d, t, s, bit=bit: (d ^ bit, t, s), (d // bit) % 2))
            bit *= 2
        return steps


def to_sibling(d, t, s):
    return (d ^ 1, t, s) if d % 2 == t else None


def swap_core(d, t, s):
    return (d ^ 1, t, s)


def over_home(d, t, s):
    return (d, 1 - t, s) if d % 2 == t else None


def over_away(d, t, s):
    return (d, 1 - t, s) if d % 2 != t else None


def gather_slices(grid, piece, where_from=None):
    current = piece
    for partner, bit in grid.levels():
        def target(d, t, s, partner=partner):
            if where_from is not None and not where_from(d, t):
                return None
            return partner(d, t, s)
        received = grid.send(current, target)
        current = jnp.where(
            bit == 1, jnp.concatenate([received, current]), jnp.concatenate([current, received])
        )
    return current


def reduce_gather(grid, grads, mine, core, slice_index):
    current = grads
    for partner, bit in reversed(grid.levels()):
        half = current.shape[0] // 2
        given = lax.dynamic_slice_in_dim(current, (1 - bit) * half, half).astype(BF16)
        kept = lax.dynamic_slice_in_dim(current, bit * half, half)
        current = kept + grid.send(given, partner).astype(F32)
    away = grid.send(current.astype(BF16), over_away)
    total = (current + away.astype(F32)).astype(BF16)
    total = jnp.where(mine, total, grid.send(total, to_sibling))
    half = total.shape[0] // 2
    part = lax.dynamic_slice_in_dim(total, core * half, half)
    part = gather_slices(grid, part)
    other = grid.send(part, swap_core)
    slices = grid.pairs * grid.sp
    a = part.reshape(slices, half, -1)
    b = other.reshape(slices, half, -1)
    whole = jnp.where(core == 0, jnp.concatenate([a, b], 1), jnp.concatenate([b, a], 1))
    return whole.reshape(grads.shape).astype(F32)


def layer_norm(inputs, scales, shifts):
    row_mean = jnp.mean(inputs, axis=-1, keepdims=True)
    centred = inputs - row_mean
    variance = jnp.mean(centred * centred, axis=-1, keepdims=True)
    return centred * lax.rsqrt(variance + EPSILON) * scales + shifts


def exact_gelu(inputs):
    return jax.nn.gelu(inputs, approximate=False)


def mm(left, right, dims):
    return lax.dot_general(left, right, (dims, ((), ())), preferred_element_type=F32)


def attend(queries, key_rows, values):
    scores = jnp.einsum("qhd,khd->hqk", queries, key_rows, preferred_element_type=F32)
    row_max = jnp.max(scores, axis=-1, keepdims=True)
    weights = jnp.exp(scores - row_max)
    row_total = jnp.sum(weights, axis=-1, keepdims=True)
    weights = weights / row_total
    mixed = jnp.einsum("hqk,khd->qhd", weights.astype(BF16), values, preferred_element_type=F32)
    return mixed, (row_max + jnp.log(row_total))[..., 0]


def attend_back(queries, key_rows, values, log_total, grad_mixed):
    scores = jnp.einsum("qhd,khd->hqk", queries, key_rows, preferred_element_type=F32)
    weights = jnp.exp(scores - log_total[..., None])
    grad_weights = jnp.einsum("qhd,khd->hqk", grad_mixed, values, preferred_element_type=F32)
    inner_sum = jnp.sum(grad_weights * weights, axis=-1, keepdims=True)
    grad_scores = (weights * (grad_weights - inner_sum)).astype(BF16)
    grad_queries = jnp.einsum("hqk,khd->qhd", grad_scores, key_rows, preferred_element_type=F32)
    grad_keys = jnp.einsum("hqk,qhd->khd", grad_scores, queries, preferred_element_type=F32)
    grad_values = jnp.einsum(
        "hqk,qhd->khd", weights.astype(BF16), grad_mixed, preferred_element_type=F32
    )
    return grad_queries, grad_keys, grad_values


def on_device(
    grid,
    frames,
    languages,
    present,
    lang_table,
    norm1_gain,
    norm1_shift,
    qkv_weight,
    qkv_bias,
    out_weight,
    out_bias,
    norm2_gain,
    norm2_shift,
    up_weight,
    up_bias,
    down_weight,
    down_bias,
    grad_out,
):
    d, t, s = (lax.axis_index(name) for name in AXES)
    core = d % 2
    pair = d // 2
    mine = core == t
    slices = grid.pairs * grid.sp
    slice_index = pair * grid.sp + s
    clip = 2 * pair + t
    _, rows, width = frames.shape
    head_width = qkv_weight.shape[2]
    heads = head_width // HEAD
    hidden = up_weight.shape[1]
    langs = lang_table.shape[0]

    def for_clip(value):
        return jnp.where(mine, value, grid.send(value, to_sibling))

    own_frames = for_clip(frames[0])
    across = grid.send(frames[0], lambda d, t, s: (d, t, 1 - s) if d % 2 == t else None)
    other_frames = for_clip(across)
    grad_rows_low = for_clip(grad_out[0])
    numbers = for_clip(jnp.concatenate([languages, present]))
    language, keep = numbers[0], numbers[1].astype(F32)

    def away_group(d, t):
        return d % 2 != t

    def weights_for(parts):
        columns = parts[0].shape[1]
        local = jnp.concatenate(parts) if len(parts) > 1 else parts[0]
        step = local.shape[0] // slices
        piece = lax.dynamic_slice_in_dim(local, slice_index * step, step)
        piece = grid.send(piece, over_home)
        full = gather_slices(grid, piece, away_group)
        full = jnp.where(mine, local, full)
        out, at = [], 0
        for part in parts:
            out.append(lax.slice_in_dim(full, at, at + part.shape[0]))
            at += part.shape[0]
        return out

    qkv_w = weights_for([qkv_weight.reshape(3 * width, head_width)])[0].reshape(3, width, head_width)
    up_l, up_r, down_w, out_w = weights_for(
        [up_weight[:, :width], up_weight[:, width:], down_weight, out_weight]
    )
    up_w = jnp.concatenate([up_l, up_r], axis=1)
    biases = jnp.concatenate([qkv_bias.reshape(-1), up_bias])
    biases = jnp.where(mine, biases, grid.send(biases, over_home)).astype(F32)
    query_bias, value_bias = biases[:head_width], biases[head_width : 2 * head_width]
    up_b = biases[2 * head_width :]

    one_hot = (language == lax.broadcasted_iota(jnp.int32, (1, langs), 1)).astype(F32)
    embedding = jnp.dot(one_hot, lang_table.astype(F32), precision=lax.Precision.HIGHEST)
    gain_one, shift_one = norm1_gain.astype(F32), norm1_shift.astype(F32)
    gain_two, shift_two = norm2_gain.astype(F32), norm2_shift.astype(F32)

    stream = own_frames.astype(F32) + embedding
    normed1, norm1_back = jax.vjp(layer_norm, stream, gain_one, shift_one)
    normed1 = normed1.astype(BF16)
    other_normed = layer_norm(other_frames.astype(F32) + embedding, gain_one, shift_one).astype(BF16)
    both = jnp.concatenate([normed1, other_normed])
    queries = ((mm(normed1, qkv_w[0], ((1,), (0,))) + query_bias) * QUERY_SCALE).astype(BF16)
    key_rows = mm(both, qkv_w[1], ((1,), (0,))).astype(BF16)
    values = (mm(both, qkv_w[2], ((1,), (0,))) + value_bias).astype(BF16)

    query_heads = queries.reshape(rows, heads, HEAD)
    key_heads = key_rows.reshape(-1, heads, HEAD)
    value_heads = values.reshape(-1, heads, HEAD)
    mixed_heads, log_total = attend(query_heads, key_heads, value_heads)
    mixed = mixed_heads.reshape(rows, head_width).astype(BF16)

    def both_cores(part):
        return part + grid.send(part, swap_core)

    attention = both_cores(mm(mixed, out_w, ((1,), (0,))))
    hidden1 = stream + attention + out_bias.astype(F32)
    normed2, norm2_back = jax.vjp(layer_norm, hidden1, gain_two, shift_two)
    normed2 = normed2.astype(BF16)
    pre_act = mm(normed2, up_w, ((1,), (0,))) + up_b
    activation, gelu_back = jax.vjp(exact_gelu, pre_act)
    activation = activation.astype(BF16)
    feed = both_cores(mm(activation, down_w, ((1,), (0,))))
    output = (keep * (hidden1 + feed + down_bias.astype(F32))).astype(BF16)

    grad_rows = keep * grad_rows_low.astype(F32)
    grad_low = grad_rows.astype(BF16)
    grad_activation = mm(grad_low, down_w, ((1,), (1,)))
    grad_pre = gelu_back(grad_activation)[0].astype(BF16)
    grad_normed2 = both_cores(mm(grad_pre, up_w, ((1,), (1,))))
    grad_hidden_norm, grad_norm2_gain, grad_norm2_shift = norm2_back(grad_normed2)
    grad_hidden1 = grad_rows + grad_hidden_norm
    grad_attn_low = grad_hidden1.astype(BF16)
    grad_mixed = mm(grad_attn_low, out_w, ((1,), (1,))).astype(BF16)

    grad_down = mm(activation, grad_low, ((0,), (0,)))
    grad_up = mm(normed2, grad_pre, ((0,), (0,)))
    grad_outw = mm(mixed, grad_attn_low, ((0,), (0,)))
    early = jnp.concatenate([grad_up[:, :width], grad_up[:, width:], grad_down, grad_outw])
    early = reduce_gather(grid, early, mine, core, slice_index)

    grad_query_heads, grad_key_heads, grad_value_heads = attend_back(
        query_heads, key_heads, value_heads, log_total, grad_mixed.reshape(rows, heads, HEAD)
    )
    grad_kv = jnp.stack(
        [grad_key_heads.reshape(-1, head_width), grad_value_heads.reshape(-1, head_width)]
    )
    grad_kv_other = grid.send(grad_kv[:, rows:].astype(BF16), lambda d, t, s: (d, t, 1 - s))
    grad_kv_low = (grad_kv[:, :rows] + grad_kv_other.astype(F32)).astype(BF16)
    grad_query_low = grad_query_heads.reshape(rows, head_width).astype(BF16)
    grad_query_pre = (grad_query_low.astype(F32) * QUERY_SCALE).astype(BF16)
    stacked = jnp.concatenate([grad_query_pre[None], grad_kv_low])
    grad_qkv = jnp.einsum("fd,jfe->jde", normed1, stacked, preferred_element_type=F32)
    late = reduce_gather(grid, grad_qkv.reshape(3 * width, head_width), mine, core, slice_index)
    grad_normed1 = both_cores(
        jnp.einsum("jfe,jde->fd", stacked, qkv_w, preferred_element_type=F32)
    )
    grad_stream_norm, grad_norm1_gain, grad_norm1_shift = norm1_back(grad_normed1)
    grad_stream = grad_hidden1 + grad_stream_norm
    grad_frames = grad_stream.astype(BF16)

    def to_place(value):
        return jnp.where(mine, value, grid.send(value, over_home))

    output = to_place(output)
    grad_frames = to_place(grad_frames)

    clips = grid.dp
    clip_hot = (clip == lax.broadcasted_iota(jnp.int32, (clips, 1), 0)).astype(F32)
    lang_rows = clip_hot * jnp.sum(grad_stream, axis=0, keepdims=True)
    once = jnp.where(s == 0, 1.0, 0.0)
    lang_ids = jnp.broadcast_to(clip_hot * language.astype(F32) * once, (clips, width))
    query_sum = jnp.sum(grad_query_pre.astype(F32), axis=0)
    value_sum = jnp.sum(grad_kv_low[1].astype(F32), axis=0)
    pack = jnp.concatenate(
        [
            lang_rows,
            lang_ids,
            jnp.stack(
                [
                    grad_norm1_gain,
                    grad_norm1_shift,
                    jnp.sum(grad_hidden1, axis=0),
                    grad_norm2_gain,
                    grad_norm2_shift,
                    jnp.sum(grad_rows, axis=0),
                    jnp.concatenate([query_sum, value_sum]),
                ]
            ),
            jnp.sum(grad_pre.astype(F32), axis=0).reshape(-1, width),
        ]
    )
    for partner, _ in grid.levels():
        pack = pack + grid.send(pack, partner)
    pack = pack + grid.send(pack, lambda d, t, s: (d, 1 - t, s))
    halves = pack[2 * clips + 6 :]
    halves = jnp.where(mine, halves, grid.send(halves, to_sibling))
    ids = pack[clips : 2 * clips, :1]
    hot = (ids == lax.broadcasted_iota(jnp.int32, (1, langs), 1).astype(F32)).astype(F32)
    grad_lang_table = lax.dot_general(
        hot, pack[:clips], (((0,), (0,)), ((), ())), precision=lax.Precision.HIGHEST
    )
    v = pack[2 * clips :]
    return (
        output[None],
        grad_frames[None],
        grad_lang_table,
        v[0],
        v[1],
        late.reshape(3, width, head_width),
        halves[0].reshape(2, head_width),
        early[2 * width + hidden :],
        v[2],
        v[3],
        v[4],
        jnp.concatenate([early[:width], early[width : 2 * width]], axis=1),
        halves[1:].reshape(-1),
        early[2 * width : 2 * width + hidden],
        v[5],
    )


def solution(mesh):
    grid = Grid(mesh)
    placed = (
        P("dp", "seq", None),
        P("dp"),
        P("dp"),
        P(),
        P(),
        P(),
        P(None, None, "tensor"),
        P(None, "tensor"),
        P("tensor", None),
        P(),
        P(),
        P(),
        P(None, "tensor"),
        P("tensor"),
        P("tensor", None),
        P(),
        P("dp", "seq", None),
    )
    return jax.shard_map(
        lambda *arrays: on_device(grid, *arrays),
        mesh=mesh,
        in_specs=placed,
        out_specs=(
            P("dp", "seq", None),
            P("dp", "seq", None),
            P(),
            P(),
            P(),
            P(None, None, "tensor"),
            P(None, "tensor"),
            P("tensor", None),
            P(),
            P(),
            P(),
            P(None, "tensor"),
            P("tensor"),
            P("tensor", None),
            P(),
        ),
        check_vma=False,
    )
```

```python
import functools
import types

import jax
import jax.numpy as jnp
from jax import lax
from jax.experimental import pallas as pl
from jax.experimental.pallas import tpu as pltpu
from jax.sharding import PartitionSpec as P

HEAD = 64
EPSILON = 1e-05
QUERY_SCALE = 0.125
AXES = ("dp", "tensor", "seq")
F32 = jnp.float32
BF16 = jnp.bfloat16
NN = (((1,), (0,)), ((), ()))
NT = (((1,), (1,)), ((), ()))
TN = (((0,), (0,)), ((), ()))
VMEM = pl.BlockSpec(memory_space=pltpu.VMEM)
ANY = pl.BlockSpec(memory_space=pl.ANY)
RS = 3


def dg(left, right, dims):
    return lax.dot_general(left, right, dims, preferred_element_type=F32)


def rows_at(start, size):
    return pl.ds(pl.multiple_of(start, 16), size)


class Place:
    def __init__(self, dp):
        self.d, self.t, self.s = (lax.axis_index(name) for name in AXES)
        self.core = lax.rem(self.d, 2)
        self.home = self.core == self.t
        self.away = jnp.logical_not(self.home)
        self.clip = self.d - self.core + self.t
        self.sibling = (self.d + 1 - 2 * self.core, self.t, self.s)
        self.across = (self.d, 1 - self.t, self.s)
        self.level = [((self.d, self.t, 1 - self.s), self.s)]
        bit = 2
        while bit < dp:
            value = lax.rem(self.d // bit, 2)
            self.level.append(((self.d + bit - 2 * bit * value, self.t, self.s), value))
            bit *= 2
        self.peers = [self.sibling, self.across] + [to for to, _ in self.level]

    def enter(self):
        barrier = pltpu.get_barrier_semaphore()
        for to in self.peers:
            pl.semaphore_signal(barrier, inc=1, device_id=to, device_id_type=pl.DeviceIdType.MESH)
        pl.semaphore_wait(barrier, len(self.peers))

    def order(self, part):
        levels = [self.level[(part + j) % RS] for j in range(RS)]
        return [to for to, _ in levels], [bit for _, bit in levels]


class Wires:
    def __init__(self, send_sems, recv_sems):
        self.send_sems, self.recv_sems, self.used = send_sems, recv_sems, 0

    def copy(self, src, dst, to):
        i = self.used
        self.used += 1
        return pltpu.make_async_remote_copy(
            src_ref=src,
            dst_ref=dst,
            send_sem=self.send_sems.at[i],
            recv_sem=self.recv_sems.at[i],
            device_id=to,
            device_id_type=pl.DeviceIdType.MESH,
        )


class Fetch:
    def __init__(self, place, wires, part, local, result):
        self.to, self.bits = place.order(part)
        self.place, self.wires, self.result = place, wires, result
        self.slice = local.shape[0] // 2**RS
        self.at = self.slice * (4 * self.bits[0] + 2 * self.bits[1] + self.bits[2])
        at = rows_at(self.at, self.slice)
        self.crossing = wires.copy(local.at[at], result.at[at], place.across)

        @pl.when(place.home)
        def _():
            self.crossing.start()

    def widen(self, j):
        size = self.slice * 2 ** (RS - 1 - j)
        ref = self.result.at[rows_at(self.at, size)]
        self.at = self.at - self.bits[j] * size
        return self.wires.copy(ref, ref, self.to[j])

    def arrive(self):
        self.moving = self.widen(RS - 1)

        @pl.when(self.place.home)
        def _():
            self.crossing.wait_send()

        @pl.when(self.place.away)
        def _():
            self.crossing.wait_recv()
            self.moving.start()

    def double(self, j):
        before = self.moving
        if j:
            self.moving = self.widen(j - 1)

        @pl.when(self.place.away)
        def _():
            before.wait()
            if j:
                self.moving.start()


class Reduction:
    def __init__(self, place, wires, part, kept, given, stages, lands, result):
        self.to, self.bits = place.order(part)
        self.extra = place.level[RS:]
        self.place, self.wires, self.kept, self.given = place, wires, kept, given
        self.stages, self.lands, self.result = stages, lands, result
        self.slice = result.shape[0] // 2**RS
        self.low = 0
        self.at = self.bits[0] * 4 * self.slice
        self.forwards = []

    def start(self):
        self.moving = self.wires.copy(self.given, self.lands[0], self.to[0])
        self.moving.start()

    def halve(self, j):
        self.moving.wait()
        half = self.slice * 2 ** (RS - 2 - j)
        if j == RS - 1:
            now = rows_at(self.low, self.slice)
            self.kept[now, :] += self.lands[j][...].astype(F32)
            return
        bit = self.bits[j + 1]
        away, home = (1 - bit) * half, bit * half
        self.stages[j][...] = (
            self.kept[rows_at(self.low + away, half), :]
            + self.lands[j][rows_at(away, half), :].astype(F32)
        ).astype(BF16)
        self.moving = self.wires.copy(self.stages[j], self.lands[j + 1], self.to[j + 1])
        self.moving.start()
        self.kept[rows_at(self.low + home, half), :] += self.lands[j][
            rows_at(home, half), :
        ].astype(F32)
        self.low = self.low + home
        self.at = self.at + home

    def cross(self):
        now = rows_at(self.low, self.slice)
        stage = self.stages[RS - 1]
        for number, (to, _) in enumerate(self.extra):
            land = self.lands[RS + 1 + number]
            stage[...] = self.kept[now, :].astype(BF16)
            copy = self.wires.copy(stage, land, to)
            copy.start()
            copy.wait()
            self.kept[now, :] = stage[...].astype(F32) + land[...].astype(F32)
        self.crossing = self.wires.copy(stage, self.lands[RS], self.place.across)

        @pl.when(self.place.away)
        def _():
            stage[...] = self.kept[now, :].astype(BF16)
            self.crossing.start()

    def spread(self, start, size):
        ref = self.result.at[rows_at(start, size)]
        forward = self.wires.copy(ref, ref, self.place.sibling)
        self.forwards.append(forward)
        return forward

    def widen(self, j):
        ref = self.result.at[rows_at(self.at, self.slice * 2 ** (RS - 1 - j))]
        return self.wires.copy(ref, ref, self.to[j])

    def land(self):
        first = self.spread(self.at, self.slice)
        self.moving = self.widen(RS - 1)

        @pl.when(self.place.home)
        def _():
            self.crossing.wait_recv()
            self.result[rows_at(self.at, self.slice), :] = (
                self.kept[rows_at(self.low, self.slice), :] + self.lands[RS][...].astype(F32)
            ).astype(BF16)
            self.moving.start()
            first.start()

        @pl.when(self.place.away)
        def _():
            self.crossing.wait_send()

    def double(self, j):
        size = self.slice * 2 ** (RS - 1 - j)
        bit = self.bits[j]
        came = self.at + (1 - 2 * bit) * size
        self.at = self.at - bit * size
        before, forward = self.moving, self.spread(came, size)
        if j:
            self.moving = self.widen(j - 1)

        @pl.when(self.place.home)
        def _():
            before.wait()
            if j:
                self.moving.start()
            forward.start()

    def finish(self):
        @pl.when(self.place.home)
        def _():
            for forward in self.forwards:
                forward.wait_send()

        @pl.when(self.place.away)
        def _():
            for forward in self.forwards:
                forward.wait_recv()


def pair_lanes(rows):
    return lax.broadcasted_iota(jnp.int32, (rows, 128), 1)


def one_head(pair, e, extra=None):
    lane = pair_lanes(pair.shape[0])
    own = (lane < HEAD) if e == 0 else (lane >= HEAD)
    kept = jnp.where(own, pair, jnp.zeros_like(pair))
    if extra is not None:
        kept = jnp.where(lane == (HEAD if e == 0 else 0), extra, kept)
    return kept


def masked_keys(key_ref, columns, masked, rows, valid):
    row = lax.broadcasted_iota(jnp.int32, (rows, 128), 0)
    bias = jnp.where(row >= valid, -1e30, 0.0).astype(BF16)
    for e in range(2):
        for part in range(2):
            at = pl.ds(part * rows, rows)
            masked[e, at, :] = one_head(key_ref[at, columns], e, bias)


def centre(inputs):
    centred = inputs - jnp.mean(inputs, axis=1, keepdims=True)
    scale = lax.rsqrt(jnp.mean(centred * centred, axis=1, keepdims=True) + EPSILON)
    return centred * scale, scale


def call(kernel, name, collective, ins, outs, scratch, hbm, cost):
    names = list(ins) + list(outs) + list(scratch)

    def body(*refs):
        named = dict(zip(names, refs))
        plain = {name: ref for name, ref in named.items() if isinstance(name, str)}
        kernel(types.SimpleNamespace(table=named, **plain))

    results = pl.pallas_call(
        body,
        out_shape=[jax.ShapeDtypeStruct(*item) for item in outs.values()],
        in_specs=[ANY if item in hbm else VMEM for item in ins],
        out_specs=[ANY if item in hbm else VMEM for item in outs],
        scratch_shapes=list(scratch.values()),
        compiler_params=pltpu.CompilerParams(
            collective_id=collective, has_side_effects=True, vmem_limit_bytes=60 * 2**20
        ),
        cost_estimate=cost,
        name=name,
    )(*ins.values())
    return types.SimpleNamespace(**dict(zip(outs, results)))


def forward_kernel(dp, valid, r):
    place = Place(dp)
    place.enter()
    wires = Wires(r.send_sems, r.recv_sems)
    rows, wide = r.frames.shape
    width = r.query.shape[1]
    home, away = place.home, place.away
    chunk = rows // 3

    first = [Fetch(place, wires, j, r.qkv_local.at[j], r.qkv.at[j]) for j in range(3)]
    info = wires.copy(r.info_local, r.info, place.sibling)
    bias = wires.copy(r.bias_local, r.bias, place.across)
    own = wires.copy(r.frames, r.own, place.sibling)
    beside, onward = [], []
    for c in range(3):
        at = pl.ds(c * chunk, chunk)
        beside.append(wires.copy(r.frames.at[at], r.other.at[at], place.level[0][0]))
        onward.append(wires.copy(r.other.at[at], r.other.at[at], place.sibling))
    grads = wires.copy(r.grad_local, r.grad_rows, place.sibling)
    keep = [
        pltpu.make_async_copy(src, dst, r.local_sems.at[i])
        for i, (src, dst) in enumerate(
            (
                (r.qkv_local, r.qkv),
                (r.grad_local, r.grad_rows),
                (r.up_local, r.up),
                (r.down_local, r.down),
                (r.out_local, r.out),
            )
        )
    ]
    lend = pltpu.make_async_copy(r.out_local, r.out_other, r.local_sems.at[len(keep)])
    lent = wires.copy(r.out, r.out_other, place.sibling)

    @pl.when(home)
    def _():
        info.start()
        bias.start()
        own.start()
        for copy in beside:
            copy.start()
        for copy in keep:
            copy.start()
        r.info[...] = r.info_local[...]
        r.bias[...] = r.bias_local[...]
        r.own[...] = r.frames[...]

    @pl.when(away)
    def _():
        lend.start()

    later = []
    for part in range(RS):
        for local, result in ((r.down_local, r.down), (r.up_local, r.up), (r.out_local, r.out)):
            size = local.shape[0] // RS
            at = pl.ds(part * size, size)
            later.append(Fetch(place, wires, part, local.at[at], result.at[at]))

    @pl.when(home)
    def _():
        grads.start()

    for item in first:
        item.arrive()

    @pl.when(away)
    def _():
        info.wait_recv()
        own.wait_recv()
        bias.wait_recv()

    embedding = r.info[0:1, :]

    def norm(source, c, to):
        normal, _ = centre(source[pl.ds(c * chunk, chunk), :].astype(F32) + embedding)
        normed = normal * r.gain[...] + r.shift[...]
        r.normed[pl.ds(to + c * chunk, chunk), :] = normed.astype(BF16)
        return normed

    for c in range(3):
        r.normed_t[:, c * chunk : (c + 1) * chunk] = norm(r.own, c, 0).T.astype(BF16)
        if c == 0:
            for item in first:
                item.double(2)

        @pl.when(home)
        def _():
            beside[c].wait()
            onward[c].start()

    for item in first:
        item.double(1)
    for c in range(3):

        @pl.when(away)
        def _():
            onward[c].wait_recv()

        norm(r.other, c, rows)
    for item in first:
        item.double(0)

    @pl.when(home)
    def _():
        keep[0].wait()

    r.query[...] = (
        (dg(r.normed[:rows, :], r.qkv[0], NN) + r.bias[0:1, :width]) * QUERY_SCALE
    ).astype(BF16)
    for part in range(2):
        at = pl.ds(part * rows, rows)
        r.key[at, :] = dg(r.normed[at, :], r.qkv[1], NN).astype(BF16)
        r.value[at, :] = (dg(r.normed[at, :], r.qkv[2], NN) + r.bias[0:1, width:]).astype(BF16)
    for item in later:
        item.arrive()

    block = 256
    mixed_copies = []

    def one_pair(p):
        columns = pl.ds(p * 128, 128)
        masked_keys(r.key, columns, r.masked, rows, valid)
        for j in range(3):
            r.qkv_pairs[p, :, j * 128 : (j + 1) * 128] = r.qkv[j, :, columns]

        def one_block(i, _):
            at = pl.ds(pl.multiple_of(i * block, block), block)
            parts, rests = [], []
            for e in range(2):
                queries = one_head(r.query[at, columns], e, jnp.ones((), BF16))
                scores = dg(queries, r.masked[e], NT)
                top = jnp.max(scores, axis=1, keepdims=True)
                weights = jnp.exp(scores - top)
                total = jnp.sum(weights, axis=1, keepdims=True)
                weights = weights * (1.0 / total)
                low = weights.astype(BF16)
                rest = (weights - low.astype(F32)).astype(BF16)
                parts.append(dg(low, r.value[:, columns], NN))
                rests.append(parts[-1] + dg(rest, r.value[:, columns], NN))
                r.lse[pl.ds(2 * p + e, 1), at] = (top + jnp.log(total)).reshape(1, block)
            first = pair_lanes(block) < HEAD
            r.mixed[at, columns] = jnp.where(first, parts[0], parts[1]).astype(BF16)
            r.exact[at, columns] = jnp.where(first, rests[0], rests[1])
            return 0

        lax.fori_loop(0, rows // block, one_block, 0)
        copy = wires.copy(r.mixed.at[:, columns], r.mixed_other.at[:, columns], place.sibling)
        copy.start()
        mixed_copies.append(copy)

    one_pair(0)
    for item in later:
        item.double(2)
    one_pair(1)
    for item in later:
        item.double(1)
    one_pair(2)
    for item in later:
        item.double(0)

    @pl.when(away)
    def _():
        lend.wait()
        lent.start()
        grads.wait_recv()
        lent.wait_send()

    @pl.when(home)
    def _():
        lent.wait_recv()
        for copy in keep[1:]:
            copy.wait()
        info.wait_send()
        bias.wait_send()
        own.wait_send()
        grads.wait_send()
        for copy in onward:
            copy.wait_send()

    for copy in mixed_copies:
        copy.wait()


DOWN, UP, LATE = range(3)


def backward_kernel(dp, valid, r):
    place = Place(dp)
    place.enter()
    wires = Wires(r.send_sems, r.recv_sems)
    extra = len(place.level) - RS
    rows, width = r.query.shape
    wide = r.normed_t.shape[0]
    home, away = place.home, place.away

    def part_of(kind, part):
        stages = [r.table[0, kind, part, i] for i in range(4 if kind == LATE else 3)]
        lands = [r.table[1, kind, part, i] for i in range(4 + extra)]
        return stages, lands

    out_copy = wires.copy(r.output, r.output_to, place.across)

    keep_in = pltpu.make_async_copy(r.output, r.share_stage, r.local_sem)
    keep_out = pltpu.make_async_copy(r.share_stage, r.output_to, r.local_sem)

    @pl.when(home)
    def _():
        out_copy.start()
        keep_in.start()

    early = []
    for part in range(RS):
        for kind, kept, given, result in (
            (DOWN, r.down_keep, r.down_give, r.down_sum),
            (UP, r.up_keep, r.up_give, r.up_sum),
        ):
            stages, lands = part_of(kind, part)
            early.append(
                Reduction(
                    place,
                    wires,
                    part,
                    kept.at[part],
                    given.at[part],
                    stages,
                    lands,
                    result.at[part],
                )
            )
    for item in early:
        item.start()

    def back_pair(p):
        columns = pl.ds(p * 128, 128)
        masked, scaled, plain, given = r.masked, r.scaled, r.plain, r.given
        masked_keys(r.key, columns, masked, rows, valid)
        grad = r.grad_mixed[:, columns]
        for e in range(2):
            query = r.query[:, columns]
            scaled[e] = one_head(query, e, jnp.ones((), BF16))
            plain[e] = one_head(query, e)
            given[e] = one_head(grad, e)
        block = 384

        def one_block(store, first, i, total):
            at = pl.ds(pl.multiple_of(first + i * block, block), block)
            grad_keys, grad_values = [], []
            for e in range(2):
                scores = dg(masked[e, at, :], scaled[e], NT)
                weights = jnp.exp(scores - r.lse[pl.ds(2 * p + e, 1), :])
                grad_weights = dg(r.value[at, columns], given[e], NT)
                grad_scores = (weights * (grad_weights - r.inner[pl.ds(2 * p + e, 1), :])).astype(BF16)
                grad_values.append(dg(weights.astype(BF16), given[e], NN))
                grad_keys.append(dg(grad_scores, plain[e], NN))
                total = total + dg(one_head(r.key[at, columns], e), grad_scores, TN)
            to = pl.ds(pl.multiple_of(i * block, block), block)
            store[p, to, :128] = (grad_keys[0] + grad_keys[1]).astype(store.dtype)
            store[p, to, 128:] = (grad_values[0] + grad_values[1]).astype(store.dtype)
            return total

        total = jnp.zeros((128, rows), F32)
        for store, first in ((r.kv_own, 0), (r.kv_stage, rows)):
            total = lax.fori_loop(
                0, rows // block, functools.partial(one_block, store, first), total
            )
        low = total.T.astype(BF16)
        r.stacked[p, :, :128] = (low.astype(F32) * QUERY_SCALE).astype(BF16)
        copy = wires.copy(r.kv_stage.at[p], r.kv_land.at[p], place.level[0][0])
        copy.start()
        return copy

    late = []

    def after_pair(p, copy):
        copy.wait()
        r.stacked[p, :, 128:] = (r.kv_own[p] + r.kv_land[p].astype(F32)).astype(BF16)
        stacked = r.stacked[p]
        columns = pl.ds(p * 128, 128)
        total = r.late_total.at[p]
        total[:wide, :] = dg(r.normed_t[...], stacked, NN)
        outer = dg(r.mixed_low[:, columns], r.grad_attn[...], TN)
        total[wide : wide + 128, :] = outer[:, : wide // 2]
        total[wide + 128 :, :] = outer[:, wide // 2 :]
        stages, lands = part_of(LATE, p)
        item = Reduction(place, wires, p, total, stages[0], stages[1:], lands, r.late_sum.at[p])
        half = 4 * item.slice
        stages[0][...] = total[rows_at((1 - item.bits[0]) * half, half), :].astype(BF16)
        item.low = item.bits[0] * half
        item.start()
        late.append(item)
        share = dg(stacked, r.qkv_pairs[p], NT)
        if p == 0:
            r.share[...] = share
        else:
            r.share[...] += share
        sums = jnp.sum(stacked.astype(F32), axis=0, keepdims=True)
        r.bias_row[:, p * 128 : (p + 1) * 128] = sums[:, :128]
        r.bias_row[:, width + p * 128 : width + (p + 1) * 128] = sums[:, 256:]

    copy0 = back_pair(0)

    @pl.when(home)
    def _():
        keep_in.wait()
        keep_out.start()

    copy1 = back_pair(1)
    after_pair(0, copy0)
    for item in early:
        item.halve(0)
    copy2 = back_pair(2)
    after_pair(1, copy1)
    late[0].halve(0)
    for item in early:
        item.halve(1)
    after_pair(2, copy2)

    @pl.when(home)
    def _():
        keep_out.wait()

    r.share_stage[...] = r.share[...].astype(BF16)
    share_copy = wires.copy(r.share_stage, r.share_land, place.sibling)
    share_copy.start()
    hidden_copy = pltpu.make_async_copy(r.grad_hidden, r.share, r.hidden_sem)
    hidden_copy.start()
    for item in early:
        item.halve(2)
        item.cross()
    late[0].halve(1)
    late[1].halve(0)
    share_copy.wait()
    hidden_copy.wait()

    gain = r.gain[...]
    chunk = rows // 3
    grad_gain = grad_shift = grad_stream_sum = jnp.zeros((1, wide), F32)
    frame_copies = []
    for c in range(3):
        at = pl.ds(c * chunk, chunk)
        stream = r.frames[at, :].astype(F32) + r.embedding[...]
        normal, scale = centre(stream)
        grad = r.share_stage[at, :].astype(F32) + r.share_land[at, :].astype(F32)
        grad_shift = grad_shift + jnp.sum(grad, axis=0, keepdims=True)
        grad_gain = grad_gain + jnp.sum(grad * normal, axis=0, keepdims=True)
        grad = grad * gain
        grad = (
            grad
            - jnp.mean(grad, axis=1, keepdims=True)
            - normal * jnp.mean(grad * normal, axis=1, keepdims=True)
        ) * scale + r.share[at, :]
        grad_stream_sum = grad_stream_sum + jnp.sum(grad, axis=0, keepdims=True)
        out = r.grad_frames.at[at]
        frame_copy = wires.copy(out, out, place.across)
        frame_copies.append(frame_copy)

        @pl.when(home)
        def _():
            out[...] = grad.astype(BF16)
            frame_copy.start()

    late[2].halve(0)
    late[0].halve(2)
    late[0].cross()
    late[1].halve(1)

    pack = r.pack
    row = lax.broadcasted_iota(jnp.int32, (dp, wide), 0)
    pack[:dp, :] = jnp.where(row == place.clip, grad_stream_sum, 0.0)
    pack[dp:, :] = r.pack_in[...]
    row = lax.broadcasted_iota(jnp.int32, (8, wide), 0)
    pack[dp : dp + 8, :] += (
        jnp.where(row == 0, grad_gain, 0.0)
        + jnp.where(row == 1, grad_shift, 0.0)
        + jnp.where(row == 6, r.bias_row[...], 0.0)
    )
    steps = [to for to, _ in place.level] + [place.across]
    pack_copies = []

    def pack_step(i):
        copy = wires.copy(pack.at[i] if False else r.pack_stage, r.pack_land.at[i], steps[i])
        r.pack_stage[...] = pack[...]
        copy.start()
        pack_copies.append(copy)

    def pack_add(i):
        pack_copies[i].wait()
        pack[...] += r.pack_land[i]

    pack_step(0)
    for item in early:
        item.land()
    pack_add(0)
    pack_step(1)
    late[1].halve(2)
    late[1].cross()
    late[2].halve(1)
    late[0].land()
    for item in early:
        item.double(2)
    pack_add(1)
    pack_step(2)
    late[2].halve(2)
    late[2].cross()
    late[1].land()
    late[0].double(2)
    for item in early:
        item.double(1)
    for i in range(2, len(steps)):
        pack_add(i)
        if i + 1 < len(steps):
            pack_step(i + 1)
    tail_copy = wires.copy(pack.at[pl.ds(dp, 16)], r.pack_tail, place.sibling)
    tail_copy.start()
    late[2].land()
    late[1].double(2)
    late[0].double(1)
    late[2].double(2)
    late[1].double(1)
    for item in early:
        item.double(0)
    late[0].double(0)
    late[2].double(1)
    late[1].double(0)
    late[2].double(0)
    tail_copy.wait()

    @pl.when(home)
    def _():
        out_copy.wait_send()
        for copy in frame_copies:
            copy.wait_send()

    @pl.when(away)
    def _():
        out_copy.wait_recv()
        for copy in frame_copies:
            copy.wait_recv()

    for item in early + late:
        item.finish()


def reduction_buffers(scratch, kind, slice_rows, columns, extra):
    stages = [4, 2, 1, 1] if kind == LATE else [2, 1, 1]
    lands = [4, 2, 1, 1] + [1] * extra
    for part in range(RS):
        for side, sizes in enumerate((stages, lands)):
            for i, size in enumerate(sizes):
                scratch[side, kind, part, i] = pltpu.VMEM((size * slice_rows, columns), BF16)


def levels_of(dp):
    levels = 1
    while 2**levels < dp:
        levels += 1
    return levels


def backward(dp, valid, ins):
    rows, width = ins["query"].shape
    wide = ins["normed_t"].shape[0]
    pairs = width // 128
    levels = levels_of(dp)
    extra = levels - RS
    down, up = ins["down_give"].shape, ins["up_give"].shape
    late_rows = wide + 256
    pack_rows = dp + ins["pack_in"].shape[0]
    outs = dict(
        output_to=((rows, wide), BF16),
        grad_frames=((rows, wide), BF16),
        down_sum=((RS, 2 * down[1], down[2]), BF16),
        up_sum=((RS, 2 * up[1], up[2]), BF16),
        late_sum=((pairs, late_rows, 3 * 128), BF16),
        pack=((pack_rows, wide), F32),
        pack_tail=((16, wide), F32),
    )
    wires = 9 * (2 * RS + 2 + RS + extra) + pairs + 1 + 1 + 3 + levels + 1 + 1
    scratch = dict(
        masked=pltpu.VMEM((2, 2 * rows, 128), BF16),
        scaled=pltpu.VMEM((2, rows, 128), BF16),
        plain=pltpu.VMEM((2, rows, 128), BF16),
        given=pltpu.VMEM((2, rows, 128), BF16),
        kv_own=pltpu.VMEM((pairs, rows, 256), F32),
        kv_stage=pltpu.VMEM((pairs, rows, 256), BF16),
        kv_land=pltpu.VMEM((pairs, rows, 256), BF16),
        stacked=pltpu.VMEM((pairs, rows, 384), BF16),
        late_total=pltpu.VMEM((pairs, late_rows, 384), F32),
        share=pltpu.VMEM((rows, wide), F32),
        share_stage=pltpu.VMEM((rows, wide), BF16),
        share_land=pltpu.VMEM((rows, wide), BF16),
        bias_row=pltpu.VMEM((1, 2 * width), F32),
        pack_stage=pltpu.VMEM((pack_rows, wide), F32),
        pack_land=pltpu.VMEM((levels + 1, pack_rows, wide), F32),
        send_sems=pltpu.SemaphoreType.DMA((wires,)),
        recv_sems=pltpu.SemaphoreType.DMA((wires,)),
        local_sem=pltpu.SemaphoreType.DMA,
        hidden_sem=pltpu.SemaphoreType.DMA,
    )
    reduction_buffers(scratch, DOWN, down[1] // 4, down[2], extra)
    reduction_buffers(scratch, UP, up[1] // 4, up[2], extra)
    reduction_buffers(scratch, LATE, late_rows // 8, 384, extra)
    cost = pl.CostEstimate(flops=2 * 10**10, bytes_accessed=10**8, transcendentals=10**7)
    kernel = functools.partial(backward_kernel, dp, valid)
    hbm = ("output", "output_to", "grad_hidden")
    return call(kernel, "backward", 1, ins, outs, scratch, hbm, cost)


def forward(dp, valid, ins):
    rows, wide = ins["frames"].shape
    width = ins["qkv_local"].shape[2]
    hidden = ins["up_local"].shape[1]
    outs = dict(
        own=((rows, wide), BF16),
        grad_rows=((rows, wide), BF16),
        info=((8, wide), F32),
        bias=((8, wide), F32),
        normed_t=((wide, rows), BF16),
        query=((rows, width), BF16),
        key=((2 * rows, width), BF16),
        value=((2 * rows, width), BF16),
        lse=((width // HEAD, rows), F32),
        mixed=((rows, width), BF16),
        mixed_other=((rows, width), BF16),
        exact=((rows, width), F32),
        qkv_pairs=((width // 128, wide, 384), BF16),
        up=((wide, hidden), BF16),
        down=((hidden, wide), BF16),
        out=((width, wide), BF16),
        out_other=((width, wide), BF16),
    )
    wires = 4 * RS * (1 + RS) + 3 + 6 + 1 + 1 + 3
    scratch = dict(
        other=pltpu.VMEM((rows, wide), BF16),
        normed=pltpu.VMEM((2 * rows, wide), BF16),
        qkv=pltpu.VMEM((3, wide, width), BF16),
        masked=pltpu.VMEM((2, 2 * rows, 128), BF16),
        send_sems=pltpu.SemaphoreType.DMA((wires,)),
        recv_sems=pltpu.SemaphoreType.DMA((wires,)),
        local_sems=pltpu.SemaphoreType.DMA((6,)),
    )
    hbm = (
        "qkv_local",
        "grad_local",
        "up_local",
        "down_local",
        "out_local",
    )
    cost = pl.CostEstimate(flops=10**10, bytes_accessed=10**7, transcendentals=10**7)
    kernel = functools.partial(forward_kernel, dp, valid)
    return call(kernel, "forward", 2, ins, outs, scratch, hbm, cost)


def layer_norm(inputs, scales, shifts):
    row_mean = jnp.mean(inputs, axis=-1, keepdims=True)
    centred = inputs - row_mean
    variance = jnp.mean(centred * centred, axis=-1, keepdims=True)
    return centred * lax.rsqrt(variance + EPSILON) * scales + shifts


def exact_gelu(inputs):
    return jax.nn.gelu(inputs, approximate=False)


def on_device(
    sizes,
    frames,
    languages,
    present,
    lang_table,
    norm1_gain,
    norm1_shift,
    qkv_weight,
    qkv_bias,
    out_weight,
    out_bias,
    norm2_gain,
    norm2_shift,
    up_weight,
    up_bias,
    down_weight,
    down_bias,
    grad_out,
):
    d, t, s = (lax.axis_index(name) for name in AXES)
    home = d % 2 == t
    clips = sizes["dp"]
    _, valid, width = frames.shape
    rows = -(-valid // 256) * 256
    head_width = qkv_weight.shape[2]
    hidden = up_weight.shape[1]
    langs = lang_table.shape[0]
    pairs = head_width // 128
    pad = ((0, rows - valid), (0, 0))

    one_hot = (languages[:, None] == lax.broadcasted_iota(jnp.int32, (1, langs), 1)).astype(F32)
    embedding = jnp.dot(one_hot, lang_table.astype(F32), precision=lax.Precision.HIGHEST)
    lane = lax.broadcasted_iota(jnp.int32, (1, width), 1)
    once = jnp.where(s == 0, languages[:, None].astype(F32), 0.0)
    info = jnp.concatenate(
        [
            embedding,
            jnp.broadcast_to(present[:, None].astype(F32), (1, width)),
            jnp.where(lane == d, once, 0.0),
            jnp.zeros((5, width), F32),
        ]
    )
    biases = jnp.concatenate([qkv_bias.reshape(1, width), up_bias.reshape(-1, width)]).astype(F32)
    gain_one, shift_one = norm1_gain.astype(F32)[None], norm1_shift.astype(F32)[None]
    gain_two, shift_two = norm2_gain.astype(F32), norm2_shift.astype(F32)
    f = forward(
        clips,
        valid,
        dict(
            frames=jnp.pad(frames[0], pad),
            grad_local=jnp.pad(grad_out[0], pad),
            info_local=info,
            bias_local=jnp.pad(biases, ((0, 8 - biases.shape[0]), (0, 0))),
            gain=gain_one,
            shift=shift_one,
            qkv_local=qkv_weight,
            up_local=up_weight,
            down_local=down_weight,
            out_local=out_weight,
        ),
    )
    keep = f.info[1, 0]

    moves = []
    group = sizes["tensor"] * sizes["seq"]
    for a in range(sizes["dp"]):
        moves += [(a * group + b, (a ^ 1) * group + b) for b in range(group)]

    def both_cores(part):
        return part + lax.ppermute(part, AXES, moves)

    attention = dg(f.mixed, f.out, NN) + dg(f.mixed_other, f.out_other, NN)
    stream = f.own.astype(F32) + f.info[:1]
    hidden1 = stream + attention + out_bias.astype(F32)
    normed2, norm2_back = jax.vjp(layer_norm, hidden1, gain_two, shift_two)
    normed2 = normed2.astype(BF16)
    pre_act = dg(normed2, f.up, NN) + f.bias[1:3].reshape(-1)
    activation, gelu_back = jax.vjp(exact_gelu, pre_act)
    activation = activation.astype(BF16)
    feed = both_cores(dg(activation, f.down, NN))
    output = (keep * (hidden1 + feed + down_bias.astype(F32))).astype(BF16)

    grad_rows = keep * f.grad_rows.astype(F32)
    grad_low = grad_rows.astype(BF16)
    grad_activation = dg(grad_low, f.down, NT)
    grad_pre = gelu_back(grad_activation)[0].astype(BF16)
    grad_normed2 = both_cores(dg(grad_pre, f.up, NT))
    grad_hidden_norm, grad_norm2_gain, grad_norm2_shift = norm2_back(grad_normed2)
    grad_hidden1 = grad_rows + grad_hidden_norm
    grad_attn_low = grad_hidden1.astype(BF16)
    grad_mixed = lax.optimization_barrier(dg(grad_attn_low, f.out, NT).astype(BF16))
    grad_down = dg(activation, grad_low, TN)
    grad_up = dg(normed2, grad_pre, TN)

    def halves(grads):
        bits = [s, (d // 2) % 2, (d // 4) % 2]
        give, kept = [], []
        for part, bit in zip(grads.reshape(RS, -1, grads.shape[1]), bits):
            half = part.shape[0] // 2
            give.append(lax.dynamic_slice_in_dim(part, (1 - bit) * half, half).astype(BF16))
            kept.append(lax.dynamic_slice_in_dim(part, bit * half, half))
        return jnp.stack(give), jnp.stack(kept)

    down_give, down_keep = halves(grad_down)
    up_give, up_keep = halves(grad_up)
    zero = jnp.zeros((width,), F32)
    vectors = jnp.concatenate(
        [
            jnp.stack(
                [
                    zero,
                    zero,
                    jnp.sum(grad_hidden1, axis=0),
                    grad_norm2_gain,
                    grad_norm2_shift,
                    jnp.sum(grad_rows, axis=0),
                    zero,
                ]
            ),
            jnp.sum(grad_pre.astype(F32), axis=0).reshape(-1, width),
            f.info[2:3],
        ]
    )
    vectors = jnp.pad(vectors, ((0, 16 - vectors.shape[0]), (0, 0)))
    inner = jnp.sum((grad_mixed.astype(F32) * f.exact).reshape(rows, -1, HEAD), axis=2).T
    b = backward(
        clips,
        valid,
        dict(
            query=f.query,
            key=f.key,
            value=f.value,
            lse=f.lse,
            inner=inner,
            mixed_low=f.mixed,
            grad_mixed=grad_mixed,
            grad_attn=grad_attn_low,
            grad_hidden=grad_hidden1,
            frames=f.own,
            embedding=f.info[:1],
            gain=gain_one,
            normed_t=f.normed_t,
            qkv_pairs=f.qkv_pairs,
            output=output,
            down_give=down_give,
            down_keep=down_keep,
            up_give=up_give,
            up_keep=up_keep,
            pack_in=vectors,
        ),
    )
    v = b.pack[clips:]
    tail = jnp.where(home, v, b.pack_tail)
    late = b.late_sum.astype(F32)
    grad_qkv = late[:, :width].reshape(pairs, width, 3, 128).transpose(2, 1, 0, 3)
    grad_outw = jnp.concatenate([late[:, width : width + 128], late[:, width + 128 :]], axis=2)
    ids = v[9, :clips][:, None]
    hot = (ids == lax.broadcasted_iota(jnp.int32, (1, langs), 1).astype(F32)).astype(F32)
    grad_lang_table = lax.dot_general(
        hot, b.pack[:clips], (((0,), (0,)), ((), ())), precision=lax.Precision.HIGHEST
    )
    return (
        b.output_to[None, :valid],
        b.grad_frames[None, :valid],
        grad_lang_table,
        v[0],
        v[1],
        grad_qkv.reshape(3, width, head_width),
        tail[6].reshape(2, head_width),
        grad_outw.reshape(head_width, width),
        v[2],
        v[3],
        v[4],
        b.up_sum.astype(F32).reshape(width, hidden),
        tail[7:9].reshape(-1),
        b.down_sum.astype(F32).reshape(hidden, width),
        v[5],
    )


def solution(mesh):
    rows = P("dp", "seq", None)
    columns, one = P(None, "tensor"), P("dp")
    placed = (
        rows,
        one,
        one,
        P(),
        P(),
        P(),
        P(None, None, "tensor"),
        columns,
        P("tensor", None),
        P(),
        P(),
        P(),
        columns,
        P("tensor"),
        P("tensor", None),
        P(),
        rows,
    )
    out = (
        rows,
        rows,
        P(),
        P(),
        P(),
        P(None, None, "tensor"),
        columns,
        P("tensor", None),
        P(),
        P(),
        P(),
        columns,
        P("tensor"),
        P("tensor", None),
        P(),
    )
    return jax.shard_map(
        functools.partial(on_device, dict(mesh.shape)),
        mesh=mesh,
        in_specs=placed,
        out_specs=out,
        check_vma=False,
    )
```

```python
import functools
import types

import jax
import jax.numpy as jnp
from jax import lax
from jax.experimental import pallas as pl
from jax.experimental.pallas import tpu as pltpu
from jax.sharding import PartitionSpec as P

HEAD = 64
EPSILON = 1e-05
QUERY_SCALE = 0.125
AXES = ("dp", "tensor", "seq")
F32 = jnp.float32
BF16 = jnp.bfloat16
NN = (((1,), (0,)), ((), ()))
NT = (((1,), (1,)), ((), ()))
TN = (((0,), (0,)), ((), ()))
VMEM = pl.BlockSpec(memory_space=pltpu.VMEM)
ANY = pl.BlockSpec(memory_space=pl.ANY)
RS = 3


def dg(left, right, dims):
    return lax.dot_general(left, right, dims, preferred_element_type=F32)


def rows_at(start, size):
    return pl.ds(pl.multiple_of(start, 16), size)


class Place:
    def __init__(self, dp):
        self.d, self.t, self.s = (lax.axis_index(name) for name in AXES)
        self.core = lax.rem(self.d, 2)
        self.home = self.core == self.t
        self.away = jnp.logical_not(self.home)
        self.clip = self.d - self.core + self.t
        self.sibling = (self.d + 1 - 2 * self.core, self.t, self.s)
        self.across = (self.d, 1 - self.t, self.s)
        self.level = [((self.d, self.t, 1 - self.s), self.s)]
        bit = 2
        while bit < dp:
            value = lax.rem(self.d // bit, 2)
            self.level.append(((self.d + bit - 2 * bit * value, self.t, self.s), value))
            bit *= 2
        self.peers = [self.sibling, self.across] + [to for to, _ in self.level]

    def enter(self):
        barrier = pltpu.get_barrier_semaphore()
        for to in self.peers:
            pl.semaphore_signal(barrier, inc=1, device_id=to, device_id_type=pl.DeviceIdType.MESH)
        pl.semaphore_wait(barrier, len(self.peers))

    def order(self, part):
        levels = [self.level[(part + j) % RS] for j in range(RS)]
        return [to for to, _ in levels], [bit for _, bit in levels]


class Wires:
    def __init__(self, send_sems, recv_sems):
        self.send_sems, self.recv_sems, self.used = send_sems, recv_sems, 0

    def copy(self, src, dst, to):
        i = self.used
        self.used += 1
        return pltpu.make_async_remote_copy(
            src_ref=src,
            dst_ref=dst,
            send_sem=self.send_sems.at[i],
            recv_sem=self.recv_sems.at[i],
            device_id=to,
            device_id_type=pl.DeviceIdType.MESH,
        )


class Fetch:
    def __init__(self, place, wires, part, local, result):
        self.to, self.bits = place.order(part)
        self.place, self.wires, self.result = place, wires, result
        self.slice = local.shape[0] // 2**RS
        self.at = self.slice * (4 * self.bits[0] + 2 * self.bits[1] + self.bits[2])
        at = rows_at(self.at, self.slice)
        self.crossing = wires.copy(local.at[at], result.at[at], place.across)

        @pl.when(place.home)
        def _():
            self.crossing.start()

    def widen(self, j):
        size = self.slice * 2 ** (RS - 1 - j)
        ref = self.result.at[rows_at(self.at, size)]
        self.at = self.at - self.bits[j] * size
        return self.wires.copy(ref, ref, self.to[j])

    def arrive(self):
        self.moving = self.widen(RS - 1)

        @pl.when(self.place.home)
        def _():
            self.crossing.wait_send()

        @pl.when(self.place.away)
        def _():
            self.crossing.wait_recv()
            self.moving.start()

    def double(self, j):
        before = self.moving
        if j:
            self.moving = self.widen(j - 1)

        @pl.when(self.place.away)
        def _():
            before.wait()
            if j:
                self.moving.start()


class Reduction:
    def __init__(self, place, wires, part, r, index, stage, result):
        self.to, self.bits = place.order(part)
        self.extra = place.level[RS:]
        self.place, self.wires, self.stage, self.result = place, wires, stage, result
        self.kept, self.land_ref = r.kept.at[index], r.land.at[index]
        self.more = [r.more_land.at[index, i] for i in range(len(self.extra))] if self.extra else []
        self.local = lambda src, dst: pltpu.make_async_copy(src, dst, r.part_sems.at[index])
        self.slice = result.shape[0] // 2**RS
        self.low = 0
        self.at = self.bits[0] * 4 * self.slice
        self.forwards = []
        sizes = [4, 2, 1, 1]
        starts = [sum(sizes[:i]) for i in range(4)]
        self.lands = [
            self.land_ref.at[pl.ds(start * self.slice, size * self.slice)]
            for start, size in zip(starts, sizes)
        ]
        self.last = stage.at[pl.ds(3 * self.slice, self.slice)]

    def start(self, total):
        half = 4 * self.slice
        bit = self.bits[0]
        self.stage[...] = total[rows_at((1 - bit) * half, half), :].astype(BF16)
        self.moving = self.wires.copy(self.stage, self.lands[0], self.to[0])
        self.moving.start()
        self.kept[...] = total[rows_at(bit * half, half), :]

    def halve(self, j):
        self.moving.wait()
        half = self.slice * 2 ** (RS - 2 - j)
        if j == RS - 1:
            now = rows_at(self.low, self.slice)
            self.kept[now, :] += self.lands[j][...].astype(F32)
            return
        bit = self.bits[j + 1]
        away, home = (1 - bit) * half, bit * half
        stage = self.stage.at[pl.ds(0 if j == 0 else 2 * self.slice, half)]
        stage[...] = (
            self.kept[rows_at(self.low + away, half), :]
            + self.lands[j][rows_at(away, half), :].astype(F32)
        ).astype(BF16)
        self.moving = self.wires.copy(stage, self.lands[j + 1], self.to[j + 1])
        self.moving.start()
        self.kept[rows_at(self.low + home, half), :] += self.lands[j][
            rows_at(home, half), :
        ].astype(F32)
        self.low = self.low + home
        self.at = self.at + home

    def cross(self):
        now = rows_at(self.low, self.slice)
        for (to, _), land in zip(self.extra, self.more):
            self.last[...] = self.kept[now, :].astype(BF16)
            copy = self.wires.copy(self.last, land, to)
            copy.start()
            copy.wait()
            self.kept[now, :] = self.last[...].astype(F32) + land[...].astype(F32)
        self.crossing = self.wires.copy(self.last, self.lands[RS], self.place.across)

        @pl.when(self.place.away)
        def _():
            self.last[...] = self.kept[now, :].astype(BF16)
            self.crossing.start()

    def spread(self, src, start, size):
        ref = self.result.at[rows_at(start, size)]
        forward = self.wires.copy(ref if src is None else src, ref, self.place.sibling)
        self.forwards.append(forward)
        return forward

    def widen(self, src, j):
        ref = self.result.at[rows_at(self.at, self.slice * 2 ** (RS - 1 - j))]
        return self.wires.copy(ref if src is None else src, ref, self.to[j])

    def land(self):
        first = self.spread(self.last, self.at, self.slice)
        self.moving = self.widen(self.last, RS - 1)
        self.writing = self.local(self.last, self.result.at[rows_at(self.at, self.slice)])

        @pl.when(self.place.home)
        def _():
            self.crossing.wait_recv()
            self.last[...] = (
                self.kept[rows_at(self.low, self.slice), :] + self.lands[RS][...].astype(F32)
            ).astype(BF16)
            self.moving.start()
            first.start()
            self.writing.start()

        @pl.when(self.place.away)
        def _():
            self.crossing.wait_send()

    def double(self, j):
        size = self.slice * 2 ** (RS - 1 - j)
        bit = self.bits[j]
        came = self.at + (1 - 2 * bit) * size
        self.at = self.at - bit * size
        before, forward = self.moving, self.spread(None, came, size)
        if j:
            self.moving = self.widen(None, j - 1)

        @pl.when(self.place.home)
        def _():
            before.wait()
            if j == RS - 1:
                self.writing.wait()
            if j:
                self.moving.start()
            forward.start()

    def finish(self):
        @pl.when(self.place.home)
        def _():
            for forward in self.forwards:
                forward.wait_send()

        @pl.when(self.place.away)
        def _():
            for forward in self.forwards:
                forward.wait_recv()


def pair_lanes(rows):
    return lax.broadcasted_iota(jnp.int32, (rows, 128), 1)


def one_head(pair, e, extra=None):
    lane = pair_lanes(pair.shape[0])
    own = (lane < HEAD) if e == 0 else (lane >= HEAD)
    kept = jnp.where(own, pair, jnp.zeros_like(pair))
    if extra is not None:
        kept = jnp.where(lane == (HEAD if e == 0 else 0), extra, kept)
    return kept


def masked_keys(key_ref, columns, masked, rows, valid):
    row = lax.broadcasted_iota(jnp.int32, (rows, 128), 0)
    bias = jnp.where(row >= valid, -1e30, 0.0).astype(BF16)
    for e in range(2):
        for part in range(2):
            at = pl.ds(part * rows, rows)
            masked[e, at, :] = one_head(key_ref[at, columns], e, bias)


def centre(inputs):
    centred = inputs - jnp.mean(inputs, axis=1, keepdims=True)
    scale = lax.rsqrt(jnp.mean(centred * centred, axis=1, keepdims=True) + EPSILON)
    return centred * scale, scale


def call(kernel, name, collective, ins, outs, scratch, hbm, cost):
    names = list(ins) + list(outs) + list(scratch)

    def body(*refs):
        named = dict(zip(names, refs))
        plain = {name: ref for name, ref in named.items() if isinstance(name, str)}
        kernel(types.SimpleNamespace(table=named, **plain))

    results = pl.pallas_call(
        body,
        out_shape=[jax.ShapeDtypeStruct(*item) for item in outs.values()],
        in_specs=[ANY if item in hbm else VMEM for item in ins],
        out_specs=[ANY if item in hbm else VMEM for item in outs],
        scratch_shapes=list(scratch.values()),
        compiler_params=pltpu.CompilerParams(
            collective_id=collective,
            has_side_effects=collective is not None,
            vmem_limit_bytes=60 * 2**20,
        ),
        cost_estimate=cost,
        name=name,
    )(*ins.values())
    return types.SimpleNamespace(**dict(zip(outs, results)))


def forward_kernel(dp, valid, r):
    place = Place(dp)
    place.enter()
    wires = Wires(r.send_sems, r.recv_sems)
    rows, wide = r.frames.shape
    width = r.query.shape[1]
    home, away = place.home, place.away
    chunk = rows // 3

    first = [Fetch(place, wires, j, r.qkv_local.at[j], r.qkv.at[j]) for j in range(3)]
    info = wires.copy(r.info_local, r.info, place.sibling)
    bias = wires.copy(r.bias_local, r.bias, place.across)
    own = wires.copy(r.frames, r.own, place.sibling)
    beside, onward = [], []
    for c in range(3):
        at = pl.ds(c * chunk, chunk)
        beside.append(wires.copy(r.frames.at[at], r.other.at[at], place.level[0][0]))
        onward.append(wires.copy(r.other.at[at], r.other.at[at], place.sibling))
    grads = wires.copy(r.grad_local, r.grad_rows, place.sibling)
    own_out = r.out.at[rows_at(place.core * width, width)]
    keep = [
        pltpu.make_async_copy(src, dst, r.local_sems.at[i])
        for i, (src, dst) in enumerate(
            (
                (r.qkv_local, r.qkv),
                (r.grad_local, r.grad_rows),
                (r.up_local, r.up),
                (r.down_local, r.down),
                (r.out_local, own_out),
            )
        )
    ]
    other_out = r.out.at[rows_at((1 - place.core) * width, width)]
    lend = pltpu.make_async_copy(r.out_local, other_out, r.local_sems.at[len(keep)])
    lent = wires.copy(own_out, own_out, place.sibling)

    @pl.when(home)
    def _():
        info.start()
        bias.start()
        own.start()
        for copy in beside:
            copy.start()
        for copy in keep:
            copy.start()
        r.info[...] = r.info_local[...]
        r.bias[...] = r.bias_local[...]
        r.own[...] = r.frames[...]

    @pl.when(away)
    def _():
        lend.start()

    later = []
    for part in range(RS):
        for local, result in ((r.down_local, r.down), (r.up_local, r.up), (r.out_local, own_out)):
            size = local.shape[0] // RS
            at = pl.ds(part * size, size)
            later.append(Fetch(place, wires, part, local.at[at], result.at[at]))

    @pl.when(home)
    def _():
        grads.start()

    for item in first:
        item.arrive()

    @pl.when(away)
    def _():
        info.wait_recv()
        own.wait_recv()
        bias.wait_recv()

    embedding = r.info[0:1, :]

    def norm(source, c, to):
        normal, _ = centre(source[pl.ds(c * chunk, chunk), :].astype(F32) + embedding)
        normed = normal * r.gain[...] + r.shift[...]
        r.normed[pl.ds(to + c * chunk, chunk), :] = normed.astype(BF16)
        return normed

    for c in range(3):
        r.normed_t[:, c * chunk : (c + 1) * chunk] = norm(r.own, c, 0).T.astype(BF16)
        if c == 0:
            for item in first:
                item.double(2)

        @pl.when(home)
        def _():
            beside[c].wait()
            onward[c].start()

    for item in first:
        item.double(1)
    for c in range(3):

        @pl.when(away)
        def _():
            onward[c].wait_recv()

        norm(r.other, c, rows)
    for item in first:
        item.double(0)

    @pl.when(home)
    def _():
        keep[0].wait()

    r.query[...] = (
        (dg(r.normed[:rows, :], r.qkv[0], NN) + r.bias[0:1, :width]) * QUERY_SCALE
    ).astype(BF16)
    for part in range(2):
        at = pl.ds(part * rows, rows)
        r.key[at, :] = dg(r.normed[at, :], r.qkv[1], NN).astype(BF16)
        r.value[at, :] = (dg(r.normed[at, :], r.qkv[2], NN) + r.bias[0:1, width:]).astype(BF16)
    for item in later:
        item.arrive()

    block = 256
    mixed_copies = []

    def one_pair(p):
        columns = pl.ds(p * 128, 128)
        whole = pl.ds(pl.multiple_of(place.core * width + p * 128, 128), 128)
        masked_keys(r.key, columns, r.masked, rows, valid)
        for j in range(3):
            r.qkv_pairs[p, :, j * 128 : (j + 1) * 128] = r.qkv[j, :, columns]

        def one_block(i, _):
            at = pl.ds(pl.multiple_of(i * block, block), block)
            parts, rests = [], []
            for e in range(2):
                queries = one_head(r.query[at, columns], e, jnp.ones((), BF16))
                scores = dg(queries, r.masked[e], NT)
                top = jnp.max(scores, axis=1, keepdims=True)
                weights = jnp.exp(scores - top)
                total = jnp.sum(weights, axis=1, keepdims=True)
                weights = weights * (1.0 / total)
                low = weights.astype(BF16)
                rest = (weights - low.astype(F32)).astype(BF16)
                parts.append(dg(low, r.value[:, columns], NN))
                rests.append(dg(rest, r.value[:, columns], NN))
                r.lse[pl.ds(2 * p + e, 1), at] = (top + jnp.log(total)).reshape(1, block)
            first = pair_lanes(block) < HEAD
            mixed = jnp.where(first, parts[0], parts[1])
            low = mixed.astype(BF16)
            r.mixed[at, whole] = low
            rest = mixed - low.astype(F32) + jnp.where(first, rests[0], rests[1])
            r.mixed_rest[at, columns] = rest.astype(BF16)
            return 0

        lax.fori_loop(0, rows // block, one_block, 0)
        copy = wires.copy(r.mixed.at[:, whole], r.mixed.at[:, whole], place.sibling)
        copy.start()
        mixed_copies.append(copy)

    one_pair(0)
    for item in later:
        item.double(2)
    one_pair(1)
    for item in later:
        item.double(1)
    one_pair(2)
    for item in later:
        item.double(0)

    @pl.when(away)
    def _():
        lend.wait()
        lent.start()
        grads.wait_recv()
        lent.wait_send()

    @pl.when(home)
    def _():
        lent.wait_recv()
        for copy in keep[1:]:
            copy.wait()
        info.wait_send()
        bias.wait_send()
        own.wait_send()
        grads.wait_send()
        for copy in onward:
            copy.wait_send()

    for c in range(3):
        at = pl.ds(c * chunk, chunk)
        r.grad_rows[at, :] = (r.grad_rows[at, :].astype(F32) * r.info[1:2, :]).astype(BF16)
    for copy in mixed_copies:
        copy.wait()


def gelu_pair(inputs):
    half = 0.5 + 0.5 * lax.erf(inputs * 0.7071067811865476)
    slope = inputs * (jnp.exp(inputs * inputs * -0.5) * 0.3989422804014327)
    return inputs * half, half + slope


def backward_kernel(dp, valid, r):
    place = Place(dp)
    place.enter()
    wires = Wires(r.send_sems, r.recv_sems)
    rows, width = r.query.shape
    wide = r.normed_t.shape[0]
    hidden = r.up.shape[1]
    home, away = place.home, place.away
    chunk = rows // 3
    chunks = [pl.ds(c * chunk, chunk) for c in range(3)]
    embedding, keep = r.info[0:1, :], r.info[1:2, :]
    gain_one, gain_two, shift_two, out_bias, down_bias = (r.vectors[i : i + 1, :] for i in range(5))
    zero = jnp.zeros((1, wide), F32)

    bring = [
        pltpu.make_async_copy(src, dst, r.local_sems.at[i])
        for i, (src, dst) in enumerate(((r.up, r.up_vmem), (r.down, r.down_vmem)))
    ]
    for copy in bring:
        copy.start()

    for at in chunks:
        attention = dg(r.mixed[at, :], r.out[...], NN)
        rows_in = r.frames[at, :].astype(F32) + embedding + attention + out_bias
        r.hidden[at, :] = rows_in
        normal, _ = centre(rows_in)
        r.normed2[at, :] = (normal * gain_two + shift_two).astype(BF16)

    for copy in bring:
        copy.wait()
    block = 512
    up_sums = [jnp.zeros((1, block), F32) for _ in range(hidden // block)]
    for at in chunks:
        for h in range(hidden // block):
            units = pl.ds(h * block, block)
            start = h * block
            bias = r.bias[1 + start // wide : 2 + start // wide, start % wide : start % wide + block]
            if start % wide + block > wide:
                bias = jnp.concatenate(
                    [
                        r.bias[1 + start // wide : 2 + start // wide, start % wide :],
                        r.bias[2 + start // wide : 3 + start // wide, : start % wide + block - wide],
                    ],
                    axis=1,
                )
            active, slope = gelu_pair(dg(r.normed2[at, :], r.up_vmem[:, units], NN) + bias)
            r.active[at, units] = active.astype(BF16)
            grad = dg(r.grad_rows[at, :], r.down_vmem[units, :], NT)
            low = (grad * slope).astype(BF16)
            r.grad_pre[at, units] = low
            up_sums[h] = up_sums[h] + jnp.sum(low.astype(F32), axis=0, keepdims=True)
    norm_copies, feed_copies = [], []
    for at in chunks:
        r.norm_stage[at, :] = dg(r.grad_pre[at, :], r.up_vmem[...], NT)
        copy = wires.copy(r.norm_stage.at[at], r.norm_land.at[at], place.sibling)
        copy.start()
        norm_copies.append(copy)
    for at in chunks:
        r.stage[at, :] = dg(r.active[at, :], r.down_vmem[...], NN).astype(BF16)
        copy = wires.copy(r.stage.at[at], r.feed_land.at[at], place.sibling)
        copy.start()
        feed_copies.append(copy)

    def reduction(kind, part, stage, result):
        return Reduction(place, wires, part, r, kind * RS + part, stage, result.at[part])

    down, up, late = [], [], []
    for p in range(RS):
        columns = pl.ds(p * block, block)
        r.total[...] = dg(r.active[:, columns], r.grad_rows[...], TN)
        down.append(reduction(0, p, r.part_stage.at[p], r.down_sum))
        down[p].start(r.total)
    for p in range(RS):
        columns = pl.ds(p * chunk, chunk)
        outer = dg(r.normed2[:, columns], r.grad_pre[...], TN)
        r.total[:chunk, :] = outer[:, :wide]
        r.total[chunk:, :] = outer[:, wide:]
        up.append(reduction(1, p, r.part_stage.at[RS + p], r.up_sum))
        up[p].start(r.total)

    grad_gain_two = grad_shift_two = grad_out_bias = grad_down_bias = zero
    for c, at in enumerate(chunks):
        norm_copies[c].wait()
        feed_copies[c].wait()
        rows_in = r.hidden[at, :]
        normal, scale = centre(rows_in)
        feed = r.stage[at, :].astype(F32) + r.feed_land[at, :].astype(F32)
        r.stage[at, :] = (keep * (rows_in + feed + down_bias)).astype(BF16)
        grad = r.norm_stage[at, :] + r.norm_land[at, :]
        grad_shift_two = grad_shift_two + jnp.sum(grad, axis=0, keepdims=True)
        grad_gain_two = grad_gain_two + jnp.sum(grad * normal, axis=0, keepdims=True)
        grad = grad * gain_two
        grad = (
            grad
            - jnp.mean(grad, axis=1, keepdims=True)
            - normal * jnp.mean(grad * normal, axis=1, keepdims=True)
        ) * scale
        grad_out = r.grad_rows[at, :].astype(F32)
        grad_down_bias = grad_down_bias + jnp.sum(grad_out, axis=0, keepdims=True)
        grad = grad + grad_out
        grad_out_bias = grad_out_bias + jnp.sum(grad, axis=0, keepdims=True)
        r.hidden[at, :] = grad
        low = grad.astype(BF16)
        r.grad_attn[at, :] = low
        r.grad_mixed[at, :] = dg(low, r.out[rows_at(place.core * width, width), :], NT).astype(BF16)
    out_copy = wires.copy(r.stage, r.output, place.across)
    out_keep = pltpu.make_async_copy(r.stage, r.output, r.local_sems.at[2])

    @pl.when(home)
    def _():
        out_copy.start()
        out_keep.start()

    def masked(e, part):
        return r.grad_pre.at[:, pl.ds((2 * e + part) * 128, 128)]

    def operand(i):
        return r.grad_pre.at[:, pl.ds((4 + i) * 128, 128)]

    def kv(ref, p):
        return ref.at[:, pl.ds(p * 256, 256)]

    def whole(p):
        return pl.ds(pl.multiple_of(place.core * width + p * 128, 128), 128)

    row = lax.broadcasted_iota(jnp.int32, (rows, 128), 0)
    pad = jnp.where(row >= valid, -1e30, 0.0).astype(BF16)

    def prepare(p):
        columns = pl.ds(p * 128, 128)
        grad = r.grad_mixed[:, columns]
        product = grad.astype(F32) * (
            r.mixed[:, whole(p)].astype(F32) + r.mixed_rest[:, columns].astype(F32)
        )
        query = r.query[:, columns]
        lane = pair_lanes(rows)
        for e in range(2):
            for part in range(2):
                masked(e, part)[...] = one_head(r.key[pl.ds(part * rows, rows), columns], e, pad)
            operand(e)[...] = one_head(query, e, jnp.ones((), BF16))
            operand(2 + e)[...] = one_head(query, e)
            operand(4 + e)[...] = one_head(grad, e)
            own = (lane < HEAD) if e == 0 else (lane >= HEAD)
            r.inner[e : e + 1, :] = jnp.sum(
                jnp.where(own, product, 0.0), axis=1, keepdims=True
            ).reshape(1, rows)

    def back_half(p, part, total):
        columns = pl.ds(p * 128, 128)
        size = 384
        store = kv(r.norm_stage if part == 0 else r.normed2, p)

        def one_block(i, total):
            at = pl.ds(pl.multiple_of(i * size, size), size)
            from_all = pl.ds(pl.multiple_of(part * rows + i * size, size), size)
            grad_keys, grad_values = [], []
            for e in range(2):
                scores = dg(masked(e, part)[at, :], operand(e)[...], NT)
                weights = jnp.exp(scores - r.lse[2 * p + e : 2 * p + e + 1, :])
                grad_weights = dg(r.value[from_all, columns], operand(4 + e)[...], NT)
                grad_scores = (weights * (grad_weights - r.inner[e : e + 1, :])).astype(BF16)
                grad_values.append(dg(weights.astype(BF16), operand(4 + e)[...], NN))
                grad_keys.append(dg(grad_scores, operand(2 + e)[...], NN))
                total = total + dg(one_head(r.key[from_all, columns], e), grad_scores, TN)
            store[at, :128] = (grad_keys[0] + grad_keys[1]).astype(store.dtype)
            store[at, 128:] = (grad_values[0] + grad_values[1]).astype(store.dtype)
            return total

        return lax.fori_loop(0, rows // size, one_block, total)

    def send_kv(p):
        copy = wires.copy(kv(r.normed2, p), kv(r.kv_land, p), place.level[0][0])
        copy.start()
        return copy

    def stacked(p):
        return r.active.at[:, pl.ds(p * 384, 384)]

    def end_queries(p, total):
        low = total.T.astype(BF16)
        stacked(p)[:, :128] = (low.astype(F32) * QUERY_SCALE).astype(BF16)

    def after_pair(p, copy):
        copy.wait()
        mine = stacked(p)
        mine[:, 128:] = (kv(r.norm_stage, p)[...] + kv(r.kv_land, p)[...].astype(F32)).astype(BF16)
        grads = mine[...]
        share = dg(grads, r.qkv_pairs[p], NT)
        if p == 0:
            r.norm_land[...] = share
        else:
            r.norm_land[...] += share
        if p == RS - 1:
            return
        weigh_pair(p)

    def weigh_pair(p):
        grads = stacked(p)[...]
        outer = dg(r.normed_t[...], grads, NN)
        half = wide // 2
        r.total[:half, :half] = outer[:half, :]
        r.total[:half, half:] = outer[half:, :]
        r.total[half:, :] = dg(r.mixed[:, whole(p)], r.grad_attn[...], TN)
        item = reduction(2, p, r.down_vmem.at[pl.ds(p * 256, 256)], r.late_sum)
        item.start(r.total)
        late.append(item)
        sums = jnp.sum(grads.astype(F32), axis=0, keepdims=True)
        r.bias_row[:, p * 128 : (p + 1) * 128] = sums[:, :128]
        r.bias_row[:, width + p * 128 : width + (p + 1) * 128] = sums[:, 256:]

    none = jnp.zeros((128, rows), F32)
    prepare(0)
    total = back_half(0, 1, none)
    copy0 = send_kv(0)
    for item in down:
        item.halve(0)
    total = back_half(0, 0, total)
    end_queries(0, total)
    prepare(1)
    total = back_half(1, 1, none)
    copy1 = send_kv(1)
    for item in up:
        item.halve(0)
    total = back_half(1, 0, total)
    end_queries(1, total)
    after_pair(0, copy0)
    for item in down:
        item.halve(1)
    prepare(2)
    total = back_half(2, 1, none)
    copy2 = send_kv(2)
    for item in up:
        item.halve(1)
    for item in down:
        item.halve(2)
        item.cross()
    total = back_half(2, 0, total)
    end_queries(2, total)
    after_pair(1, copy1)
    for item in up:
        item.halve(2)
        item.cross()
    late[0].halve(0)
    after_pair(2, copy2)

    @pl.when(home)
    def _():
        out_copy.wait_send()
        out_keep.wait()

    @pl.when(away)
    def _():
        out_copy.wait_recv()

    share_copies = []
    for at in chunks:
        r.stage[at, :] = r.norm_land[at, :].astype(BF16)
        copy = wires.copy(r.stage.at[at], r.share_land.at[at], place.sibling)
        copy.start()
        share_copies.append(copy)
    weigh_pair(2)

    grad_gain = grad_shift = grad_stream_sum = zero
    frame_copies = []
    for c, at in enumerate(chunks):
        share_copies[c].wait()
        normal, scale = centre(r.frames[at, :].astype(F32) + embedding)
        grad = r.stage[at, :].astype(F32) + r.share_land[at, :].astype(F32)
        grad_shift = grad_shift + jnp.sum(grad, axis=0, keepdims=True)
        grad_gain = grad_gain + jnp.sum(grad * normal, axis=0, keepdims=True)
        grad = grad * gain_one
        grad = (
            grad
            - jnp.mean(grad, axis=1, keepdims=True)
            - normal * jnp.mean(grad * normal, axis=1, keepdims=True)
        ) * scale + r.hidden[at, :]
        grad_stream_sum = grad_stream_sum + jnp.sum(grad, axis=0, keepdims=True)
        r.normed2[at, :] = grad.astype(BF16)
        frame_copy = wires.copy(r.normed2.at[at], r.grad_frames.at[at], place.across)
        frame_keep = pltpu.make_async_copy(
            r.normed2.at[at], r.grad_frames.at[at], r.local_sems.at[3 + c]
        )
        frame_copies.append((frame_copy, frame_keep))

        @pl.when(home)
        def _():
            frame_copy.start()
            frame_keep.start()

    pack = r.pack
    row = lax.broadcasted_iota(jnp.int32, (dp, wide), 0)
    pack[:dp, :] = jnp.where(row == place.clip, grad_stream_sum, 0.0)
    up_sum = jnp.concatenate(up_sums, axis=1)
    items = [
        grad_gain,
        grad_shift,
        grad_out_bias,
        grad_gain_two,
        grad_shift_two,
        grad_down_bias,
        r.bias_row[...],
    ]
    items += [up_sum[:, i * wide : (i + 1) * wide] for i in range(hidden // wide)]
    items.append(r.info[2:3, :])
    row = lax.broadcasted_iota(jnp.int32, (16, wide), 0)
    table = jnp.zeros((16, wide), F32)
    for i, item in enumerate(items):
        table = table + jnp.where(row == i, item, 0.0)
    pack[dp:, :] = table
    steps = [to for to, _ in place.level] + [place.across]
    pack_copies = []

    def pack_step(i):
        copy = wires.copy(r.pack_stage, r.pack_land.at[i], steps[i])
        r.pack_stage[...] = pack[...]
        copy.start()
        pack_copies.append(copy)

    def pack_add(i):
        pack_copies[i].wait()
        pack[...] += r.pack_land[i]

    pack_step(0)
    late[0].halve(1)
    late[1].halve(0)
    for item in down:
        item.land()
    pack_add(0)
    pack_step(1)
    late[2].halve(0)
    late[0].halve(2)
    late[0].cross()
    late[1].halve(1)
    for item in up:
        item.land()
    pack_add(1)
    pack_step(2)
    for item in down:
        item.double(2)
    late[2].halve(1)
    late[1].halve(2)
    late[1].cross()
    late[0].land()
    for item in up:
        item.double(2)
    for i in range(2, len(steps)):
        pack_add(i)
        if i + 1 < len(steps):
            pack_step(i + 1)
    tail_copy = wires.copy(pack.at[pl.ds(dp, 16)], r.pack_tail, place.sibling)
    tail_copy.start()
    for item in down:
        item.double(1)
    late[2].halve(2)
    late[2].cross()
    late[1].land()
    late[0].double(2)
    for item in up:
        item.double(1)
    late[2].land()
    late[1].double(2)
    late[0].double(1)
    for item in down:
        item.double(0)
    late[2].double(2)
    late[1].double(1)
    late[0].double(0)
    for item in up:
        item.double(0)
    late[2].double(1)
    late[1].double(0)
    late[2].double(0)
    tail_copy.wait()

    @pl.when(home)
    def _():
        for copy, local in frame_copies:
            copy.wait_send()
            local.wait()

    @pl.when(away)
    def _():
        for copy, _ in frame_copies:
            copy.wait_recv()

    for item in down + up + late:
        item.finish()


def levels_of(dp):
    levels = 1
    while 2**levels < dp:
        levels += 1
    return levels


def backward(dp, valid, ins):
    rows, width = ins["query"].shape
    wide = ins["normed_t"].shape[0]
    hidden = ins["up"].shape[1]
    levels = levels_of(dp)
    extra = levels - RS
    part = (2 * wide * hidden // (2 * RS * wide), wide)
    half = (part[0] // 2, wide)
    outs = dict(
        output=((rows, wide), BF16),
        grad_frames=((rows, wide), BF16),
        down_sum=((RS,) + part, BF16),
        up_sum=((RS,) + part, BF16),
        late_sum=((RS,) + part, BF16),
        pack=((dp + 16, wide), F32),
        pack_tail=((16, wide), F32),
    )
    wires = 9 * (2 * RS + 2 + RS + extra) + 3 + 3 + 1 + 3 + 3 + 3 + levels + 1 + 1
    square = (rows, wide)
    scratch = dict(
        up_vmem=pltpu.VMEM((wide, hidden), BF16),
        down_vmem=pltpu.VMEM((hidden, wide), BF16),
        hidden=pltpu.VMEM(square, F32),
        normed2=pltpu.VMEM(square, BF16),
        active=pltpu.VMEM((rows, hidden), BF16),
        grad_pre=pltpu.VMEM((rows, hidden), BF16),
        grad_attn=pltpu.VMEM(square, BF16),
        grad_mixed=pltpu.VMEM((rows, width), BF16),
        inner=pltpu.VMEM((8, rows), F32),
        norm_stage=pltpu.VMEM(square, F32),
        norm_land=pltpu.VMEM(square, F32),
        stage=pltpu.VMEM(square, BF16),
        feed_land=pltpu.VMEM(square, BF16),
        share_land=pltpu.VMEM(square, BF16),
        kv_land=pltpu.VMEM(square, BF16),
        total=pltpu.VMEM(part, F32),
        kept=pltpu.VMEM((9,) + half, F32),
        land=pltpu.VMEM((9,) + part, BF16),
        part_stage=pltpu.VMEM((6,) + half, BF16),
        bias_row=pltpu.VMEM((1, 2 * width), F32),
        pack_stage=pltpu.VMEM((dp + 16, wide), F32),
        pack_land=pltpu.VMEM((levels + 1, dp + 16, wide), F32),
        send_sems=pltpu.SemaphoreType.DMA((wires,)),
        recv_sems=pltpu.SemaphoreType.DMA((wires,)),
        part_sems=pltpu.SemaphoreType.DMA((9,)),
        local_sems=pltpu.SemaphoreType.DMA((6,)),
    )
    if extra:
        scratch.update(more_land=pltpu.VMEM((9, extra, part[0] // 8, wide), BF16))
    cost = pl.CostEstimate(flops=2 * 10**10, bytes_accessed=10**8, transcendentals=10**7)
    kernel = functools.partial(backward_kernel, dp, valid)
    hbm = ("up", "down", "output", "grad_frames", "down_sum", "up_sum", "late_sum")
    return call(kernel, "backward", 1, ins, outs, scratch, hbm, cost)


def forward(dp, valid, ins):
    rows, wide = ins["frames"].shape
    width = ins["qkv_local"].shape[2]
    hidden = ins["up_local"].shape[1]
    outs = dict(
        own=((rows, wide), BF16),
        grad_rows=((rows, wide), BF16),
        info=((8, wide), F32),
        bias=((8, wide), F32),
        normed_t=((wide, rows), BF16),
        query=((rows, width), BF16),
        key=((2 * rows, width), BF16),
        value=((2 * rows, width), BF16),
        lse=((width // HEAD, rows), F32),
        mixed=((rows, wide), BF16),
        mixed_rest=((rows, width), BF16),
        qkv_pairs=((width // 128, wide, 384), BF16),
        up=((wide, hidden), BF16),
        down=((hidden, wide), BF16),
        out=((wide, wide), BF16),
    )
    wires = 4 * RS * (1 + RS) + 3 + 6 + 1 + 1 + 3
    scratch = dict(
        other=pltpu.VMEM((rows, wide), BF16),
        normed=pltpu.VMEM((2 * rows, wide), BF16),
        qkv=pltpu.VMEM((3, wide, width), BF16),
        masked=pltpu.VMEM((2, 2 * rows, 128), BF16),
        send_sems=pltpu.SemaphoreType.DMA((wires,)),
        recv_sems=pltpu.SemaphoreType.DMA((wires,)),
        local_sems=pltpu.SemaphoreType.DMA((6,)),
    )
    hbm = (
        "qkv_local",
        "grad_local",
        "up_local",
        "down_local",
        "out_local",
    )
    cost = pl.CostEstimate(flops=10**10, bytes_accessed=10**7, transcendentals=10**7)
    kernel = functools.partial(forward_kernel, dp, valid)
    return call(kernel, "forward", 2, ins, outs, scratch, hbm, cost)


def finish_kernel(valid, r):
    wide = r.down.shape[1]
    half = wide // 2
    for p in range(RS):
        r.down[p * 512 : (p + 1) * 512, :] = r.down_sum[p].astype(F32)
        chunk = r.up.shape[0] // RS
        at = pl.ds(p * chunk, chunk)
        for i in range(r.up.shape[1] // wide):
            r.up[at, i * wide : (i + 1) * wide] = r.up_sum[p, i * chunk : (i + 1) * chunk, :].astype(
                F32
            )
        for j in range(3):
            for i in range(2):
                columns = pl.ds(i * half + j * 128, 128)
                r.qkv[j, i * half : (i + 1) * half, p * 128 : (p + 1) * 128] = r.late_sum[
                    p, :half, columns
                ].astype(F32)
        r.out[p * 128 : (p + 1) * 128, :] = r.late_sum[p, half:, :].astype(F32)
    r.output[...] = r.output_rows[:valid, :]
    r.grad_frames[...] = r.grad_rows[:valid, :]


def finish(valid, ins, width):
    wide = ins["output_rows"].shape[1]
    hidden = ins["down_sum"].shape[1] * RS
    outs = dict(
        output=((valid, wide), BF16),
        grad_frames=((valid, wide), BF16),
        down=((hidden, wide), F32),
        up=((wide, hidden), F32),
        qkv=((3, wide, width), F32),
        out=((width, wide), F32),
    )
    return call(functools.partial(finish_kernel, valid), "finish", None, ins, outs, {}, (), None)


def on_device(
    sizes,
    frames,
    languages,
    present,
    lang_table,
    norm1_gain,
    norm1_shift,
    qkv_weight,
    qkv_bias,
    out_weight,
    out_bias,
    norm2_gain,
    norm2_shift,
    up_weight,
    up_bias,
    down_weight,
    down_bias,
    grad_out,
):
    d, t, s = (lax.axis_index(name) for name in AXES)
    home = d % 2 == t
    clips = sizes["dp"]
    _, valid, width = frames.shape
    rows = -(-valid // 256) * 256
    head_width = qkv_weight.shape[2]
    langs = lang_table.shape[0]
    pad = ((0, rows - valid), (0, 0))

    one_hot = (languages[:, None] == lax.broadcasted_iota(jnp.int32, (1, langs), 1)).astype(F32)
    embedding = jnp.dot(one_hot, lang_table.astype(F32), precision=lax.Precision.HIGHEST)
    lane = lax.broadcasted_iota(jnp.int32, (1, width), 1)
    once = jnp.where(s == 0, languages[:, None].astype(F32), 0.0)
    info = jnp.concatenate(
        [
            embedding,
            jnp.broadcast_to(present[:, None].astype(F32), (1, width)),
            jnp.where(lane == d, once, 0.0),
            jnp.zeros((5, width), F32),
        ]
    )
    biases = jnp.concatenate([qkv_bias.reshape(1, width), up_bias.reshape(-1, width)]).astype(F32)
    gain_one, shift_one = norm1_gain.astype(F32)[None], norm1_shift.astype(F32)[None]
    f = forward(
        clips,
        valid,
        dict(
            frames=jnp.pad(frames[0], pad),
            grad_local=jnp.pad(grad_out[0], pad),
            info_local=info,
            bias_local=jnp.pad(biases, ((0, 8 - biases.shape[0]), (0, 0))),
            gain=gain_one,
            shift=shift_one,
            qkv_local=qkv_weight,
            up_local=up_weight,
            down_local=down_weight,
            out_local=out_weight,
        ),
    )
    vectors = jnp.stack([norm1_gain, norm2_gain, norm2_shift, out_bias, down_bias]).astype(F32)
    b = backward(
        clips,
        valid,
        dict(
            query=f.query,
            key=f.key,
            value=f.value,
            lse=f.lse,
            mixed=f.mixed,
            mixed_rest=f.mixed_rest,
            frames=f.own,
            grad_rows=f.grad_rows,
            normed_t=f.normed_t,
            qkv_pairs=f.qkv_pairs,
            out=f.out,
            up=f.up,
            down=f.down,
            info=f.info,
            bias=f.bias,
            vectors=jnp.pad(vectors, ((0, 3), (0, 0))),
        ),
    )
    v = b.pack[clips:]
    tail = jnp.where(home, v, b.pack_tail)
    o = finish(
        valid,
        dict(
            output_rows=b.output,
            grad_rows=b.grad_frames,
            down_sum=b.down_sum,
            up_sum=b.up_sum,
            late_sum=b.late_sum,
        ),
        head_width,
    )
    ids = v[9, :clips][:, None]
    hot = (ids == lax.broadcasted_iota(jnp.int32, (1, langs), 1).astype(F32)).astype(F32)
    grad_lang_table = lax.dot_general(
        hot, b.pack[:clips], (((0,), (0,)), ((), ())), precision=lax.Precision.HIGHEST
    )
    return (
        o.output[None],
        o.grad_frames[None],
        grad_lang_table,
        v[0],
        v[1],
        o.qkv,
        tail[6].reshape(2, head_width),
        o.out,
        v[2],
        v[3],
        v[4],
        o.up,
        tail[7:9].reshape(-1),
        o.down,
        v[5],
    )


def solution(mesh):
    rows = P("dp", "seq", None)
    columns, one = P(None, "tensor"), P("dp")
    placed = (
        rows,
        one,
        one,
        P(),
        P(),
        P(),
        P(None, None, "tensor"),
        columns,
        P("tensor", None),
        P(),
        P(),
        P(),
        columns,
        P("tensor"),
        P("tensor", None),
        P(),
        rows,
    )
    out = (
        rows,
        rows,
        P(),
        P(),
        P(),
        P(None, None, "tensor"),
        columns,
        P("tensor", None),
        P(),
        P(),
        P(),
        columns,
        P("tensor"),
        P("tensor", None),
        P(),
    )
    return jax.shard_map(
        functools.partial(on_device, dict(mesh.shape)),
        mesh=mesh,
        in_specs=placed,
        out_specs=out,
        check_vma=False,
    )
```

```python
import functools
import types

import jax
import jax.numpy as jnp
from jax import lax
from jax.experimental import pallas as pl
from jax.experimental.pallas import tpu as pltpu
from jax.sharding import PartitionSpec as P

HEAD = 64
EPSILON = 1e-05
QUERY_SCALE = 0.125
AXES = ("dp", "tensor", "seq")
F32 = jnp.float32
BF16 = jnp.bfloat16
NN = (((1,), (0,)), ((), ()))
NT = (((1,), (1,)), ((), ()))
TN = (((0,), (0,)), ((), ()))
VMEM = pl.BlockSpec(memory_space=pltpu.VMEM)
ANY = pl.BlockSpec(memory_space=pl.ANY)
RS = 3


ORDERS = (
    (0, 2, 1),
    (0, 1, 2),
    (2, 1, 0),
    (1, 2, 0),
    (2, 1, 0),
    (1, 2, 0),
    (1, 2, 0),
    (1, 2, 0),
    (1, 2, 0),
    (1, 2, 0),
    (2, 1, 0),
    (2, 1, 0),
    (1, 2, 0),
    (0, 2, 1),
    (0, 2, 1),
)
SCHEDULE = (
    (),
    (),
    (),
    (),
    (),
    (0, 2, 3),
    (1,),
    (),
    (4, 5),
    (2, 0, 3),
    (1,),
    (),
    (5,),
    (1, 4, 0, 2),
    (3, 6, 5, 7, 1),
    (0, 8),
    (2, 6, 7, 0, 3, 1),
    (),
    (8, 5),
    (9, 4),
    (),
    (2, 6, 10, 1, 7),
    (3,),
    (4, 11, 8, 5),
    (7, 6),
    (0, 12, 13, 9, 2, 3, 10, 14, 11, 5, 12, 1, 13, 4, 7, 6, 3),
    (2, 14, 5, 7, 13, 6, 0, 9, 8, 4, 10, 11),
    (12, 14, 8, 7, 6, 4),
    (13, 8, 9, 10, 11, 12, 13, 14, 9, 10, 8),
    (11, 12, 13, 14, 9, 10, 11, 12, 14, 13, 9, 10, 12, 11, 14),
)


def dg(left, right, dims):
    return lax.dot_general(left, right, dims, preferred_element_type=F32)


def rows_at(start, size):
    return pl.ds(pl.multiple_of(start, 16), size)


class Place:
    def __init__(self, dp):
        self.d, self.t, self.s = (lax.axis_index(name) for name in AXES)
        self.core = lax.rem(self.d, 2)
        self.home = self.core == self.t
        self.away = jnp.logical_not(self.home)
        self.clip = self.d - self.core + self.t
        self.sibling = (self.d + 1 - 2 * self.core, self.t, self.s)
        self.across = (self.d, 1 - self.t, self.s)
        self.level = [((self.d, self.t, 1 - self.s), self.s)]
        bit = 2
        while bit < dp:
            value = lax.rem(self.d // bit, 2)
            self.level.append(((self.d + bit - 2 * bit * value, self.t, self.s), value))
            bit *= 2
        self.peers = [self.sibling, self.across] + [to for to, _ in self.level]

    def enter(self):
        barrier = pltpu.get_barrier_semaphore()
        for to in self.peers:
            pl.semaphore_signal(barrier, inc=1, device_id=to, device_id_type=pl.DeviceIdType.MESH)
        pl.semaphore_wait(barrier, len(self.peers))

    def order(self, numbers):
        levels = [self.level[i] for i in numbers]
        return [to for to, _ in levels], [bit for _, bit in levels]


class Wires:
    def __init__(self, send_sems, recv_sems):
        self.send_sems, self.recv_sems, self.used = send_sems, recv_sems, 0

    def copy(self, src, dst, to):
        i = self.used
        self.used += 1
        return pltpu.make_async_remote_copy(
            src_ref=src,
            dst_ref=dst,
            send_sem=self.send_sems.at[i],
            recv_sem=self.recv_sems.at[i],
            device_id=to,
            device_id_type=pl.DeviceIdType.MESH,
        )


class Fetch:
    def __init__(self, place, wires, part, local, result):
        self.to, self.bits = place.order([(part + j) % RS for j in range(RS)])
        self.place, self.wires, self.result = place, wires, result
        self.slice = local.shape[0] // 2**RS
        self.at = self.slice * (4 * self.bits[0] + 2 * self.bits[1] + self.bits[2])
        at = rows_at(self.at, self.slice)
        self.crossing = wires.copy(local.at[at], result.at[at], place.across)

        @pl.when(place.home)
        def _():
            self.crossing.start()

    def widen(self, j):
        size = self.slice * 2 ** (RS - 1 - j)
        ref = self.result.at[rows_at(self.at, size)]
        self.at = self.at - self.bits[j] * size
        return self.wires.copy(ref, ref, self.to[j])

    def arrive(self):
        self.moving = self.widen(RS - 1)

        @pl.when(self.place.home)
        def _():
            self.crossing.wait_send()

        @pl.when(self.place.away)
        def _():
            self.crossing.wait_recv()
            self.moving.start()

    def double(self, j):
        before = self.moving
        if j:
            self.moving = self.widen(j - 1)

        @pl.when(self.place.away)
        def _():
            before.wait()
            if j:
                self.moving.start()


class Reduction:
    def __init__(self, place, wires, order, kept, land, more, stage, result, sem):
        self.to, self.bits = place.order(order)
        self.place, self.wires, self.stage, self.result = place, wires, stage, result
        self.kept, self.land_ref = kept, land
        self.extra = list(zip(place.level[RS:], more))
        self.local = lambda src, dst: pltpu.make_async_copy(src, dst, sem)
        self.steps = [
            functools.partial(self.halve, 0),
            functools.partial(self.halve, 1),
            self.cross,
            self.land,
            functools.partial(self.double, 2),
            functools.partial(self.double, 1),
            functools.partial(self.double, 0),
        ]
        self.slice = result.shape[0] // 2**RS
        self.low = 0
        self.at = self.bits[0] * 4 * self.slice
        self.forwards = []
        sizes = [4, 2, 1, 1]
        starts = [sum(sizes[:i]) for i in range(4)]
        self.lands = [
            self.land_ref.at[pl.ds(start * self.slice, size * self.slice)]
            for start, size in zip(starts, sizes)
        ]
        self.last = stage.at[pl.ds(3 * self.slice, self.slice)]

    def start(self, total):
        half = 4 * self.slice
        bit = self.bits[0]
        self.stage[...] = total[rows_at((1 - bit) * half, half), :].astype(BF16)
        self.moving = self.wires.copy(self.stage, self.lands[0], self.to[0])
        self.moving.start()
        self.kept[...] = total[rows_at(bit * half, half), :]

    def halve(self, j):
        self.moving.wait()
        half = self.slice * 2 ** (RS - 2 - j)
        bit = self.bits[j + 1]
        away, home = (1 - bit) * half, bit * half
        stage = self.stage.at[pl.ds(0 if j == 0 else 2 * self.slice, half)]
        stage[...] = (
            self.kept[rows_at(self.low + away, half), :]
            + self.lands[j][rows_at(away, half), :].astype(F32)
        ).astype(BF16)
        self.moving = self.wires.copy(stage, self.lands[j + 1], self.to[j + 1])
        self.moving.start()
        self.kept[rows_at(self.low + home, half), :] += self.lands[j][
            rows_at(home, half), :
        ].astype(F32)
        self.low = self.low + home
        self.at = self.at + home

    def cross(self):
        self.moving.wait()
        now = rows_at(self.low, self.slice)
        self.kept[now, :] += self.lands[RS - 1][...].astype(F32)
        for (to, _), land in self.extra:
            self.last[...] = self.kept[now, :].astype(BF16)
            copy = self.wires.copy(self.last, land, to)
            copy.start()
            copy.wait()
            self.kept[now, :] = self.last[...].astype(F32) + land[...].astype(F32)
        self.crossing = self.wires.copy(self.last, self.lands[RS], self.place.across)

        @pl.when(self.place.away)
        def _():
            self.last[...] = self.kept[now, :].astype(BF16)
            self.crossing.start()

    def spread(self, src, start, size):
        ref = self.result.at[rows_at(start, size)]
        forward = self.wires.copy(ref if src is None else src, ref, self.place.sibling)
        self.forwards.append(forward)
        return forward

    def widen(self, src, j):
        ref = self.result.at[rows_at(self.at, self.slice * 2 ** (RS - 1 - j))]
        return self.wires.copy(ref if src is None else src, ref, self.to[j])

    def land(self):
        first = self.spread(self.last, self.at, self.slice)
        self.moving = self.widen(self.last, RS - 1)
        self.writing = self.local(self.last, self.result.at[rows_at(self.at, self.slice)])

        @pl.when(self.place.home)
        def _():
            self.crossing.wait_recv()
            self.last[...] = (
                self.kept[rows_at(self.low, self.slice), :] + self.lands[RS][...].astype(F32)
            ).astype(BF16)
            self.moving.start()
            first.start()
            self.writing.start()

        @pl.when(self.place.away)
        def _():
            self.crossing.wait_send()

    def double(self, j):
        size = self.slice * 2 ** (RS - 1 - j)
        bit = self.bits[j]
        came = self.at + (1 - 2 * bit) * size
        self.at = self.at - bit * size
        before, forward = self.moving, self.spread(None, came, size)
        if j:
            self.moving = self.widen(None, j - 1)

        @pl.when(self.place.home)
        def _():
            before.wait()
            if j == RS - 1:
                self.writing.wait()
            if j:
                self.moving.start()
            forward.start()

    def finish(self):
        @pl.when(self.place.home)
        def _():
            for forward in self.forwards:
                forward.wait_send()

        @pl.when(self.place.away)
        def _():
            for forward in self.forwards:
                forward.wait_recv()


def pair_lanes(rows):
    return lax.broadcasted_iota(jnp.int32, (rows, 128), 1)


def one_head(pair, e, extra=None):
    lane = pair_lanes(pair.shape[0])
    own = (lane < HEAD) if e == 0 else (lane >= HEAD)
    kept = jnp.where(own, pair, jnp.zeros_like(pair))
    if extra is not None:
        kept = jnp.where(lane == (HEAD if e == 0 else 0), extra, kept)
    return kept


def masked_keys(key_ref, columns, masked, rows, valid):
    row = lax.broadcasted_iota(jnp.int32, (rows, 128), 0)
    bias = jnp.where(row >= valid, -1e30, 0.0).astype(BF16)
    for e in range(2):
        for part in range(2):
            at = pl.ds(part * rows, rows)
            masked[e, at, :] = one_head(key_ref[at, columns], e, bias)


def centre(inputs):
    centred = inputs - jnp.mean(inputs, axis=1, keepdims=True)
    scale = lax.rsqrt(jnp.mean(centred * centred, axis=1, keepdims=True) + EPSILON)
    return centred * scale, scale


def call(kernel, name, collective, ins, outs, scratch, hbm, cost):
    names = list(ins) + list(outs) + list(scratch)

    def body(*refs):
        named = dict(zip(names, refs))
        plain = {name: ref for name, ref in named.items() if isinstance(name, str)}
        kernel(types.SimpleNamespace(table=named, **plain))

    results = pl.pallas_call(
        body,
        out_shape=[jax.ShapeDtypeStruct(*item) for item in outs.values()],
        in_specs=[ANY if item in hbm else VMEM for item in ins],
        out_specs=[ANY if item in hbm else VMEM for item in outs],
        scratch_shapes=list(scratch.values()),
        compiler_params=pltpu.CompilerParams(
            collective_id=collective,
            has_side_effects=collective is not None,
            vmem_limit_bytes=60 * 2**20,
        ),
        cost_estimate=cost,
        name=name,
    )(*ins.values())
    return types.SimpleNamespace(**dict(zip(outs, results)))


def forward_kernel(dp, valid, r):
    place = Place(dp)
    place.enter()
    wires = Wires(r.send_sems, r.recv_sems)
    rows, wide = r.frames.shape
    width = r.query.shape[1]
    home, away = place.home, place.away
    chunk = rows // 3

    first = [Fetch(place, wires, j, r.qkv_local.at[j], r.qkv.at[j]) for j in range(3)]
    info = wires.copy(r.info_local, r.info, place.sibling)
    bias = wires.copy(r.bias_local, r.bias, place.across)
    own = wires.copy(r.frames, r.own, place.sibling)
    beside, onward = [], []
    for c in range(3):
        at = pl.ds(c * chunk, chunk)
        beside.append(wires.copy(r.frames.at[at], r.other.at[at], place.level[0][0]))
        onward.append(wires.copy(r.other.at[at], r.other.at[at], place.sibling))
    grads = wires.copy(r.grad_local, r.grad_rows, place.sibling)
    own_out = r.out.at[rows_at(place.core * width, width)]
    keep = [
        pltpu.make_async_copy(src, dst, r.local_sems.at[i])
        for i, (src, dst) in enumerate(
            (
                (r.qkv_local, r.qkv),
                (r.grad_local, r.grad_rows),
                (r.up_local, r.up),
                (r.down_local, r.down),
                (r.out_local, own_out),
            )
        )
    ]
    other_out = r.out.at[rows_at((1 - place.core) * width, width)]
    lend = pltpu.make_async_copy(r.out_local, other_out, r.local_sems.at[len(keep)])
    lent = wires.copy(own_out, own_out, place.sibling)

    @pl.when(home)
    def _():
        info.start()
        bias.start()
        own.start()
        for copy in beside:
            copy.start()
        for copy in keep:
            copy.start()
        r.info[...] = r.info_local[...]
        r.bias[...] = r.bias_local[...]
        r.own[...] = r.frames[...]

    @pl.when(away)
    def _():
        lend.start()

    later = []
    for part in range(RS):
        for local, result in ((r.down_local, r.down), (r.up_local, r.up), (r.out_local, own_out)):
            size = local.shape[0] // RS
            at = pl.ds(part * size, size)
            later.append(Fetch(place, wires, part, local.at[at], result.at[at]))

    @pl.when(home)
    def _():
        grads.start()

    for item in first:
        item.arrive()

    @pl.when(away)
    def _():
        info.wait_recv()
        own.wait_recv()
        bias.wait_recv()

    embedding = r.info[0:1, :]

    def norm(source, c, to):
        normal, _ = centre(source[pl.ds(c * chunk, chunk), :].astype(F32) + embedding)
        normed = normal * r.gain[...] + r.shift[...]
        r.normed[pl.ds(to + c * chunk, chunk), :] = normed.astype(BF16)
        return normed

    for c in range(3):
        r.normed_t[:, c * chunk : (c + 1) * chunk] = norm(r.own, c, 0).T.astype(BF16)
        if c == 1:
            for item in first:
                item.double(2)

        @pl.when(home)
        def _():
            beside[c].wait()
            onward[c].start()

    for item in first:
        item.double(1)
    for c in range(3):

        @pl.when(away)
        def _():
            onward[c].wait_recv()

        norm(r.other, c, rows)
    for item in first:
        item.double(0)
    for item in later:
        item.arrive()

    @pl.when(home)
    def _():
        keep[0].wait()

    r.query[...] = (
        (dg(r.normed[:rows, :], r.qkv[0], NN) + r.bias[0:1, :width]) * QUERY_SCALE
    ).astype(BF16)
    for part in range(2):
        at = pl.ds(part * rows, rows)
        r.key[at, :] = dg(r.normed[at, :], r.qkv[1], NN).astype(BF16)
        r.value[at, :] = (dg(r.normed[at, :], r.qkv[2], NN) + r.bias[0:1, width:]).astype(BF16)
    for item in later:
        item.double(2)

    block = 256
    mixed_copies = []

    def one_pair(p):
        columns = pl.ds(p * 128, 128)
        whole = pl.ds(pl.multiple_of(place.core * width + p * 128, 128), 128)
        masked_keys(r.key, columns, r.masked, rows, valid)
        for j in range(3):
            r.qkv_pairs[p, :, j * 128 : (j + 1) * 128] = r.qkv[j, :, columns]

        def one_block(i, _):
            at = pl.ds(pl.multiple_of(i * block, block), block)
            parts, rests = [], []
            for e in range(2):
                queries = one_head(r.query[at, columns], e, jnp.ones((), BF16))
                scores = dg(queries, r.masked[e], NT)
                top = jnp.max(scores, axis=1, keepdims=True)
                weights = jnp.exp(scores - top)
                total = jnp.sum(weights, axis=1, keepdims=True)
                weights = weights * (1.0 / total)
                low = weights.astype(BF16)
                rest = (weights - low.astype(F32)).astype(BF16)
                parts.append(dg(low, r.value[:, columns], NN))
                rests.append(dg(rest, r.value[:, columns], NN))
                r.lse[pl.ds(2 * p + e, 1), at] = (top + jnp.log(total)).reshape(1, block)
            first = pair_lanes(block) < HEAD
            mixed = jnp.where(first, parts[0], parts[1])
            low = mixed.astype(BF16)
            r.mixed[at, whole] = low
            rest = mixed - low.astype(F32) + jnp.where(first, rests[0], rests[1])
            r.mixed_rest[at, columns] = rest.astype(BF16)
            return 0

        lax.fori_loop(0, rows // block, one_block, 0)
        copy = wires.copy(r.mixed.at[:, whole], r.mixed.at[:, whole], place.sibling)
        copy.start()
        mixed_copies.append(copy)

    one_pair(0)
    for item in later:
        item.double(1)
    one_pair(1)
    for item in later:
        item.double(0)
    one_pair(2)

    @pl.when(away)
    def _():
        lend.wait()
        lent.start()
        grads.wait_recv()
        lent.wait_send()

    @pl.when(home)
    def _():
        lent.wait_recv()
        for copy in keep[1:]:
            copy.wait()
        info.wait_send()
        bias.wait_send()
        own.wait_send()
        grads.wait_send()
        for copy in onward:
            copy.wait_send()

    for c in range(3):
        at = pl.ds(c * chunk, chunk)
        r.grad_rows[at, :] = (r.grad_rows[at, :].astype(F32) * r.info[1:2, :]).astype(BF16)
    for copy in mixed_copies:
        copy.wait()


def gelu_pair(inputs):
    half = 0.5 + 0.5 * lax.erf(inputs * 0.7071067811865476)
    slope = inputs * (jnp.exp(inputs * inputs * -0.5) * 0.3989422804014327)
    return inputs * half, half + slope


def backward_kernel(dp, valid, r):
    place = Place(dp)
    place.enter()
    wires = Wires(r.send_sems, r.recv_sems)
    rows, width = r.query.shape
    wide = r.normed_t.shape[0]
    hidden = r.up.shape[1]
    home, away = place.home, place.away
    chunk = rows // 3
    chunks = [pl.ds(c * chunk, chunk) for c in range(3)]
    embedding, keep = r.info[0:1, :], r.info[1:2, :]
    gain_one, gain_two, shift_two, out_bias, down_bias = (r.vectors[i : i + 1, :] for i in range(5))
    zero = jnp.zeros((1, wide), F32)

    bring = [
        pltpu.make_async_copy(src, dst, r.local_sems.at[i])
        for i, (src, dst) in enumerate(((r.up, r.up_vmem), (r.down, r.down_vmem)))
    ]
    for copy in bring:
        copy.start()

    for at in chunks:
        attention = dg(r.mixed[at, :], r.out[...], NN)
        rows_in = r.frames[at, :].astype(F32) + embedding + attention + out_bias
        r.hidden[at, :] = rows_in
        normal, _ = centre(rows_in)
        r.normed2[at, :] = (normal * gain_two + shift_two).astype(BF16)

    for copy in bring:
        copy.wait()
    block = 512
    up_sums = [jnp.zeros((1, block), F32) for _ in range(hidden // block)]
    for at in chunks:
        for h in range(hidden // block):
            units = pl.ds(h * block, block)
            start = h * block
            bias = r.bias[1 + start // wide : 2 + start // wide, start % wide : start % wide + block]
            if start % wide + block > wide:
                bias = jnp.concatenate(
                    [
                        r.bias[1 + start // wide : 2 + start // wide, start % wide :],
                        r.bias[2 + start // wide : 3 + start // wide, : start % wide + block - wide],
                    ],
                    axis=1,
                )
            active, slope = gelu_pair(dg(r.normed2[at, :], r.up_vmem[:, units], NN) + bias)
            r.active[at, units] = active.astype(BF16)
            grad = dg(r.grad_rows[at, :], r.down_vmem[units, :], NT)
            low = (grad * slope).astype(BF16)
            r.grad_pre[at, units] = low
            up_sums[h] = up_sums[h] + jnp.sum(low.astype(F32), axis=0, keepdims=True)
    norm_copies, feed_copies = [], []
    for at in chunks:
        r.norm_stage[at, :] = dg(r.grad_pre[at, :], r.up_vmem[...], NT)
        copy = wires.copy(r.norm_stage.at[at], r.norm_land.at[at], place.sibling)
        copy.start()
        norm_copies.append(copy)
    for at in chunks:
        r.stage[at, :] = dg(r.active[at, :], r.down_vmem[...], NN).astype(BF16)
        copy = wires.copy(r.stage.at[at], r.feed_land.at[at], place.sibling)
        copy.start()
        feed_copies.append(copy)

    parts = []

    def reduction(slot, cut, stage, result):
        number = len(parts)
        views = [ref.at[:, cut] for ref in (r.kept.at[slot], r.land.at[slot])]
        more = [r.more_land.at[slot, i].at[:, cut] for i in range(len(place.level) - RS)]
        item = Reduction(
            place,
            wires,
            ORDERS[number],
            *views,
            more,
            stage.at[:, cut],
            result.at[:, cut],
            r.part_sems.at[number],
        )
        item.start(r.total.at[:, cut])
        parts.append(item)

    groups = iter(SCHEDULE)

    def tick():
        for number in next(groups):
            parts[number].steps.pop(0)()

    every = pl.ds(0, wide)
    for p in range(RS):
        columns = pl.ds(p * block, block)
        r.total[...] = dg(r.active[:, columns], r.grad_rows[...], TN)
        reduction(p, every, r.part_stage.at[p], r.down_sum.at[p])
    for p in range(RS):
        columns = pl.ds(p * chunk, chunk)
        outer = dg(r.normed2[:, columns], r.grad_pre[...], TN)
        r.total[:chunk, :] = outer[:, :wide]
        r.total[chunk:, :] = outer[:, wide:]
        reduction(RS + p, every, r.part_stage.at[RS + p], r.up_sum.at[p])

    grad_gain_two = grad_shift_two = grad_out_bias = grad_down_bias = zero
    for c, at in enumerate(chunks):
        tick()
        norm_copies[c].wait()
        feed_copies[c].wait()
        rows_in = r.hidden[at, :]
        normal, scale = centre(rows_in)
        feed = r.stage[at, :].astype(F32) + r.feed_land[at, :].astype(F32)
        r.stage[at, :] = (keep * (rows_in + feed + down_bias)).astype(BF16)
        grad = r.norm_stage[at, :] + r.norm_land[at, :]
        grad_shift_two = grad_shift_two + jnp.sum(grad, axis=0, keepdims=True)
        grad_gain_two = grad_gain_two + jnp.sum(grad * normal, axis=0, keepdims=True)
        grad = grad * gain_two
        grad = (
            grad
            - jnp.mean(grad, axis=1, keepdims=True)
            - normal * jnp.mean(grad * normal, axis=1, keepdims=True)
        ) * scale
        grad_out = r.grad_rows[at, :].astype(F32)
        grad_down_bias = grad_down_bias + jnp.sum(grad_out, axis=0, keepdims=True)
        grad = grad + grad_out
        grad_out_bias = grad_out_bias + jnp.sum(grad, axis=0, keepdims=True)
        r.hidden[at, :] = grad
        low = grad.astype(BF16)
        r.grad_attn[at, :] = low
        r.grad_mixed[at, :] = dg(low, r.out[rows_at(place.core * width, width), :], NT).astype(BF16)
    out_copy = wires.copy(r.stage, r.output, place.across)
    out_keep = pltpu.make_async_copy(r.stage, r.output, r.local_sems.at[2])

    @pl.when(home)
    def _():
        out_copy.start()
        out_keep.start()

    def masked(e, part):
        return r.grad_pre.at[:, pl.ds((2 * e + part) * 128, 128)]

    def operand(i):
        return r.grad_pre.at[:, pl.ds((4 + i) * 128, 128)]

    def kv(ref, p):
        return ref.at[:, pl.ds(p * 256, 256)]

    def whole(p):
        return pl.ds(pl.multiple_of(place.core * width + p * 128, 128), 128)

    row = lax.broadcasted_iota(jnp.int32, (rows, 128), 0)
    pad = jnp.where(row >= valid, -1e30, 0.0).astype(BF16)

    def prepare(p):
        columns = pl.ds(p * 128, 128)
        grad = r.grad_mixed[:, columns]
        product = grad.astype(F32) * (
            r.mixed[:, whole(p)].astype(F32) + r.mixed_rest[:, columns].astype(F32)
        )
        query = r.query[:, columns]
        lane = pair_lanes(rows)
        for e in range(2):
            for part in range(2):
                masked(e, part)[...] = one_head(r.key[pl.ds(part * rows, rows), columns], e, pad)
            operand(e)[...] = one_head(query, e, jnp.ones((), BF16))
            operand(2 + e)[...] = one_head(query, e)
            operand(4 + e)[...] = one_head(grad, e)
            own = (lane < HEAD) if e == 0 else (lane >= HEAD)
            r.inner[e : e + 1, :] = jnp.sum(
                jnp.where(own, product, 0.0), axis=1, keepdims=True
            ).reshape(1, rows)

    def back_half(p, part, total):
        columns = pl.ds(p * 128, 128)
        size = 384
        store = kv(r.norm_stage if part == 0 else r.normed2, p)

        def one_block(i, total):
            at = pl.ds(pl.multiple_of(i * size, size), size)
            from_all = pl.ds(pl.multiple_of(part * rows + i * size, size), size)
            grad_keys, grad_values = [], []
            for e in range(2):
                scores = dg(masked(e, part)[at, :], operand(e)[...], NT)
                weights = jnp.exp(scores - r.lse[2 * p + e : 2 * p + e + 1, :])
                grad_weights = dg(r.value[from_all, columns], operand(4 + e)[...], NT)
                grad_scores = (weights * (grad_weights - r.inner[e : e + 1, :])).astype(BF16)
                grad_values.append(dg(weights.astype(BF16), operand(4 + e)[...], NN))
                grad_keys.append(dg(grad_scores, operand(2 + e)[...], NN))
                total = total + dg(one_head(r.key[from_all, columns], e), grad_scores, TN)
            store[at, :128] = (grad_keys[0] + grad_keys[1]).astype(store.dtype)
            store[at, 128:] = (grad_values[0] + grad_values[1]).astype(store.dtype)
            return total

        return lax.fori_loop(0, rows // size, one_block, total)

    def send_kv(p):
        copy = wires.copy(kv(r.normed2, p), kv(r.kv_land, p), place.level[0][0])
        copy.start()
        return copy

    def stacked(p):
        return r.active.at[:, pl.ds(p * 384, 384)]

    def end_queries(p, total):
        low = total.T.astype(BF16)
        stacked(p)[:, :128] = (low.astype(F32) * QUERY_SCALE).astype(BF16)

    def after_pair(p, copy):
        copy.wait()
        mine = stacked(p)
        mine[:, 128:] = (kv(r.norm_stage, p)[...] + kv(r.kv_land, p)[...].astype(F32)).astype(BF16)
        grads = mine[...]
        share = dg(grads, r.qkv_pairs[p], NT)
        if p == 0:
            r.norm_land[...] = share
        else:
            r.norm_land[...] += share

    def weigh_pair(p):
        grads = stacked(p)[...]
        outer = dg(r.normed_t[...], grads, NN)
        half = wide // 2
        r.total[:half, :half] = outer[:half, :]
        r.total[:half, half:] = outer[half:, :]
        r.total[half:, :] = dg(r.mixed[:, whole(p)], r.grad_attn[...], TN)
        for q in range(3):
            stage = r.down_vmem.at[pl.ds(p * 256, 256)]
            reduction(2 * RS + p, pl.ds(q * 256, 256), stage, r.late_sum.at[p])
        sums = jnp.sum(grads.astype(F32), axis=0, keepdims=True)
        r.bias_row[:, p * 128 : (p + 1) * 128] = sums[:, :128]
        r.bias_row[:, width + p * 128 : width + (p + 1) * 128] = sums[:, 256:]

    none = jnp.zeros((128, rows), F32)
    kv_copies = []
    for p in range(3):
        tick()
        prepare(p)
        tick()
        total = back_half(p, 1, none)
        kv_copies.append(send_kv(p))
        tick()
        total = back_half(p, 0, total)
        end_queries(p, total)
        if p:
            tick()
            after_pair(p - 1, kv_copies[p - 1])
            tick()
            weigh_pair(p - 1)
    tick()
    after_pair(2, kv_copies[2])

    @pl.when(home)
    def _():
        out_copy.wait_send()
        out_keep.wait()

    @pl.when(away)
    def _():
        out_copy.wait_recv()

    share_copies = []
    for at in chunks:
        tick()
        r.stage[at, :] = r.norm_land[at, :].astype(BF16)
        copy = wires.copy(r.stage.at[at], r.share_land.at[at], place.sibling)
        copy.start()
        share_copies.append(copy)
    tick()
    weigh_pair(2)

    grad_gain = grad_shift = grad_stream_sum = zero
    frame_copies = []
    for c, at in enumerate(chunks):
        tick()
        share_copies[c].wait()
        normal, scale = centre(r.frames[at, :].astype(F32) + embedding)
        grad = r.stage[at, :].astype(F32) + r.share_land[at, :].astype(F32)
        grad_shift = grad_shift + jnp.sum(grad, axis=0, keepdims=True)
        grad_gain = grad_gain + jnp.sum(grad * normal, axis=0, keepdims=True)
        grad = grad * gain_one
        grad = (
            grad
            - jnp.mean(grad, axis=1, keepdims=True)
            - normal * jnp.mean(grad * normal, axis=1, keepdims=True)
        ) * scale + r.hidden[at, :]
        grad_stream_sum = grad_stream_sum + jnp.sum(grad, axis=0, keepdims=True)
        r.normed2[at, :] = grad.astype(BF16)
        frame_copy = wires.copy(r.normed2.at[at], r.grad_frames.at[at], place.across)
        frame_keep = pltpu.make_async_copy(
            r.normed2.at[at], r.grad_frames.at[at], r.local_sems.at[3 + c]
        )
        frame_copies.append((frame_copy, frame_keep))

        @pl.when(home)
        def _():
            frame_copy.start()
            frame_keep.start()

    tick()
    pack = r.pack
    row = lax.broadcasted_iota(jnp.int32, (dp, wide), 0)
    pack[:dp, :] = jnp.where(row == place.clip, grad_stream_sum, 0.0)
    up_sum = jnp.concatenate(up_sums, axis=1)
    items = [
        grad_gain,
        grad_shift,
        grad_out_bias,
        grad_gain_two,
        grad_shift_two,
        grad_down_bias,
        r.bias_row[...],
    ]
    items += [up_sum[:, i * wide : (i + 1) * wide] for i in range(hidden // wide)]
    items.append(r.info[2:3, :])
    row = lax.broadcasted_iota(jnp.int32, (16, wide), 0)
    table = jnp.zeros((16, wide), F32)
    for i, item in enumerate(items):
        table = table + jnp.where(row == i, item, 0.0)
    pack[dp:, :] = table
    steps = [to for to, _ in place.level] + [place.across]
    for i, to in enumerate(steps):
        r.pack_stage[...] = pack[...]
        copy = wires.copy(r.pack_stage, r.pack_land.at[i], to)
        copy.start()
        if i < 3 or i == len(steps) - 1:
            tick()
        copy.wait()
        pack[...] += r.pack_land[i]
    tail_copy = wires.copy(pack.at[pl.ds(dp, 16)], r.pack_tail, place.sibling)
    tail_copy.start()
    tick()
    tail_copy.wait()

    @pl.when(home)
    def _():
        for copy, local in frame_copies:
            copy.wait_send()
            local.wait()

    @pl.when(away)
    def _():
        for copy, _ in frame_copies:
            copy.wait_recv()

    for item in parts:
        item.finish()


def levels_of(dp):
    levels = 1
    while 2**levels < dp:
        levels += 1
    return levels


def backward(dp, valid, ins):
    rows, width = ins["query"].shape
    wide = ins["normed_t"].shape[0]
    hidden = ins["up"].shape[1]
    levels = levels_of(dp)
    extra = levels - RS
    part = (2 * wide * hidden // (2 * RS * wide), wide)
    half = (part[0] // 2, wide)
    outs = dict(
        output=((rows, wide), BF16),
        grad_frames=((rows, wide), BF16),
        down_sum=((RS,) + part, BF16),
        up_sum=((RS,) + part, BF16),
        late_sum=((RS,) + part, BF16),
        pack=((dp + 16, wide), F32),
        pack_tail=((16, wide), F32),
    )
    wires = 15 * (2 * RS + 2 + RS + extra) + 3 + 3 + 1 + 3 + 3 + 3 + levels + 1 + 1
    square = (rows, wide)
    scratch = dict(
        up_vmem=pltpu.VMEM((wide, hidden), BF16),
        down_vmem=pltpu.VMEM((hidden, wide), BF16),
        hidden=pltpu.VMEM(square, F32),
        normed2=pltpu.VMEM(square, BF16),
        active=pltpu.VMEM((rows, hidden), BF16),
        grad_pre=pltpu.VMEM((rows, hidden), BF16),
        grad_attn=pltpu.VMEM(square, BF16),
        grad_mixed=pltpu.VMEM((rows, width), BF16),
        inner=pltpu.VMEM((8, rows), F32),
        norm_stage=pltpu.VMEM(square, F32),
        norm_land=pltpu.VMEM(square, F32),
        stage=pltpu.VMEM(square, BF16),
        feed_land=pltpu.VMEM(square, BF16),
        share_land=pltpu.VMEM(square, BF16),
        kv_land=pltpu.VMEM(square, BF16),
        total=pltpu.VMEM(part, F32),
        kept=pltpu.VMEM((9,) + half, F32),
        land=pltpu.VMEM((9,) + part, BF16),
        part_stage=pltpu.VMEM((6,) + half, BF16),
        bias_row=pltpu.VMEM((1, 2 * width), F32),
        pack_stage=pltpu.VMEM((dp + 16, wide), F32),
        pack_land=pltpu.VMEM((levels + 1, dp + 16, wide), F32),
        send_sems=pltpu.SemaphoreType.DMA((wires,)),
        recv_sems=pltpu.SemaphoreType.DMA((wires,)),
        part_sems=pltpu.SemaphoreType.DMA((15,)),
        local_sems=pltpu.SemaphoreType.DMA((6,)),
    )
    if extra:
        scratch.update(more_land=pltpu.VMEM((9, extra, part[0] // 8, wide), BF16))
    cost = pl.CostEstimate(flops=2 * 10**10, bytes_accessed=10**8, transcendentals=10**7)
    kernel = functools.partial(backward_kernel, dp, valid)
    hbm = ("up", "down", "output", "grad_frames", "down_sum", "up_sum", "late_sum")
    return call(kernel, "backward", 1, ins, outs, scratch, hbm, cost)


def forward(dp, valid, ins):
    rows, wide = ins["frames"].shape
    width = ins["qkv_local"].shape[2]
    hidden = ins["up_local"].shape[1]
    outs = dict(
        own=((rows, wide), BF16),
        grad_rows=((rows, wide), BF16),
        info=((8, wide), F32),
        bias=((8, wide), F32),
        normed_t=((wide, rows), BF16),
        query=((rows, width), BF16),
        key=((2 * rows, width), BF16),
        value=((2 * rows, width), BF16),
        lse=((width // HEAD, rows), F32),
        mixed=((rows, wide), BF16),
        mixed_rest=((rows, width), BF16),
        qkv_pairs=((width // 128, wide, 384), BF16),
        up=((wide, hidden), BF16),
        down=((hidden, wide), BF16),
        out=((wide, wide), BF16),
    )
    wires = 4 * RS * (1 + RS) + 3 + 6 + 1 + 1 + 3
    scratch = dict(
        other=pltpu.VMEM((rows, wide), BF16),
        normed=pltpu.VMEM((2 * rows, wide), BF16),
        qkv=pltpu.VMEM((3, wide, width), BF16),
        masked=pltpu.VMEM((2, 2 * rows, 128), BF16),
        send_sems=pltpu.SemaphoreType.DMA((wires,)),
        recv_sems=pltpu.SemaphoreType.DMA((wires,)),
        local_sems=pltpu.SemaphoreType.DMA((6,)),
    )
    hbm = (
        "qkv_local",
        "grad_local",
        "up_local",
        "down_local",
        "out_local",
    )
    cost = pl.CostEstimate(flops=10**10, bytes_accessed=10**7, transcendentals=10**7)
    kernel = functools.partial(forward_kernel, dp, valid)
    return call(kernel, "forward", 2, ins, outs, scratch, hbm, cost)


def finish_kernel(valid, r):
    wide = r.down.shape[1]
    half = wide // 2
    for p in range(RS):
        r.down[p * 512 : (p + 1) * 512, :] = r.down_sum[p].astype(F32)
        chunk = r.up.shape[0] // RS
        at = pl.ds(p * chunk, chunk)
        for i in range(r.up.shape[1] // wide):
            r.up[at, i * wide : (i + 1) * wide] = r.up_sum[p, i * chunk : (i + 1) * chunk, :].astype(
                F32
            )
        for j in range(3):
            for i in range(2):
                columns = pl.ds(i * half + j * 128, 128)
                r.qkv[j, i * half : (i + 1) * half, p * 128 : (p + 1) * 128] = r.late_sum[
                    p, :half, columns
                ].astype(F32)
        r.out[p * 128 : (p + 1) * 128, :] = r.late_sum[p, half:, :].astype(F32)
    r.output[...] = r.output_rows[:valid, :]
    r.grad_frames[...] = r.grad_rows[:valid, :]


def finish(valid, ins, width):
    wide = ins["output_rows"].shape[1]
    hidden = ins["down_sum"].shape[1] * RS
    outs = dict(
        output=((valid, wide), BF16),
        grad_frames=((valid, wide), BF16),
        down=((hidden, wide), F32),
        up=((wide, hidden), F32),
        qkv=((3, wide, width), F32),
        out=((width, wide), F32),
    )
    return call(functools.partial(finish_kernel, valid), "finish", None, ins, outs, {}, (), None)


def on_device(
    sizes,
    frames,
    languages,
    present,
    lang_table,
    norm1_gain,
    norm1_shift,
    qkv_weight,
    qkv_bias,
    out_weight,
    out_bias,
    norm2_gain,
    norm2_shift,
    up_weight,
    up_bias,
    down_weight,
    down_bias,
    grad_out,
):
    d, t, s = (lax.axis_index(name) for name in AXES)
    home = d % 2 == t
    clips = sizes["dp"]
    _, valid, width = frames.shape
    rows = -(-valid // 256) * 256
    head_width = qkv_weight.shape[2]
    langs = lang_table.shape[0]
    pad = ((0, rows - valid), (0, 0))

    one_hot = (languages[:, None] == lax.broadcasted_iota(jnp.int32, (1, langs), 1)).astype(F32)
    embedding = jnp.dot(one_hot, lang_table.astype(F32), precision=lax.Precision.HIGHEST)
    lane = lax.broadcasted_iota(jnp.int32, (1, width), 1)
    once = jnp.where(s == 0, languages[:, None].astype(F32), 0.0)
    info = jnp.concatenate(
        [
            embedding,
            jnp.broadcast_to(present[:, None].astype(F32), (1, width)),
            jnp.where(lane == d, once, 0.0),
            jnp.zeros((5, width), F32),
        ]
    )
    biases = jnp.concatenate([qkv_bias.reshape(1, width), up_bias.reshape(-1, width)]).astype(F32)
    gain_one, shift_one = norm1_gain.astype(F32)[None], norm1_shift.astype(F32)[None]
    f = forward(
        clips,
        valid,
        dict(
            frames=jnp.pad(frames[0], pad),
            grad_local=jnp.pad(grad_out[0], pad),
            info_local=info,
            bias_local=jnp.pad(biases, ((0, 8 - biases.shape[0]), (0, 0))),
            gain=gain_one,
            shift=shift_one,
            qkv_local=qkv_weight,
            up_local=up_weight,
            down_local=down_weight,
            out_local=out_weight,
        ),
    )
    vectors = jnp.stack([norm1_gain, norm2_gain, norm2_shift, out_bias, down_bias]).astype(F32)
    b = backward(
        clips,
        valid,
        dict(
            query=f.query,
            key=f.key,
            value=f.value,
            lse=f.lse,
            mixed=f.mixed,
            mixed_rest=f.mixed_rest,
            frames=f.own,
            grad_rows=f.grad_rows,
            normed_t=f.normed_t,
            qkv_pairs=f.qkv_pairs,
            out=f.out,
            up=f.up,
            down=f.down,
            info=f.info,
            bias=f.bias,
            vectors=jnp.pad(vectors, ((0, 3), (0, 0))),
        ),
    )
    v = b.pack[clips:]
    tail = jnp.where(home, v, b.pack_tail)
    o = finish(
        valid,
        dict(
            output_rows=b.output,
            grad_rows=b.grad_frames,
            down_sum=b.down_sum,
            up_sum=b.up_sum,
            late_sum=b.late_sum,
        ),
        head_width,
    )
    ids = v[9, :clips][:, None]
    hot = (ids == lax.broadcasted_iota(jnp.int32, (1, langs), 1).astype(F32)).astype(F32)
    grad_lang_table = lax.dot_general(
        hot, b.pack[:clips], (((0,), (0,)), ((), ())), precision=lax.Precision.HIGHEST
    )
    return (
        o.output[None],
        o.grad_frames[None],
        grad_lang_table,
        v[0],
        v[1],
        o.qkv,
        tail[6].reshape(2, head_width),
        o.out,
        v[2],
        v[3],
        v[4],
        o.up,
        tail[7:9].reshape(-1),
        o.down,
        v[5],
    )


def solution(mesh):
    rows = P("dp", "seq", None)
    columns, one = P(None, "tensor"), P("dp")
    placed = (
        rows,
        one,
        one,
        P(),
        P(),
        P(),
        P(None, None, "tensor"),
        columns,
        P("tensor", None),
        P(),
        P(),
        P(),
        columns,
        P("tensor"),
        P("tensor", None),
        P(),
        rows,
    )
    out = (
        rows,
        rows,
        P(),
        P(),
        P(),
        P(None, None, "tensor"),
        columns,
        P("tensor", None),
        P(),
        P(),
        P(),
        columns,
        P("tensor"),
        P("tensor", None),
        P(),
    )
    return jax.shard_map(
        functools.partial(on_device, dict(mesh.shape)),
        mesh=mesh,
        in_specs=placed,
        out_specs=out,
        check_vma=False,
    )
```

```python
import functools
import types

import jax
import jax.numpy as jnp
from jax import lax
from jax.experimental import pallas as pl
from jax.experimental.pallas import tpu as pltpu
from jax.sharding import PartitionSpec as P

HEAD = 64
EPSILON = 1e-05
QUERY_SCALE = 0.125
AXES = ("dp", "tensor", "seq")
F32 = jnp.float32
BF16 = jnp.bfloat16
NN = (((1,), (0,)), ((), ()))
NT = (((1,), (1,)), ((), ()))
TN = (((0,), (0,)), ((), ()))
VMEM = pl.BlockSpec(memory_space=pltpu.VMEM)
ANY = pl.BlockSpec(memory_space=pl.ANY)
RS = 3


ORDERS = (
    (0, 2, 1),
    (0, 1, 2),
    (2, 1, 0),
    (1, 2, 0),
    (2, 1, 0),
    (1, 2, 0),
    (1, 2, 0),
    (1, 2, 0),
    (1, 2, 0),
    (1, 2, 0),
    (2, 1, 0),
    (2, 1, 0),
    (1, 2, 0),
    (0, 2, 1),
    (0, 2, 1),
)
SCHEDULE = (
    (),
    (),
    (),
    (),
    (),
    (0, 2, 3),
    (1,),
    (),
    (4, 5),
    (2, 0, 3),
    (1,),
    (),
    (5,),
    (1, 4, 0, 2),
    (3, 6, 5, 7, 1),
    (0, 8),
    (2, 6, 7, 0, 3, 1),
    (),
    (8, 5),
    (9, 4),
    (),
    (2, 6, 10, 1, 7),
    (3,),
    (4, 11, 8, 5),
    (7, 6),
    (0, 12, 13, 9, 2, 3, 10, 14, 11, 5, 12, 1, 13, 4, 7, 6, 3),
    (2, 14, 5, 7, 13, 6, 0, 9, 8, 4, 10, 11),
    (12, 14, 8, 7, 6, 4),
    (13, 8, 9, 10, 11, 12, 13, 14, 9, 10, 8),
    (11, 12, 13, 14, 9, 10, 11, 12, 14, 13, 9, 10, 12, 11, 14),
)


def dg(left, right, dims):
    return lax.dot_general(left, right, dims, preferred_element_type=F32)


def rows_at(start, size):
    return pl.ds(pl.multiple_of(start, 16), size)


class Place:
    def __init__(self, dp):
        self.d, self.t, self.s = (lax.axis_index(name) for name in AXES)
        self.core = lax.rem(self.d, 2)
        self.home = self.core == self.t
        self.away = jnp.logical_not(self.home)
        self.clip = self.d - self.core + self.t
        self.sibling = (self.d + 1 - 2 * self.core, self.t, self.s)
        self.across = (self.d, 1 - self.t, self.s)
        self.level = [((self.d, self.t, 1 - self.s), self.s)]
        bit = 2
        while bit < dp:
            value = lax.rem(self.d // bit, 2)
            self.level.append(((self.d + bit - 2 * bit * value, self.t, self.s), value))
            bit *= 2
        self.peers = [self.sibling, self.across] + [to for to, _ in self.level]

    def enter(self):
        barrier = pltpu.get_barrier_semaphore()
        for to in self.peers:
            pl.semaphore_signal(barrier, inc=1, device_id=to, device_id_type=pl.DeviceIdType.MESH)
        pl.semaphore_wait(barrier, len(self.peers))

    def order(self, numbers):
        levels = [self.level[i] for i in numbers]
        return [to for to, _ in levels], [bit for _, bit in levels]


class Wires:
    def __init__(self, send_sems, recv_sems):
        self.send_sems, self.recv_sems, self.used = send_sems, recv_sems, 0

    def copy(self, src, dst, to):
        i = self.used
        self.used += 1
        return pltpu.make_async_remote_copy(
            src_ref=src,
            dst_ref=dst,
            send_sem=self.send_sems.at[i],
            recv_sem=self.recv_sems.at[i],
            device_id=to,
            device_id_type=pl.DeviceIdType.MESH,
        )


class Fetch:
    def __init__(self, place, wires, part, local, result):
        self.to, self.bits = place.order([(part + j) % RS for j in range(RS)])
        self.place, self.wires, self.result = place, wires, result
        self.slice = local.shape[0] // 2**RS
        self.at = self.slice * (4 * self.bits[0] + 2 * self.bits[1] + self.bits[2])
        at = rows_at(self.at, self.slice)
        self.crossing = wires.copy(local.at[at], result.at[at], place.across)

        @pl.when(place.home)
        def _():
            self.crossing.start()

    def widen(self, j):
        size = self.slice * 2 ** (RS - 1 - j)
        ref = self.result.at[rows_at(self.at, size)]
        self.at = self.at - self.bits[j] * size
        return self.wires.copy(ref, ref, self.to[j])

    def arrive(self):
        self.moving = self.widen(RS - 1)

        @pl.when(self.place.home)
        def _():
            self.crossing.wait_send()

        @pl.when(self.place.away)
        def _():
            self.crossing.wait_recv()
            self.moving.start()

    def double(self, j):
        before = self.moving
        if j:
            self.moving = self.widen(j - 1)

        @pl.when(self.place.away)
        def _():
            before.wait()
            if j:
                self.moving.start()


class Reduction:
    def __init__(self, place, wires, order, kept, land, more, stage, result, sem):
        self.to, self.bits = place.order(order)
        self.place, self.wires, self.stage, self.result = place, wires, stage, result
        self.kept, self.land_ref = kept, land
        self.extra = list(zip(place.level[RS:], more))
        self.local = lambda src, dst: pltpu.make_async_copy(src, dst, sem)
        self.steps = [
            functools.partial(self.halve, 0),
            functools.partial(self.halve, 1),
            self.cross,
            self.land,
            functools.partial(self.double, 2),
            functools.partial(self.double, 1),
            functools.partial(self.double, 0),
        ]
        self.slice = result.shape[0] // 2**RS
        self.low = 0
        self.at = self.bits[0] * 4 * self.slice
        self.forwards = []
        sizes = [4, 2, 1, 1]
        starts = [sum(sizes[:i]) for i in range(4)]
        self.lands = [
            self.land_ref.at[pl.ds(start * self.slice, size * self.slice)]
            for start, size in zip(starts, sizes)
        ]
        self.last = stage.at[pl.ds(3 * self.slice, self.slice)]

    def start(self, total):
        half = 4 * self.slice
        bit = self.bits[0]
        self.stage[...] = total[rows_at((1 - bit) * half, half), :].astype(BF16)
        self.moving = self.wires.copy(self.stage, self.lands[0], self.to[0])
        self.moving.start()
        self.kept[...] = total[rows_at(bit * half, half), :]

    def halve(self, j):
        self.moving.wait()
        half = self.slice * 2 ** (RS - 2 - j)
        bit = self.bits[j + 1]
        away, home = (1 - bit) * half, bit * half
        stage = self.stage.at[pl.ds(0 if j == 0 else 2 * self.slice, half)]
        stage[...] = (
            self.kept[rows_at(self.low + away, half), :]
            + self.lands[j][rows_at(away, half), :].astype(F32)
        ).astype(BF16)
        self.moving = self.wires.copy(stage, self.lands[j + 1], self.to[j + 1])
        self.moving.start()
        self.kept[rows_at(self.low + home, half), :] += self.lands[j][
            rows_at(home, half), :
        ].astype(F32)
        self.low = self.low + home
        self.at = self.at + home

    def cross(self):
        self.moving.wait()
        now = rows_at(self.low, self.slice)
        self.kept[now, :] += self.lands[RS - 1][...].astype(F32)
        for (to, _), land in self.extra:
            self.last[...] = self.kept[now, :].astype(BF16)
            copy = self.wires.copy(self.last, land, to)
            copy.start()
            copy.wait()
            self.kept[now, :] = self.last[...].astype(F32) + land[...].astype(F32)
        self.crossing = self.wires.copy(self.last, self.lands[RS], self.place.across)

        @pl.when(self.place.away)
        def _():
            self.last[...] = self.kept[now, :].astype(BF16)
            self.crossing.start()

    def spread(self, src, start, size):
        ref = self.result.at[rows_at(start, size)]
        forward = self.wires.copy(ref if src is None else src, ref, self.place.sibling)
        self.forwards.append(forward)
        return forward

    def widen(self, src, j):
        ref = self.result.at[rows_at(self.at, self.slice * 2 ** (RS - 1 - j))]
        return self.wires.copy(ref if src is None else src, ref, self.to[j])

    def land(self):
        first = self.spread(self.last, self.at, self.slice)
        self.moving = self.widen(self.last, RS - 1)
        self.writing = self.local(self.last, self.result.at[rows_at(self.at, self.slice)])

        @pl.when(self.place.home)
        def _():
            self.crossing.wait_recv()
            self.last[...] = (
                self.kept[rows_at(self.low, self.slice), :] + self.lands[RS][...].astype(F32)
            ).astype(BF16)
            self.moving.start()
            first.start()
            self.writing.start()

        @pl.when(self.place.away)
        def _():
            self.crossing.wait_send()

    def double(self, j):
        size = self.slice * 2 ** (RS - 1 - j)
        bit = self.bits[j]
        came = self.at + (1 - 2 * bit) * size
        self.at = self.at - bit * size
        before, forward = self.moving, self.spread(None, came, size)
        if j:
            self.moving = self.widen(None, j - 1)

        @pl.when(self.place.home)
        def _():
            before.wait()
            if j == RS - 1:
                self.writing.wait()
            if j:
                self.moving.start()
            forward.start()

    def finish(self):
        @pl.when(self.place.home)
        def _():
            for forward in self.forwards:
                forward.wait_send()

        @pl.when(self.place.away)
        def _():
            for forward in self.forwards:
                forward.wait_recv()


def pair_lanes(rows):
    return lax.broadcasted_iota(jnp.int32, (rows, 128), 1)


def one_head(pair, e, extra=None):
    lane = pair_lanes(pair.shape[0])
    own = (lane < HEAD) if e == 0 else (lane >= HEAD)
    kept = jnp.where(own, pair, jnp.zeros_like(pair))
    if extra is not None:
        kept = jnp.where(lane == (HEAD if e == 0 else 0), extra, kept)
    return kept


def masked(r, e, part):
    return r.grad_pre.at[:, pl.ds((2 * e + part) * 128, 128)]


def mask_keys(r, columns, valid):
    rows = r.query.shape[0]
    row = lax.broadcasted_iota(jnp.int32, (rows, 128), 0)
    bias = jnp.where(row >= valid, -1e30, 0.0).astype(BF16)
    for e in range(2):
        for part in range(2):
            masked(r, e, part)[...] = one_head(r.key[pl.ds(part * rows, rows), columns], e, bias)


def centre(inputs):
    centred = inputs - jnp.mean(inputs, axis=1, keepdims=True)
    scale = lax.rsqrt(jnp.mean(centred * centred, axis=1, keepdims=True) + EPSILON)
    return centred * scale, scale


def call(kernel, name, collective, ins, outs, scratch, hbm, cost):
    names = list(ins) + list(outs) + list(scratch)

    def body(*refs):
        named = dict(zip(names, refs))
        plain = {name: ref for name, ref in named.items() if isinstance(name, str)}
        kernel(types.SimpleNamespace(table=named, **plain))

    results = pl.pallas_call(
        body,
        out_shape=[jax.ShapeDtypeStruct(*item) for item in outs.values()],
        in_specs=[ANY if item in hbm else VMEM for item in ins],
        out_specs=[ANY if item in hbm else VMEM for item in outs],
        scratch_shapes=list(scratch.values()),
        compiler_params=pltpu.CompilerParams(
            collective_id=collective,
            has_side_effects=collective is not None,
            vmem_limit_bytes=60 * 2**20,
        ),
        cost_estimate=cost,
        name=name,
    )(*ins.values())
    return types.SimpleNamespace(**dict(zip(outs, results)))


def attention_forward(place, wires, valid, r):
    rows, width = r.query.shape
    home, away = place.home, place.away
    chunk = rows // 3
    chunks = [pl.ds(c * chunk, chunk) for c in range(3)]
    gain, shift = r.vectors[0:1, :], r.vectors[5:6, :]

    def weight(j):
        return r.active.at[:, pl.ds(j * width, width)]

    first = [Fetch(place, wires, j, r.qkv_local.at[j], weight(j)) for j in range(3)]
    info = wires.copy(r.info_local, r.info, place.sibling)
    bias = wires.copy(r.bias_local, r.bias, place.across)
    own = wires.copy(r.frames_local, r.frames, place.sibling)
    beside, onward = [], []
    for at in chunks:
        to = r.share_land.at[at]
        beside.append(wires.copy(r.frames_local.at[at], to, place.level[0][0]))
        onward.append(wires.copy(to, to, place.sibling))
    grads = wires.copy(r.grad_local, r.grad_rows, place.sibling)
    own_out = r.out.at[rows_at(place.core * width, width)]
    other_out = r.out.at[rows_at((1 - place.core) * width, width)]
    pairs_of = [(r.frames_local, r.frames)] + [(r.qkv_local.at[j], weight(j)) for j in range(3)]
    pairs_of += [(r.grad_local, r.grad_rows), (r.out_local, own_out)]
    pairs_of += [(r.up_local, r.up), (r.down_local, r.down)]
    keep = [
        pltpu.make_async_copy(src, dst, r.local_sems.at[i]) for i, (src, dst) in enumerate(pairs_of)
    ]
    lend = pltpu.make_async_copy(r.out_local, other_out, r.local_sems.at[len(keep)])
    lent = wires.copy(own_out, own_out, place.sibling)

    @pl.when(home)
    def _():
        own.start()
        for copy in beside:
            copy.start()
        info.start()
        bias.start()
        for copy in keep:
            copy.start()
        r.info[...] = r.info_local[...]
        r.bias[...] = r.bias_local[...]

    @pl.when(away)
    def _():
        lend.start()

    def fetch(local, result):
        size = local.shape[0] // RS
        cuts = [pl.ds(part * size, size) for part in range(RS)]
        return [Fetch(place, wires, p, local.at[at], result.at[at]) for p, at in enumerate(cuts)]

    later = fetch(r.out_local, own_out) + fetch(r.up_local, r.up) + fetch(r.down_local, r.down)

    @pl.when(home)
    def _():
        grads.start()

    for item in first:
        item.arrive()

    @pl.when(home)
    def _():
        keep[0].wait()

    @pl.when(away)
    def _():
        info.wait_recv()
        own.wait_recv()
        bias.wait_recv()

    embedding = r.info[0:1, :]

    def norm(source, at, to):
        normal, _ = centre(source[at, :].astype(F32) + embedding)
        normed = normal * gain + shift
        to[at, :] = normed.astype(BF16)
        return normed

    for c, at in enumerate(chunks):
        r.normed_t[:, at] = norm(r.frames, at, r.normed2).T.astype(BF16)
        if c == 1:
            for item in first:
                item.double(2)

        @pl.when(home)
        def _():
            beside[c].wait()
            onward[c].start()

    for item in first:
        item.double(1)
    for c, at in enumerate(chunks):

        @pl.when(away)
        def _():
            onward[c].wait_recv()

        norm(r.share_land, at, r.stage)
    for item in first:
        item.double(0)
    for item in later:
        item.arrive()

    @pl.when(home)
    def _():
        for copy in keep[1:4]:
            copy.wait()

    r.query[...] = (
        (dg(r.normed2[...], weight(0)[...], NN) + r.bias[0:1, :width]) * QUERY_SCALE
    ).astype(BF16)
    for part, normed in enumerate((r.normed2, r.stage)):
        at = pl.ds(part * rows, rows)
        r.key[at, :] = dg(normed[...], weight(1)[...], NN).astype(BF16)
        r.value[at, :] = (dg(normed[...], weight(2)[...], NN) + r.bias[0:1, width:]).astype(BF16)
    for item in later:
        item.double(2)

    block = 256
    mixed_copies = []

    def one_pair(p):
        columns = pl.ds(p * 128, 128)
        whole = pl.ds(pl.multiple_of(place.core * width + p * 128, 128), 128)
        mask_keys(r, columns, valid)
        for j in range(3):
            r.qkv_pairs[p, :, j * 128 : (j + 1) * 128] = weight(j)[:, columns]

        def one_block(i, _):
            at = pl.ds(pl.multiple_of(i * block, block), block)
            parts, rests = [], []
            for e in range(2):
                queries = one_head(r.query[at, columns], e, jnp.ones((), BF16))
                scores = [dg(queries, masked(r, e, part)[...], NT) for part in range(2)]
                top = jnp.maximum(*(jnp.max(half, axis=1, keepdims=True) for half in scores))
                weights = [jnp.exp(half - top) for half in scores]
                total = sum(jnp.sum(half, axis=1, keepdims=True) for half in weights)
                scale = 1.0 / total
                near = rest = 0.0
                for part in range(2):
                    values = r.value[part * rows : (part + 1) * rows, columns]
                    exact = weights[part] * scale
                    low = exact.astype(BF16)
                    near = near + dg(low, values, NN)
                    rest = rest + dg((exact - low.astype(F32)).astype(BF16), values, NN)
                parts.append(near)
                rests.append(rest)
                r.lse[pl.ds(2 * p + e, 1), at] = (top + jnp.log(total)).reshape(1, block)
            first = pair_lanes(block) < HEAD
            mixed = jnp.where(first, parts[0], parts[1])
            low = mixed.astype(BF16)
            r.mixed[at, whole] = low
            rest = mixed - low.astype(F32) + jnp.where(first, rests[0], rests[1])
            r.mixed_rest[at, columns] = rest.astype(BF16)
            return 0

        lax.fori_loop(0, rows // block, one_block, 0)
        copy = wires.copy(r.mixed.at[:, whole], r.mixed.at[:, whole], place.sibling)
        copy.start()
        mixed_copies.append(copy)

    one_pair(0)
    for item in later:
        item.double(1)
    one_pair(1)
    for item in later:
        item.double(0)

    @pl.when(away)
    def _():
        lent.start()
        lend.wait()
        grads.wait_recv()

    one_pair(2)

    @pl.when(away)
    def _():
        lent.wait_send()

    @pl.when(home)
    def _():
        lent.wait_recv()
        for copy in keep[4:]:
            copy.wait()
        info.wait_send()
        bias.wait_send()
        own.wait_send()
        grads.wait_send()
        for copy in onward:
            copy.wait_send()

    for at in chunks:
        r.grad_rows[at, :] = (r.grad_rows[at, :].astype(F32) * r.info[1:2, :]).astype(BF16)
    for copy in mixed_copies:
        copy.wait()


def gelu_pair(inputs):
    half = 0.5 + 0.5 * lax.erf(inputs * 0.7071067811865476)
    slope = inputs * (jnp.exp(inputs * inputs * -0.5) * 0.3989422804014327)
    return inputs * half, half + slope


def layer_kernel(dp, valid, r):
    place = Place(dp)
    place.enter()
    wires = Wires(r.send_sems, r.recv_sems)
    attention_forward(place, wires, valid, r)
    rows, width = r.query.shape
    wide = r.normed_t.shape[0]
    hidden = r.up.shape[1]
    home, away = place.home, place.away
    chunk = rows // 3
    chunks = [pl.ds(c * chunk, chunk) for c in range(3)]
    embedding, keep = r.info[0:1, :], r.info[1:2, :]
    gain_one, gain_two, shift_two, out_bias, down_bias = (r.vectors[i : i + 1, :] for i in range(5))
    zero = jnp.zeros((1, wide), F32)

    for at in chunks:
        attention = dg(r.mixed[at, :], r.out[...], NN)
        rows_in = r.frames[at, :].astype(F32) + embedding + attention + out_bias
        r.hidden[at, :] = rows_in
        normal, _ = centre(rows_in)
        r.normed2[at, :] = (normal * gain_two + shift_two).astype(BF16)

    block = 512
    up_sums = [jnp.zeros((1, block), F32) for _ in range(hidden // block)]
    for at in chunks:
        for h in range(hidden // block):
            units = pl.ds(h * block, block)
            start = h * block
            bias = r.bias[1 + start // wide : 2 + start // wide, start % wide : start % wide + block]
            if start % wide + block > wide:
                bias = jnp.concatenate(
                    [
                        r.bias[1 + start // wide : 2 + start // wide, start % wide :],
                        r.bias[2 + start // wide : 3 + start // wide, : start % wide + block - wide],
                    ],
                    axis=1,
                )
            active, slope = gelu_pair(dg(r.normed2[at, :], r.up[:, units], NN) + bias)
            r.active[at, units] = active.astype(BF16)
            grad = dg(r.grad_rows[at, :], r.down[units, :], NT)
            low = (grad * slope).astype(BF16)
            r.grad_pre[at, units] = low
            up_sums[h] = up_sums[h] + jnp.sum(low.astype(F32), axis=0, keepdims=True)
    norm_copies, feed_copies = [], []
    for at in chunks:
        r.norm_stage[at, :] = dg(r.grad_pre[at, :], r.up[...], NT)
        copy = wires.copy(r.norm_stage.at[at], r.norm_land.at[at], place.sibling)
        copy.start()
        norm_copies.append(copy)
    for at in chunks:
        r.stage[at, :] = dg(r.active[at, :], r.down[...], NN).astype(BF16)
        copy = wires.copy(r.stage.at[at], r.feed_land.at[at], place.sibling)
        copy.start()
        feed_copies.append(copy)

    parts = []

    def reduction(slot, cut, stage, result):
        number = len(parts)
        views = [ref.at[:, cut] for ref in (r.kept.at[slot], r.land.at[slot])]
        more = [r.more_land.at[slot, i].at[:, cut] for i in range(len(place.level) - RS)]
        item = Reduction(
            place,
            wires,
            ORDERS[number],
            *views,
            more,
            stage.at[:, cut],
            result.at[:, cut],
            r.part_sems.at[number],
        )
        item.start(r.total.at[:, cut])
        parts.append(item)

    groups = iter(SCHEDULE)

    def tick():
        for number in next(groups):
            parts[number].steps.pop(0)()

    every = pl.ds(0, wide)
    for p in range(RS):
        columns = pl.ds(p * block, block)
        r.total[...] = dg(r.active[:, columns], r.grad_rows[...], TN)
        reduction(p, every, r.part_stage.at[p], r.down_sum.at[p])
    for p in range(RS):
        columns = pl.ds(p * chunk, chunk)
        outer = dg(r.normed2[:, columns], r.grad_pre[...], TN)
        r.total[:chunk, :] = outer[:, :wide]
        r.total[chunk:, :] = outer[:, wide:]
        reduction(RS + p, every, r.part_stage.at[RS + p], r.up_sum.at[p])

    grad_gain_two = grad_shift_two = grad_out_bias = grad_down_bias = zero
    for c, at in enumerate(chunks):
        tick()
        norm_copies[c].wait()
        feed_copies[c].wait()
        rows_in = r.hidden[at, :]
        normal, scale = centre(rows_in)
        feed = r.stage[at, :].astype(F32) + r.feed_land[at, :].astype(F32)
        r.stage[at, :] = (keep * (rows_in + feed + down_bias)).astype(BF16)
        grad = r.norm_stage[at, :] + r.norm_land[at, :]
        grad_shift_two = grad_shift_two + jnp.sum(grad, axis=0, keepdims=True)
        grad_gain_two = grad_gain_two + jnp.sum(grad * normal, axis=0, keepdims=True)
        grad = grad * gain_two
        grad = (
            grad
            - jnp.mean(grad, axis=1, keepdims=True)
            - normal * jnp.mean(grad * normal, axis=1, keepdims=True)
        ) * scale
        grad_out = r.grad_rows[at, :].astype(F32)
        grad_down_bias = grad_down_bias + jnp.sum(grad_out, axis=0, keepdims=True)
        grad = grad + grad_out
        grad_out_bias = grad_out_bias + jnp.sum(grad, axis=0, keepdims=True)
        r.hidden[at, :] = grad
        low = grad.astype(BF16)
        r.grad_attn[at, :] = low
        r.grad_mixed[at, :] = dg(low, r.out[rows_at(place.core * width, width), :], NT).astype(BF16)
    out_copy = wires.copy(r.stage, r.output, place.across)
    out_keep = pltpu.make_async_copy(r.stage, r.output, r.local_sems.at[0])

    @pl.when(home)
    def _():
        out_copy.start()
        out_keep.start()

    def operand(i):
        return r.grad_pre.at[:, pl.ds((4 + i) * 128, 128)]

    def kv(ref, p):
        return ref.at[:, pl.ds(p * 256, 256)]

    def whole(p):
        return pl.ds(pl.multiple_of(place.core * width + p * 128, 128), 128)

    def prepare(p):
        columns = pl.ds(p * 128, 128)
        grad = r.grad_mixed[:, columns]
        product = grad.astype(F32) * (
            r.mixed[:, whole(p)].astype(F32) + r.mixed_rest[:, columns].astype(F32)
        )
        query = r.query[:, columns]
        lane = pair_lanes(rows)
        mask_keys(r, columns, valid)
        for e in range(2):
            operand(e)[...] = one_head(query, e, jnp.ones((), BF16))
            operand(2 + e)[...] = one_head(query, e)
            operand(4 + e)[...] = one_head(grad, e)
            own = (lane < HEAD) if e == 0 else (lane >= HEAD)
            r.inner[e : e + 1, :] = jnp.sum(
                jnp.where(own, product, 0.0), axis=1, keepdims=True
            ).reshape(1, rows)

    def back_half(p, part, total):
        columns = pl.ds(p * 128, 128)
        size = 384
        store = kv(r.norm_stage if part == 0 else r.normed2, p)

        def one_block(i, total):
            at = pl.ds(pl.multiple_of(i * size, size), size)
            from_all = pl.ds(pl.multiple_of(part * rows + i * size, size), size)
            grad_keys, grad_values = [], []
            for e in range(2):
                scores = dg(masked(r, e, part)[at, :], operand(e)[...], NT)
                weights = jnp.exp(scores - r.lse[2 * p + e : 2 * p + e + 1, :])
                grad_weights = dg(r.value[from_all, columns], operand(4 + e)[...], NT)
                grad_scores = (weights * (grad_weights - r.inner[e : e + 1, :])).astype(BF16)
                grad_values.append(dg(weights.astype(BF16), operand(4 + e)[...], NN))
                grad_keys.append(dg(grad_scores, operand(2 + e)[...], NN))
                total = total + dg(one_head(r.key[from_all, columns], e), grad_scores, TN)
            store[at, :128] = (grad_keys[0] + grad_keys[1]).astype(store.dtype)
            store[at, 128:] = (grad_values[0] + grad_values[1]).astype(store.dtype)
            return total

        return lax.fori_loop(0, rows // size, one_block, total)

    def send_kv(p):
        copy = wires.copy(kv(r.normed2, p), kv(r.kv_land, p), place.level[0][0])
        copy.start()
        return copy

    def stacked(p):
        return r.active.at[:, pl.ds(p * 384, 384)]

    def end_queries(p, total):
        low = total.T.astype(BF16)
        stacked(p)[:, :128] = (low.astype(F32) * QUERY_SCALE).astype(BF16)

    def after_pair(p, copy):
        copy.wait()
        mine = stacked(p)
        mine[:, 128:] = (kv(r.norm_stage, p)[...] + kv(r.kv_land, p)[...].astype(F32)).astype(BF16)
        grads = mine[...]
        share = dg(grads, r.qkv_pairs[p], NT)
        if p == 0:
            r.norm_land[...] = share
        else:
            r.norm_land[...] += share

    def weigh_pair(p):
        grads = stacked(p)[...]
        outer = dg(r.normed_t[...], grads, NN)
        half = wide // 2
        r.total[:half, :half] = outer[:half, :]
        r.total[:half, half:] = outer[half:, :]
        r.total[half:, :] = dg(r.mixed[:, whole(p)], r.grad_attn[...], TN)
        for q in range(3):
            stage = r.down.at[pl.ds(p * 256, 256)]
            reduction(2 * RS + p, pl.ds(q * 256, 256), stage, r.late_sum.at[p])
        sums = jnp.sum(grads.astype(F32), axis=0, keepdims=True)
        r.bias_row[:, p * 128 : (p + 1) * 128] = sums[:, :128]
        r.bias_row[:, width + p * 128 : width + (p + 1) * 128] = sums[:, 256:]

    none = jnp.zeros((128, rows), F32)
    kv_copies = []
    for p in range(3):
        tick()
        prepare(p)
        tick()
        total = back_half(p, 1, none)
        kv_copies.append(send_kv(p))
        tick()
        total = back_half(p, 0, total)
        end_queries(p, total)
        if p:
            tick()
            after_pair(p - 1, kv_copies[p - 1])
            tick()
            weigh_pair(p - 1)
    tick()
    after_pair(2, kv_copies[2])

    @pl.when(home)
    def _():
        out_copy.wait_send()
        out_keep.wait()

    @pl.when(away)
    def _():
        out_copy.wait_recv()

    share_copies = []
    for at in chunks:
        tick()
        r.stage[at, :] = r.norm_land[at, :].astype(BF16)
        copy = wires.copy(r.stage.at[at], r.share_land.at[at], place.sibling)
        copy.start()
        share_copies.append(copy)
    tick()
    weigh_pair(2)

    grad_gain = grad_shift = grad_stream_sum = zero
    frame_copies = []
    for c, at in enumerate(chunks):
        tick()
        share_copies[c].wait()
        normal, scale = centre(r.frames[at, :].astype(F32) + embedding)
        grad = r.stage[at, :].astype(F32) + r.share_land[at, :].astype(F32)
        grad_shift = grad_shift + jnp.sum(grad, axis=0, keepdims=True)
        grad_gain = grad_gain + jnp.sum(grad * normal, axis=0, keepdims=True)
        grad = grad * gain_one
        grad = (
            grad
            - jnp.mean(grad, axis=1, keepdims=True)
            - normal * jnp.mean(grad * normal, axis=1, keepdims=True)
        ) * scale + r.hidden[at, :]
        grad_stream_sum = grad_stream_sum + jnp.sum(grad, axis=0, keepdims=True)
        r.normed2[at, :] = grad.astype(BF16)
        frame_copy = wires.copy(r.normed2.at[at], r.grad_frames.at[at], place.across)
        frame_keep = pltpu.make_async_copy(
            r.normed2.at[at], r.grad_frames.at[at], r.local_sems.at[1 + c]
        )
        frame_copies.append((frame_copy, frame_keep))

        @pl.when(home)
        def _():
            frame_copy.start()
            frame_keep.start()

    tick()
    pack = r.pack
    row = lax.broadcasted_iota(jnp.int32, (dp, wide), 0)
    pack[:dp, :] = jnp.where(row == place.clip, grad_stream_sum, 0.0)
    up_sum = jnp.concatenate(up_sums, axis=1)
    items = [
        grad_gain,
        grad_shift,
        grad_out_bias,
        grad_gain_two,
        grad_shift_two,
        grad_down_bias,
        r.bias_row[...],
    ]
    items += [up_sum[:, i * wide : (i + 1) * wide] for i in range(hidden // wide)]
    items.append(r.info[2:3, :])
    row = lax.broadcasted_iota(jnp.int32, (16, wide), 0)
    table = jnp.zeros((16, wide), F32)
    for i, item in enumerate(items):
        table = table + jnp.where(row == i, item, 0.0)
    pack[dp:, :] = table
    steps = [to for to, _ in place.level] + [place.across]
    for i, to in enumerate(steps):
        r.pack_stage[...] = pack[...]
        copy = wires.copy(r.pack_stage, r.pack_land.at[i], to)
        copy.start()
        if i < 3 or i == len(steps) - 1:
            tick()
        copy.wait()
        pack[...] += r.pack_land[i]
    tail_copy = wires.copy(pack.at[pl.ds(dp, 16)], r.pack_tail, place.sibling)
    tail_copy.start()
    tick()
    tail_copy.wait()

    @pl.when(home)
    def _():
        for copy, local in frame_copies:
            copy.wait_send()
            local.wait()

    @pl.when(away)
    def _():
        for copy, _ in frame_copies:
            copy.wait_recv()

    for item in parts:
        item.finish()


def levels_of(dp):
    levels = 1
    while 2**levels < dp:
        levels += 1
    return levels


def layer(dp, valid, ins):
    rows, wide = ins["frames_local"].shape
    width = ins["qkv_local"].shape[2]
    hidden = ins["up_local"].shape[1]
    levels = levels_of(dp)
    extra = levels - RS
    part = (2 * wide * hidden // (2 * RS * wide), wide)
    half = (part[0] // 2, wide)
    outs = dict(
        output=((rows, wide), BF16),
        grad_frames=((rows, wide), BF16),
        down_sum=((RS,) + part, BF16),
        up_sum=((RS,) + part, BF16),
        late_sum=((RS,) + part, BF16),
        pack=((dp + 16, wide), F32),
        pack_tail=((16, wide), F32),
    )
    wires = 4 * RS * (1 + RS) + 3 + 6 + 1 + 1 + 3
    wires += 15 * (2 * RS + 2 + RS + extra) + 3 + 3 + 1 + 3 + 3 + 3 + levels + 1 + 1
    square = (rows, wide)
    scratch = dict(
        frames=pltpu.VMEM(square, BF16),
        grad_rows=pltpu.VMEM(square, BF16),
        info=pltpu.VMEM((8, wide), F32),
        bias=pltpu.VMEM((8, wide), F32),
        normed_t=pltpu.VMEM((wide, rows), BF16),
        query=pltpu.VMEM((rows, width), BF16),
        key=pltpu.VMEM((2 * rows, width), BF16),
        value=pltpu.VMEM((2 * rows, width), BF16),
        lse=pltpu.VMEM((8, rows), F32),
        mixed=pltpu.VMEM(square, BF16),
        mixed_rest=pltpu.VMEM((rows, width), BF16),
        qkv_pairs=pltpu.VMEM((width // 128, wide, 384), BF16),
        out=pltpu.VMEM((wide, wide), BF16),
        up=pltpu.VMEM((wide, hidden), BF16),
        down=pltpu.VMEM((hidden, wide), BF16),
        hidden=pltpu.VMEM(square, F32),
        normed2=pltpu.VMEM(square, BF16),
        active=pltpu.VMEM((rows, hidden), BF16),
        grad_pre=pltpu.VMEM((rows, hidden), BF16),
        grad_attn=pltpu.VMEM(square, BF16),
        grad_mixed=pltpu.VMEM((rows, width), BF16),
        inner=pltpu.VMEM((8, rows), F32),
        norm_stage=pltpu.VMEM(square, F32),
        norm_land=pltpu.VMEM(square, F32),
        stage=pltpu.VMEM(square, BF16),
        feed_land=pltpu.VMEM(square, BF16),
        share_land=pltpu.VMEM(square, BF16),
        kv_land=pltpu.VMEM(square, BF16),
        total=pltpu.VMEM(part, F32),
        kept=pltpu.VMEM((9,) + half, F32),
        land=pltpu.VMEM((9,) + part, BF16),
        part_stage=pltpu.VMEM((6,) + half, BF16),
        bias_row=pltpu.VMEM((1, 2 * width), F32),
        pack_stage=pltpu.VMEM((dp + 16, wide), F32),
        pack_land=pltpu.VMEM((levels + 1, dp + 16, wide), F32),
        send_sems=pltpu.SemaphoreType.DMA((wires,)),
        recv_sems=pltpu.SemaphoreType.DMA((wires,)),
        part_sems=pltpu.SemaphoreType.DMA((15,)),
        local_sems=pltpu.SemaphoreType.DMA((9,)),
    )
    if extra:
        scratch.update(more_land=pltpu.VMEM((9, extra, part[0] // 8, wide), BF16))
    cost = pl.CostEstimate(flops=3 * 10**10, bytes_accessed=10**8, transcendentals=2 * 10**7)
    kernel = functools.partial(layer_kernel, dp, valid)
    hbm = ("frames_local", "grad_local", "qkv_local", "up_local", "down_local", "out_local")
    hbm += ("output", "grad_frames", "down_sum", "up_sum", "late_sum")
    return call(kernel, "layer", 1, ins, outs, scratch, hbm, cost)


def finish_kernel(down_sum, up_sum, late_sum, rows_a, rows_b, down, up, qkv, out, out_a, out_b):
    wide = down.shape[1]
    half = wide // 2
    chunk = up.shape[0]
    down[...] = down_sum[0].astype(F32)
    for i in range(up.shape[1] // wide):
        up[:, i * wide : (i + 1) * wide] = up_sum[0, i * chunk : (i + 1) * chunk, :].astype(F32)
    for j in range(3):
        for i in range(2):
            columns = pl.ds(i * half + j * 128, 128)
            qkv[j, i * half : (i + 1) * half, :] = late_sum[0, :half, columns].astype(F32)
    out[...] = late_sum[0, half:, :].astype(F32)
    out_a[...] = rows_a[...]
    out_b[...] = rows_b[...]


def finish(valid, width, down_sum, up_sum, late_sum, output, grad_frames):
    rows, wide = output.shape
    hidden = down_sum.shape[1] * RS
    part = pl.BlockSpec((1,) + down_sum.shape[1:], lambda p: (p, 0, 0))
    block = pl.BlockSpec((rows // RS, wide), lambda p: (p, 0))

    def by_rows(height, columns):
        return pl.BlockSpec((height // RS, columns), lambda p: (p, 0))

    return pl.pallas_call(
        finish_kernel,
        grid=(RS,),
        out_shape=[
            jax.ShapeDtypeStruct((hidden, wide), F32),
            jax.ShapeDtypeStruct((wide, hidden), F32),
            jax.ShapeDtypeStruct((3, wide, width), F32),
            jax.ShapeDtypeStruct((width, wide), F32),
            jax.ShapeDtypeStruct((valid, wide), BF16),
            jax.ShapeDtypeStruct((valid, wide), BF16),
        ],
        in_specs=[part] * 3 + [block] * 2,
        out_specs=[
            by_rows(hidden, wide),
            by_rows(wide, hidden),
            pl.BlockSpec((3, wide, width // RS), lambda p: (0, 0, p)),
            by_rows(width, wide),
            block,
            block,
        ],
        compiler_params=pltpu.CompilerParams(vmem_limit_bytes=60 * 2**20),
        name="finish",
    )(down_sum, up_sum, late_sum, output, grad_frames)


def on_device(
    sizes,
    frames,
    languages,
    present,
    lang_table,
    norm1_gain,
    norm1_shift,
    qkv_weight,
    qkv_bias,
    out_weight,
    out_bias,
    norm2_gain,
    norm2_shift,
    up_weight,
    up_bias,
    down_weight,
    down_bias,
    grad_out,
):
    d, t, s = (lax.axis_index(name) for name in AXES)
    home = d % 2 == t
    clips = sizes["dp"]
    _, valid, width = frames.shape
    rows = -(-valid // 256) * 256
    head_width = qkv_weight.shape[2]
    langs = lang_table.shape[0]
    pad = ((0, rows - valid), (0, 0))

    one_hot = (languages[:, None] == lax.broadcasted_iota(jnp.int32, (1, langs), 1)).astype(F32)
    embedding = jnp.dot(one_hot, lang_table.astype(F32), precision=lax.Precision.HIGHEST)
    lane = lax.broadcasted_iota(jnp.int32, (1, width), 1)
    once = jnp.where(s == 0, languages[:, None].astype(F32), 0.0)
    info = jnp.concatenate(
        [
            embedding,
            jnp.broadcast_to(present[:, None].astype(F32), (1, width)),
            jnp.where(lane == d, once, 0.0),
            jnp.zeros((5, width), F32),
        ]
    )
    biases = jnp.concatenate([qkv_bias.reshape(1, width), up_bias.reshape(-1, width)]).astype(F32)
    vectors = jnp.stack(
        [norm1_gain, norm2_gain, norm2_shift, out_bias, down_bias, norm1_shift, out_bias, out_bias]
    )
    b = layer(
        clips,
        valid,
        dict(
            frames_local=jnp.pad(frames[0], pad),
            grad_local=jnp.pad(grad_out[0], pad),
            info_local=info,
            bias_local=jnp.pad(biases, ((0, 8 - biases.shape[0]), (0, 0))),
            vectors=vectors.astype(F32),
            qkv_local=qkv_weight,
            up_local=up_weight,
            down_local=down_weight,
            out_local=out_weight,
        ),
    )
    v = b.pack[clips:]
    tail = jnp.where(home, v, b.pack_tail)
    down, up, qkv, out, output, grad_frames = finish(
        valid, head_width, b.down_sum, b.up_sum, b.late_sum, b.output, b.grad_frames
    )
    ids = v[9, :clips][:, None]
    hot = (ids == lax.broadcasted_iota(jnp.int32, (1, langs), 1).astype(F32)).astype(F32)
    grad_lang_table = lax.dot_general(
        hot, b.pack[:clips], (((0,), (0,)), ((), ())), precision=lax.Precision.HIGHEST
    )
    return (
        output[None],
        grad_frames[None],
        grad_lang_table,
        v[0],
        v[1],
        qkv,
        tail[6].reshape(2, head_width),
        out,
        v[2],
        v[3],
        v[4],
        up,
        tail[7:9].reshape(-1),
        down,
        v[5],
    )


def solution(mesh):
    rows = P("dp", "seq", None)
    columns, one = P(None, "tensor"), P("dp")
    placed = (
        rows,
        one,
        one,
        P(),
        P(),
        P(),
        P(None, None, "tensor"),
        columns,
        P("tensor", None),
        P(),
        P(),
        P(),
        columns,
        P("tensor"),
        P("tensor", None),
        P(),
        rows,
    )
    out = (
        rows,
        rows,
        P(),
        P(),
        P(),
        P(None, None, "tensor"),
        columns,
        P("tensor", None),
        P(),
        P(),
        P(),
        columns,
        P("tensor"),
        P("tensor", None),
        P(),
    )
    return jax.shard_map(
        functools.partial(on_device, dict(mesh.shape)),
        mesh=mesh,
        in_specs=placed,
        out_specs=out,
        check_vma=False,
    )
```

```python
import functools
import types

import jax
import jax.numpy as jnp
from jax import lax
from jax.experimental import pallas as pl
from jax.experimental.pallas import tpu as pltpu
from jax.sharding import PartitionSpec as P

HEAD = 64
EPSILON = 1e-05
QUERY_SCALE = 0.125
AXES = ("dp", "tensor", "seq")
F32 = jnp.float32
BF16 = jnp.bfloat16
NN = (((1,), (0,)), ((), ()))
NT = (((1,), (1,)), ((), ()))
TN = (((0,), (0,)), ((), ()))
VMEM = pl.BlockSpec(memory_space=pltpu.VMEM)
ANY = pl.BlockSpec(memory_space=pl.ANY)
RS = 3


ORDERS = (
    (0, 1, 2),
    (2, 1, 0),
    (2, 1, 0),
    (1, 2, 0),
    (1, 2, 0),
    (1, 2, 0),
    (1, 2, 0),
    (1, 2, 0),
    (1, 2, 0),
    (2, 1, 0),
    (1, 2, 0),
    (2, 1, 0),
    (1, 0, 2),
    (2, 1, 0),
    (1, 2, 0),
)
SCHEDULE = (
    (),
    (),
    (),
    (),
    (),
    (1, 0, 3),
    (),
    (),
    (4, 2, 3),
    (),
    (),
    (5, 4),
    (1,),
    (),
    (),
    (0, 5, 3, 2, 6, 0, 3, 7, 6),
    (8,),
    (4, 0, 7),
    (),
    (1,),
    (8,),
    (),
    (5,),
    (4, 9, 10),
    (1, 2),
    (11,),
    (0, 3, 5, 12, 6, 7, 13, 14, 10, 8, 9, 11, 3, 14, 0, 13, 4, 3, 4, 1, 2, 4),
    (5, 1, 12, 10),
    (9, 6, 11, 5, 7, 14, 8, 10, 9, 11, 14, 1, 0, 12, 13),
    (2, 5, 6, 12, 7, 13, 8, 10, 9, 11, 14),
    (6, 12, 2, 7, 13, 8, 9, 10, 11, 14, 12, 6, 7, 13, 2, 8, 9, 10, 11, 14, 13, 12),
)


def dg(left, right, dims):
    return lax.dot_general(left, right, dims, preferred_element_type=F32)


def rows_at(start, size):
    return pl.ds(pl.multiple_of(start, 16), size)


class Place:
    def __init__(self, dp):
        self.d, self.t, self.s = (lax.axis_index(name) for name in AXES)
        self.core = lax.rem(self.d, 2)
        self.home = self.core == self.t
        self.away = jnp.logical_not(self.home)
        self.clip = self.d - self.core + self.t
        self.sibling = (self.d + 1 - 2 * self.core, self.t, self.s)
        self.across = (self.d, 1 - self.t, self.s)
        self.level = [((self.d, self.t, 1 - self.s), self.s)]
        bit = 2
        while bit < dp:
            value = lax.rem(self.d // bit, 2)
            self.level.append(((self.d + bit - 2 * bit * value, self.t, self.s), value))
            bit *= 2
        self.peers = [self.sibling, self.across] + [to for to, _ in self.level]

    def enter(self):
        barrier = pltpu.get_barrier_semaphore()
        for to in self.peers:
            pl.semaphore_signal(barrier, inc=1, device_id=to, device_id_type=pl.DeviceIdType.MESH)
        pl.semaphore_wait(barrier, len(self.peers))

    def order(self, numbers):
        levels = [self.level[i] for i in numbers]
        return [to for to, _ in levels], [bit for _, bit in levels]


class Wires:
    def __init__(self, send_sems, recv_sems):
        self.send_sems, self.recv_sems, self.used = send_sems, recv_sems, 0

    def copy(self, src, dst, to):
        i = self.used
        self.used += 1
        return pltpu.make_async_remote_copy(
            src_ref=src,
            dst_ref=dst,
            send_sem=self.send_sems.at[i],
            recv_sem=self.recv_sems.at[i],
            device_id=to,
            device_id_type=pl.DeviceIdType.MESH,
        )


class Fetch:
    def __init__(self, place, wires, order, local, result):
        self.to, self.bits = place.order(order)
        self.place, self.wires, self.result = place, wires, result
        self.slice = local.shape[0] // 2**RS
        self.at = self.slice * (4 * self.bits[0] + 2 * self.bits[1] + self.bits[2])
        at = rows_at(self.at, self.slice)
        self.crossing = wires.copy(local.at[at], result.at[at], place.across)

        @pl.when(place.home)
        def _():
            self.crossing.start()

    def widen(self, j):
        size = self.slice * 2 ** (RS - 1 - j)
        ref = self.result.at[rows_at(self.at, size)]
        self.at = self.at - self.bits[j] * size
        return self.wires.copy(ref, ref, self.to[j])

    def arrive(self):
        self.moving = self.widen(RS - 1)

        @pl.when(self.place.home)
        def _():
            self.crossing.wait_send()

        @pl.when(self.place.away)
        def _():
            self.crossing.wait_recv()
            self.moving.start()

    def double(self, j):
        before = self.moving
        if j:
            self.moving = self.widen(j - 1)

        @pl.when(self.place.away)
        def _():
            before.wait()
            if j:
                self.moving.start()


class Reduction:
    def __init__(self, place, wires, order, kept, land, more, stage, result, sem):
        self.to, self.bits = place.order(order)
        self.place, self.wires, self.stage, self.result = place, wires, stage, result
        self.kept, self.land_ref = kept, land
        self.extra = list(zip(place.level[RS:], more))
        self.local = lambda src, dst: pltpu.make_async_copy(src, dst, sem)
        self.steps = [
            functools.partial(self.halve, 0),
            functools.partial(self.halve, 1),
            self.cross,
            self.land,
            functools.partial(self.double, 2),
            functools.partial(self.double, 1),
            functools.partial(self.double, 0),
        ]
        self.slice = result.shape[0] // 2**RS
        self.low = 0
        self.at = self.bits[0] * 4 * self.slice
        self.forwards = []
        sizes = [4, 2, 1, 1]
        starts = [sum(sizes[:i]) for i in range(4)]
        self.lands = [
            self.land_ref.at[pl.ds(start * self.slice, size * self.slice)]
            for start, size in zip(starts, sizes)
        ]
        self.last = stage.at[pl.ds(3 * self.slice, self.slice)]

    def start(self, total):
        half = 4 * self.slice
        bit = self.bits[0]
        self.stage[...] = total[rows_at((1 - bit) * half, half), :].astype(BF16)
        self.moving = self.wires.copy(self.stage, self.lands[0], self.to[0])
        self.moving.start()
        self.kept[...] = total[rows_at(bit * half, half), :]

    def halve(self, j):
        self.moving.wait()
        half = self.slice * 2 ** (RS - 2 - j)
        bit = self.bits[j + 1]
        away, home = (1 - bit) * half, bit * half
        stage = self.stage.at[pl.ds(0 if j == 0 else 2 * self.slice, half)]
        stage[...] = (
            self.kept[rows_at(self.low + away, half), :]
            + self.lands[j][rows_at(away, half), :].astype(F32)
        ).astype(BF16)
        self.moving = self.wires.copy(stage, self.lands[j + 1], self.to[j + 1])
        self.moving.start()
        self.kept[rows_at(self.low + home, half), :] += self.lands[j][
            rows_at(home, half), :
        ].astype(F32)
        self.low = self.low + home
        self.at = self.at + home

    def cross(self):
        self.moving.wait()
        now = rows_at(self.low, self.slice)
        self.kept[now, :] += self.lands[RS - 1][...].astype(F32)
        for (to, _), land in self.extra:
            self.last[...] = self.kept[now, :].astype(BF16)
            copy = self.wires.copy(self.last, land, to)
            copy.start()
            copy.wait()
            self.kept[now, :] = self.last[...].astype(F32) + land[...].astype(F32)
        self.crossing = self.wires.copy(self.last, self.lands[RS], self.place.across)

        @pl.when(self.place.away)
        def _():
            self.last[...] = self.kept[now, :].astype(BF16)
            self.crossing.start()

    def spread(self, src, start, size):
        ref = self.result.at[rows_at(start, size)]
        forward = self.wires.copy(ref if src is None else src, ref, self.place.sibling)
        self.forwards.append(forward)
        return forward

    def widen(self, src, j):
        ref = self.result.at[rows_at(self.at, self.slice * 2 ** (RS - 1 - j))]
        return self.wires.copy(ref if src is None else src, ref, self.to[j])

    def land(self):
        first = self.spread(self.last, self.at, self.slice)
        self.moving = self.widen(self.last, RS - 1)
        self.writing = self.local(self.last, self.result.at[rows_at(self.at, self.slice)])

        @pl.when(self.place.home)
        def _():
            self.crossing.wait_recv()
            self.last[...] = (
                self.kept[rows_at(self.low, self.slice), :] + self.lands[RS][...].astype(F32)
            ).astype(BF16)
            self.moving.start()
            first.start()
            self.writing.start()

        @pl.when(self.place.away)
        def _():
            self.crossing.wait_send()

    def double(self, j):
        size = self.slice * 2 ** (RS - 1 - j)
        bit = self.bits[j]
        came = self.at + (1 - 2 * bit) * size
        self.at = self.at - bit * size
        before, forward = self.moving, self.spread(None, came, size)
        if j:
            self.moving = self.widen(None, j - 1)

        @pl.when(self.place.home)
        def _():
            before.wait()
            if j == RS - 1:
                self.writing.wait()
            if j:
                self.moving.start()
            forward.start()

    def finish(self):
        @pl.when(self.place.home)
        def _():
            for forward in self.forwards:
                forward.wait_send()

        @pl.when(self.place.away)
        def _():
            for forward in self.forwards:
                forward.wait_recv()


def pair_lanes(rows):
    return lax.broadcasted_iota(jnp.int32, (rows, 128), 1)


def one_head(pair, e, extra=None):
    lane = pair_lanes(pair.shape[0])
    own = (lane < HEAD) if e == 0 else (lane >= HEAD)
    kept = jnp.where(own, pair, jnp.zeros_like(pair))
    if extra is not None:
        kept = jnp.where(lane == (HEAD if e == 0 else 0), extra, kept)
    return kept


def masked(r, e, part):
    return r.grad_pre.at[:, pl.ds((2 * e + part) * 128, 128)]


def mask_keys(r, columns, valid):
    rows = r.query.shape[0]
    row = lax.broadcasted_iota(jnp.int32, (rows, 128), 0)
    bias = jnp.where(row >= valid, -1e30, 0.0).astype(BF16)
    for e in range(2):
        for part in range(2):
            masked(r, e, part)[...] = one_head(r.key[pl.ds(part * rows, rows), columns], e, bias)


def centre(inputs):
    centred = inputs - jnp.mean(inputs, axis=1, keepdims=True)
    scale = lax.rsqrt(jnp.mean(centred * centred, axis=1, keepdims=True) + EPSILON)
    return centred * scale, scale


def call(kernel, name, collective, ins, outs, scratch, hbm, cost):
    names = list(ins) + list(outs) + list(scratch)

    def body(*refs):
        named = dict(zip(names, refs))
        plain = {name: ref for name, ref in named.items() if isinstance(name, str)}
        kernel(types.SimpleNamespace(table=named, **plain))

    results = pl.pallas_call(
        body,
        out_shape=[jax.ShapeDtypeStruct(*item) for item in outs.values()],
        in_specs=[ANY if item in hbm else VMEM for item in ins],
        out_specs=[ANY if item in hbm else VMEM for item in outs],
        scratch_shapes=list(scratch.values()),
        compiler_params=pltpu.CompilerParams(
            collective_id=collective,
            has_side_effects=collective is not None,
            vmem_limit_bytes=60 * 2**20,
        ),
        cost_estimate=cost,
        name=name,
    )(*ins.values())
    return types.SimpleNamespace(**dict(zip(outs, results)))


def attention_forward(place, wires, valid, r):
    rows, width = r.query.shape
    home, away = place.home, place.away
    chunk = rows // 3
    chunks = [pl.ds(c * chunk, chunk) for c in range(3)]
    gain, shift = r.vectors[0:1, :], r.vectors[5:6, :]

    def weight(j):
        return r.active.at[:, pl.ds(j * width, width)]

    light = ((1, 2, 0), (2, 1, 0), (1, 2, 0))
    turns = ((0, 1, 2), (1, 2, 0), (2, 0, 1))
    first = [Fetch(place, wires, light[j], r.qkv_local.at[j], weight(j)) for j in range(3)]
    info = wires.copy(r.info_local, r.info, place.sibling)
    bias = wires.copy(r.bias_local, r.bias, place.across)
    own = wires.copy(r.frames_local, r.frames, place.sibling)
    beside, onward = [], []
    for at in chunks:
        to = r.share_land.at[at]
        beside.append(wires.copy(r.frames_local.at[at], to, place.level[0][0]))
        onward.append(wires.copy(to, to, place.sibling))
    grads = wires.copy(r.grad_local, r.grad_rows, place.sibling)
    own_out = r.out.at[rows_at(place.core * width, width)]
    other_out = r.out.at[rows_at((1 - place.core) * width, width)]
    pairs_of = [(r.frames_local, r.frames)] + [(r.qkv_local.at[j], weight(j)) for j in range(3)]
    pairs_of += [(r.grad_local, r.grad_rows), (r.out_local, own_out)]
    pairs_of += [(r.up_local, r.up), (r.down_local, r.down)]
    keep = [
        pltpu.make_async_copy(src, dst, r.local_sems.at[i]) for i, (src, dst) in enumerate(pairs_of)
    ]
    lend = pltpu.make_async_copy(r.out_local, other_out, r.local_sems.at[len(keep)])
    lent = wires.copy(own_out, own_out, place.sibling)

    @pl.when(home)
    def _():
        own.start()
        for copy in beside:
            copy.start()
        info.start()
        bias.start()
        for copy in keep:
            copy.start()
        r.info[...] = r.info_local[...]
        r.bias[...] = r.bias_local[...]

    @pl.when(away)
    def _():
        lend.start()

    def fetch(local, result):
        size = local.shape[0] // RS
        cuts = [pl.ds(part * size, size) for part in range(RS)]
        return [
            Fetch(place, wires, turn, local.at[at], result.at[at]) for turn, at in zip(turns, cuts)
        ]

    later = fetch(r.out_local, own_out) + fetch(r.up_local, r.up) + fetch(r.down_local, r.down)

    @pl.when(home)
    def _():
        grads.start()

    for item in first:
        item.arrive()

    @pl.when(home)
    def _():
        keep[0].wait()

    @pl.when(away)
    def _():
        info.wait_recv()
        own.wait_recv()
        bias.wait_recv()

    embedding = r.info[0:1, :]

    def norm(source, at, to):
        normal, _ = centre(source[at, :].astype(F32) + embedding)
        normed = normal * gain + shift
        to[at, :] = normed.astype(BF16)
        return normed

    for c, at in enumerate(chunks):
        r.normed_t[:, at] = norm(r.frames, at, r.normed2).T.astype(BF16)
        if c == 1:
            for item in first:
                item.double(2)

        @pl.when(home)
        def _():
            beside[c].wait()
            onward[c].start()

    for item in first:
        item.double(1)
    for c, at in enumerate(chunks):

        @pl.when(away)
        def _():
            onward[c].wait_recv()

        norm(r.share_land, at, r.stage)
    for item in first:
        item.double(0)
    for item in later:
        item.arrive()

    @pl.when(home)
    def _():
        for copy in keep[1:4]:
            copy.wait()

    r.query[...] = (
        (dg(r.normed2[...], weight(0)[...], NN) + r.bias[0:1, :width]) * QUERY_SCALE
    ).astype(BF16)
    for part, normed in enumerate((r.normed2, r.stage)):
        at = pl.ds(part * rows, rows)
        r.key[at, :] = dg(normed[...], weight(1)[...], NN).astype(BF16)
        r.value[at, :] = (dg(normed[...], weight(2)[...], NN) + r.bias[0:1, width:]).astype(BF16)
    for item in later:
        item.double(2)

    block = 256
    mixed_copies = []

    def one_pair(p):
        columns = pl.ds(p * 128, 128)
        whole = pl.ds(pl.multiple_of(place.core * width + p * 128, 128), 128)
        mask_keys(r, columns, valid)
        for j in range(3):
            r.qkv_pairs[p, :, j * 128 : (j + 1) * 128] = weight(j)[:, columns]

        def one_block(i, _):
            at = pl.ds(pl.multiple_of(i * block, block), block)
            parts, rests = [], []
            for e in range(2):
                queries = one_head(r.query[at, columns], e, jnp.ones((), BF16))
                scores = [dg(queries, masked(r, e, part)[...], NT) for part in range(2)]
                top = jnp.maximum(*(jnp.max(half, axis=1, keepdims=True) for half in scores))
                weights = [jnp.exp(half - top) for half in scores]
                total = sum(jnp.sum(half, axis=1, keepdims=True) for half in weights)
                scale = 1.0 / total
                near = rest = 0.0
                for part in range(2):
                    values = r.value[part * rows : (part + 1) * rows, columns]
                    exact = weights[part] * scale
                    low = exact.astype(BF16)
                    near = near + dg(low, values, NN)
                    rest = rest + dg((exact - low.astype(F32)).astype(BF16), values, NN)
                parts.append(near)
                rests.append(rest)
                r.lse[pl.ds(2 * p + e, 1), at] = (top + jnp.log(total)).reshape(1, block)
            first = pair_lanes(block) < HEAD
            mixed = jnp.where(first, parts[0], parts[1])
            low = mixed.astype(BF16)
            r.mixed[at, whole] = low
            rest = mixed - low.astype(F32) + jnp.where(first, rests[0], rests[1])
            r.mixed_rest[at, columns] = rest.astype(BF16)
            return 0

        lax.fori_loop(0, rows // block, one_block, 0)
        copy = wires.copy(r.mixed.at[:, whole], r.mixed.at[:, whole], place.sibling)
        copy.start()
        mixed_copies.append(copy)

    one_pair(0)
    for item in later:
        item.double(1)
    one_pair(1)
    for item in later[:RS]:
        item.double(0)

    @pl.when(away)
    def _():
        lent.start()
        lend.wait()
        grads.wait_recv()

    one_pair(2)
    for item in later[RS:]:
        item.double(0)

    @pl.when(away)
    def _():
        lent.wait_send()

    @pl.when(home)
    def _():
        lent.wait_recv()
        for copy in keep[4:]:
            copy.wait()
        info.wait_send()
        bias.wait_send()
        own.wait_send()
        grads.wait_send()
        for copy in onward:
            copy.wait_send()

    for at in chunks:
        r.grad_rows[at, :] = (r.grad_rows[at, :].astype(F32) * r.info[1:2, :]).astype(BF16)
    for copy in mixed_copies:
        copy.wait()


def gelu_pair(inputs):
    half = 0.5 + 0.5 * lax.erf(inputs * 0.7071067811865476)
    slope = inputs * (jnp.exp(inputs * inputs * -0.5) * 0.3989422804014327)
    return inputs * half, half + slope


def layer_kernel(dp, valid, r):
    place = Place(dp)
    place.enter()
    wires = Wires(r.send_sems, r.recv_sems)
    attention_forward(place, wires, valid, r)
    rows, width = r.query.shape
    wide = r.normed_t.shape[0]
    hidden = r.up.shape[1]
    home, away = place.home, place.away
    chunk = rows // 3
    chunks = [pl.ds(c * chunk, chunk) for c in range(3)]
    embedding, keep = r.info[0:1, :], r.info[1:2, :]
    gain_one, gain_two, shift_two, out_bias, down_bias = (r.vectors[i : i + 1, :] for i in range(5))
    zero = jnp.zeros((1, wide), F32)

    for at in chunks:
        attention = dg(r.mixed[at, :], r.out[...], NN)
        rows_in = r.frames[at, :].astype(F32) + embedding + attention + out_bias
        r.hidden[at, :] = rows_in
        normal, _ = centre(rows_in)
        r.normed2[at, :] = (normal * gain_two + shift_two).astype(BF16)

    block = 512
    up_sums = [jnp.zeros((1, block), F32) for _ in range(hidden // block)]
    for at in chunks:
        for h in range(hidden // block):
            units = pl.ds(h * block, block)
            start = h * block
            bias = r.bias[1 + start // wide : 2 + start // wide, start % wide : start % wide + block]
            if start % wide + block > wide:
                bias = jnp.concatenate(
                    [
                        r.bias[1 + start // wide : 2 + start // wide, start % wide :],
                        r.bias[2 + start // wide : 3 + start // wide, : start % wide + block - wide],
                    ],
                    axis=1,
                )
            active, slope = gelu_pair(dg(r.normed2[at, :], r.up[:, units], NN) + bias)
            r.active[at, units] = active.astype(BF16)
            grad = dg(r.grad_rows[at, :], r.down[units, :], NT)
            low = (grad * slope).astype(BF16)
            r.grad_pre[at, units] = low
            up_sums[h] = up_sums[h] + jnp.sum(low.astype(F32), axis=0, keepdims=True)
    norm_copies, feed_copies = [], []
    for at in chunks:
        r.norm_stage[at, :] = dg(r.grad_pre[at, :], r.up[...], NT)
        copy = wires.copy(r.norm_stage.at[at], r.norm_land.at[at], place.sibling)
        copy.start()
        norm_copies.append(copy)
    for at in chunks:
        r.stage[at, :] = dg(r.active[at, :], r.down[...], NN).astype(BF16)
        copy = wires.copy(r.stage.at[at], r.feed_land.at[at], place.sibling)
        copy.start()
        feed_copies.append(copy)

    parts = []

    def reduction(slot, cut, stage, result):
        number = len(parts)
        views = [ref.at[:, cut] for ref in (r.kept.at[slot], r.land.at[slot])]
        more = [r.more_land.at[slot, i].at[:, cut] for i in range(len(place.level) - RS)]
        item = Reduction(
            place,
            wires,
            ORDERS[number],
            *views,
            more,
            stage.at[:, cut],
            result.at[:, cut],
            r.part_sems.at[number],
        )
        item.start(r.total.at[:, cut])
        parts.append(item)

    groups = iter(SCHEDULE)

    def tick():
        for number in next(groups):
            parts[number].steps.pop(0)()

    every = pl.ds(0, wide)
    for p in range(RS):
        columns = pl.ds(p * block, block)
        r.total[...] = dg(r.active[:, columns], r.grad_rows[...], TN)
        reduction(p, every, r.part_stage.at[p], r.down_sum.at[p])
    for p in range(RS):
        columns = pl.ds(p * chunk, chunk)
        outer = dg(r.normed2[:, columns], r.grad_pre[...], TN)
        r.total[:chunk, :] = outer[:, :wide]
        r.total[chunk:, :] = outer[:, wide:]
        reduction(RS + p, every, r.part_stage.at[RS + p], r.up_sum.at[p])

    grad_gain_two = grad_shift_two = grad_out_bias = grad_down_bias = zero
    for c, at in enumerate(chunks):
        tick()
        norm_copies[c].wait()
        feed_copies[c].wait()
        rows_in = r.hidden[at, :]
        normal, scale = centre(rows_in)
        feed = r.stage[at, :].astype(F32) + r.feed_land[at, :].astype(F32)
        r.stage[at, :] = (keep * (rows_in + feed + down_bias)).astype(BF16)
        grad = r.norm_stage[at, :] + r.norm_land[at, :]
        grad_shift_two = grad_shift_two + jnp.sum(grad, axis=0, keepdims=True)
        grad_gain_two = grad_gain_two + jnp.sum(grad * normal, axis=0, keepdims=True)
        grad = grad * gain_two
        grad = (
            grad
            - jnp.mean(grad, axis=1, keepdims=True)
            - normal * jnp.mean(grad * normal, axis=1, keepdims=True)
        ) * scale
        grad_out = r.grad_rows[at, :].astype(F32)
        grad_down_bias = grad_down_bias + jnp.sum(grad_out, axis=0, keepdims=True)
        grad = grad + grad_out
        grad_out_bias = grad_out_bias + jnp.sum(grad, axis=0, keepdims=True)
        r.hidden[at, :] = grad
        low = grad.astype(BF16)
        r.grad_attn[at, :] = low
        r.grad_mixed[at, :] = dg(low, r.out[rows_at(place.core * width, width), :], NT).astype(BF16)
    out_copy = wires.copy(r.stage, r.output, place.across)
    out_keep = pltpu.make_async_copy(r.stage, r.output, r.local_sems.at[0])

    @pl.when(home)
    def _():
        out_copy.start()
        out_keep.start()

    def operand(i):
        return r.grad_pre.at[:, pl.ds((4 + i) * 128, 128)]

    def kv(ref, p):
        return ref.at[:, pl.ds(p * 256, 256)]

    def whole(p):
        return pl.ds(pl.multiple_of(place.core * width + p * 128, 128), 128)

    def prepare(p):
        columns = pl.ds(p * 128, 128)
        grad = r.grad_mixed[:, columns]
        product = grad.astype(F32) * (
            r.mixed[:, whole(p)].astype(F32) + r.mixed_rest[:, columns].astype(F32)
        )
        query = r.query[:, columns]
        lane = pair_lanes(rows)
        mask_keys(r, columns, valid)
        for e in range(2):
            operand(e)[...] = one_head(query, e, jnp.ones((), BF16))
            operand(2 + e)[...] = one_head(query, e)
            operand(4 + e)[...] = one_head(grad, e)
            own = (lane < HEAD) if e == 0 else (lane >= HEAD)
            r.inner[e : e + 1, :] = jnp.sum(
                jnp.where(own, product, 0.0), axis=1, keepdims=True
            ).reshape(1, rows)

    def back_half(p, part, total):
        columns = pl.ds(p * 128, 128)
        size = 384
        store = kv(r.norm_stage if part == 0 else r.normed2, p)

        def one_block(i, total):
            at = pl.ds(pl.multiple_of(i * size, size), size)
            from_all = pl.ds(pl.multiple_of(part * rows + i * size, size), size)
            grad_keys, grad_values = [], []
            for e in range(2):
                scores = dg(masked(r, e, part)[at, :], operand(e)[...], NT)
                weights = jnp.exp(scores - r.lse[2 * p + e : 2 * p + e + 1, :])
                grad_weights = dg(r.value[from_all, columns], operand(4 + e)[...], NT)
                grad_scores = (weights * (grad_weights - r.inner[e : e + 1, :])).astype(BF16)
                grad_values.append(dg(weights.astype(BF16), operand(4 + e)[...], NN))
                grad_keys.append(dg(grad_scores, operand(2 + e)[...], NN))
                total = total + dg(one_head(r.key[from_all, columns], e), grad_scores, TN)
            store[at, :128] = (grad_keys[0] + grad_keys[1]).astype(store.dtype)
            store[at, 128:] = (grad_values[0] + grad_values[1]).astype(store.dtype)
            return total

        return lax.fori_loop(0, rows // size, one_block, total)

    def send_kv(p):
        copy = wires.copy(kv(r.normed2, p), kv(r.kv_land, p), place.level[0][0])
        copy.start()
        return copy

    def stacked(p):
        return r.active.at[:, pl.ds(p * 384, 384)]

    def end_queries(p, total):
        low = total.T.astype(BF16)
        stacked(p)[:, :128] = (low.astype(F32) * QUERY_SCALE).astype(BF16)

    def after_pair(p, copy):
        copy.wait()
        mine = stacked(p)
        mine[:, 128:] = (kv(r.norm_stage, p)[...] + kv(r.kv_land, p)[...].astype(F32)).astype(BF16)
        grads = mine[...]
        share = dg(grads, r.qkv_pairs[p], NT)
        if p == 0:
            r.norm_land[...] = share
        else:
            r.norm_land[...] += share

    def weigh_pair(p):
        grads = stacked(p)[...]
        outer = dg(r.normed_t[...], grads, NN)
        half = wide // 2
        r.total[:half, :half] = outer[:half, :]
        r.total[:half, half:] = outer[half:, :]
        r.total[half:, :] = dg(r.mixed[:, whole(p)], r.grad_attn[...], TN)
        for q in range(3):
            stage = r.down.at[pl.ds(p * 256, 256)]
            reduction(2 * RS + p, pl.ds(q * 256, 256), stage, r.late_sum.at[p])
        sums = jnp.sum(grads.astype(F32), axis=0, keepdims=True)
        r.bias_row[:, p * 128 : (p + 1) * 128] = sums[:, :128]
        r.bias_row[:, width + p * 128 : width + (p + 1) * 128] = sums[:, 256:]

    none = jnp.zeros((128, rows), F32)
    kv_copies = {}

    def others(p):
        tick()
        prepare(p)
        tick()
        total = back_half(p, 1, none)
        kv_copies[p] = send_kv(p)
        return total

    def owns(p, total):
        tick()
        end_queries(p, back_half(p, 0, total))

    def end_pair(p):
        tick()
        after_pair(p, kv_copies[p])
        tick()
        weigh_pair(p)

    owns(0, others(0))
    held = others(2)
    owns(1, others(1))
    end_pair(0)
    tick()
    prepare(2)
    owns(2, held)
    end_pair(1)
    tick()
    after_pair(2, kv_copies[2])

    @pl.when(home)
    def _():
        out_copy.wait_send()
        out_keep.wait()

    @pl.when(away)
    def _():
        out_copy.wait_recv()

    share_copies = []
    for at in chunks:
        tick()
        r.stage[at, :] = r.norm_land[at, :].astype(BF16)
        copy = wires.copy(r.stage.at[at], r.share_land.at[at], place.sibling)
        copy.start()
        share_copies.append(copy)
    tick()
    weigh_pair(2)

    grad_gain = grad_shift = grad_stream_sum = zero
    frame_copies = []
    for c, at in enumerate(chunks):
        tick()
        share_copies[c].wait()
        normal, scale = centre(r.frames[at, :].astype(F32) + embedding)
        grad = r.stage[at, :].astype(F32) + r.share_land[at, :].astype(F32)
        grad_shift = grad_shift + jnp.sum(grad, axis=0, keepdims=True)
        grad_gain = grad_gain + jnp.sum(grad * normal, axis=0, keepdims=True)
        grad = grad * gain_one
        grad = (
            grad
            - jnp.mean(grad, axis=1, keepdims=True)
            - normal * jnp.mean(grad * normal, axis=1, keepdims=True)
        ) * scale + r.hidden[at, :]
        grad_stream_sum = grad_stream_sum + jnp.sum(grad, axis=0, keepdims=True)
        r.normed2[at, :] = grad.astype(BF16)
        frame_copy = wires.copy(r.normed2.at[at], r.grad_frames.at[at], place.across)
        frame_keep = pltpu.make_async_copy(
            r.normed2.at[at], r.grad_frames.at[at], r.local_sems.at[1 + c]
        )
        frame_copies.append((frame_copy, frame_keep))

        @pl.when(home)
        def _():
            frame_copy.start()
            frame_keep.start()

    tick()
    pack = r.pack
    row = lax.broadcasted_iota(jnp.int32, (dp, wide), 0)
    pack[:dp, :] = jnp.where(row == place.clip, grad_stream_sum, 0.0)
    up_sum = jnp.concatenate(up_sums, axis=1)
    items = [
        grad_gain,
        grad_shift,
        grad_out_bias,
        grad_gain_two,
        grad_shift_two,
        grad_down_bias,
        r.bias_row[...],
    ]
    items += [up_sum[:, i * wide : (i + 1) * wide] for i in range(hidden // wide)]
    items.append(r.info[2:3, :])
    row = lax.broadcasted_iota(jnp.int32, (16, wide), 0)
    table = jnp.zeros((16, wide), F32)
    for i, item in enumerate(items):
        table = table + jnp.where(row == i, item, 0.0)
    pack[dp:, :] = table
    steps = [to for to, _ in place.level] + [place.across]
    for i, to in enumerate(steps):
        r.pack_stage[...] = pack[...]
        copy = wires.copy(r.pack_stage, r.pack_land.at[i], to)
        copy.start()
        if i < 3 or i == len(steps) - 1:
            tick()
        copy.wait()
        pack[...] += r.pack_land[i]
    tail_copy = wires.copy(pack.at[pl.ds(dp, 16)], r.pack_tail, place.sibling)
    tail_copy.start()
    tick()
    tail_copy.wait()

    @pl.when(home)
    def _():
        for copy, local in frame_copies:
            copy.wait_send()
            local.wait()

    @pl.when(away)
    def _():
        for copy, _ in frame_copies:
            copy.wait_recv()

    for item in parts:
        item.finish()


def levels_of(dp):
    levels = 1
    while 2**levels < dp:
        levels += 1
    return levels


def layer(dp, valid, ins):
    rows, wide = ins["frames_local"].shape
    width = ins["qkv_local"].shape[2]
    hidden = ins["up_local"].shape[1]
    levels = levels_of(dp)
    extra = levels - RS
    part = (2 * wide * hidden // (2 * RS * wide), wide)
    half = (part[0] // 2, wide)
    outs = dict(
        output=((rows, wide), BF16),
        grad_frames=((rows, wide), BF16),
        down_sum=((RS,) + part, BF16),
        up_sum=((RS,) + part, BF16),
        late_sum=((RS,) + part, BF16),
        pack=((dp + 16, wide), F32),
        pack_tail=((16, wide), F32),
    )
    wires = 4 * RS * (1 + RS) + 3 + 6 + 1 + 1 + 3
    wires += 15 * (2 * RS + 2 + RS + extra) + 3 + 3 + 1 + 3 + 3 + 3 + levels + 1 + 1
    square = (rows, wide)
    scratch = dict(
        frames=pltpu.VMEM(square, BF16),
        grad_rows=pltpu.VMEM(square, BF16),
        info=pltpu.VMEM((8, wide), F32),
        bias=pltpu.VMEM((8, wide), F32),
        normed_t=pltpu.VMEM((wide, rows), BF16),
        query=pltpu.VMEM((rows, width), BF16),
        key=pltpu.VMEM((2 * rows, width), BF16),
        value=pltpu.VMEM((2 * rows, width), BF16),
        lse=pltpu.VMEM((8, rows), F32),
        mixed=pltpu.VMEM(square, BF16),
        mixed_rest=pltpu.VMEM((rows, width), BF16),
        qkv_pairs=pltpu.VMEM((width // 128, wide, 384), BF16),
        out=pltpu.VMEM((wide, wide), BF16),
        up=pltpu.VMEM((wide, hidden), BF16),
        down=pltpu.VMEM((hidden, wide), BF16),
        hidden=pltpu.VMEM(square, F32),
        normed2=pltpu.VMEM(square, BF16),
        active=pltpu.VMEM((rows, hidden), BF16),
        grad_pre=pltpu.VMEM((rows, hidden), BF16),
        grad_attn=pltpu.VMEM(square, BF16),
        grad_mixed=pltpu.VMEM((rows, width), BF16),
        inner=pltpu.VMEM((8, rows), F32),
        norm_stage=pltpu.VMEM(square, F32),
        norm_land=pltpu.VMEM(square, F32),
        stage=pltpu.VMEM(square, BF16),
        feed_land=pltpu.VMEM(square, BF16),
        share_land=pltpu.VMEM(square, BF16),
        kv_land=pltpu.VMEM(square, BF16),
        total=pltpu.VMEM(part, F32),
        kept=pltpu.VMEM((9,) + half, F32),
        land=pltpu.VMEM((9,) + part, BF16),
        part_stage=pltpu.VMEM((6,) + half, BF16),
        bias_row=pltpu.VMEM((1, 2 * width), F32),
        pack_stage=pltpu.VMEM((dp + 16, wide), F32),
        pack_land=pltpu.VMEM((levels + 1, dp + 16, wide), F32),
        send_sems=pltpu.SemaphoreType.DMA((wires,)),
        recv_sems=pltpu.SemaphoreType.DMA((wires,)),
        part_sems=pltpu.SemaphoreType.DMA((15,)),
        local_sems=pltpu.SemaphoreType.DMA((9,)),
    )
    if extra:
        scratch.update(more_land=pltpu.VMEM((9, extra, part[0] // 8, wide), BF16))
    cost = pl.CostEstimate(flops=3 * 10**10, bytes_accessed=10**8, transcendentals=2 * 10**7)
    kernel = functools.partial(layer_kernel, dp, valid)
    hbm = ("frames_local", "grad_local", "qkv_local", "up_local", "down_local", "out_local")
    hbm += ("output", "grad_frames", "down_sum", "up_sum", "late_sum")
    return call(kernel, "layer", 1, ins, outs, scratch, hbm, cost)


def finish_kernel(down_sum, up_sum, late_sum, rows_a, rows_b, down, up, qkv, out, out_a, out_b):
    wide = down.shape[1]
    half = wide // 2
    chunk = up.shape[0]
    down[...] = down_sum[0].astype(F32)
    for i in range(up.shape[1] // wide):
        up[:, i * wide : (i + 1) * wide] = up_sum[0, i * chunk : (i + 1) * chunk, :].astype(F32)
    for j in range(3):
        for i in range(2):
            columns = pl.ds(i * half + j * 128, 128)
            qkv[j, i * half : (i + 1) * half, :] = late_sum[0, :half, columns].astype(F32)
    out[...] = late_sum[0, half:, :].astype(F32)
    out_a[...] = rows_a[...]
    out_b[...] = rows_b[...]


def finish(valid, width, down_sum, up_sum, late_sum, output, grad_frames):
    rows, wide = output.shape
    hidden = down_sum.shape[1] * RS
    part = pl.BlockSpec((1,) + down_sum.shape[1:], lambda p: (p, 0, 0))
    block = pl.BlockSpec((rows // RS, wide), lambda p: (p, 0))

    def by_rows(height, columns):
        return pl.BlockSpec((height // RS, columns), lambda p: (p, 0))

    return pl.pallas_call(
        finish_kernel,
        grid=(RS,),
        out_shape=[
            jax.ShapeDtypeStruct((hidden, wide), F32),
            jax.ShapeDtypeStruct((wide, hidden), F32),
            jax.ShapeDtypeStruct((3, wide, width), F32),
            jax.ShapeDtypeStruct((width, wide), F32),
            jax.ShapeDtypeStruct((valid, wide), BF16),
            jax.ShapeDtypeStruct((valid, wide), BF16),
        ],
        in_specs=[part] * 3 + [block] * 2,
        out_specs=[
            by_rows(hidden, wide),
            by_rows(wide, hidden),
            pl.BlockSpec((3, wide, width // RS), lambda p: (0, 0, p)),
            by_rows(width, wide),
            block,
            block,
        ],
        compiler_params=pltpu.CompilerParams(vmem_limit_bytes=60 * 2**20),
        name="finish",
    )(down_sum, up_sum, late_sum, output, grad_frames)


def on_device(
    sizes,
    frames,
    languages,
    present,
    lang_table,
    norm1_gain,
    norm1_shift,
    qkv_weight,
    qkv_bias,
    out_weight,
    out_bias,
    norm2_gain,
    norm2_shift,
    up_weight,
    up_bias,
    down_weight,
    down_bias,
    grad_out,
):
    d, t, s = (lax.axis_index(name) for name in AXES)
    home = d % 2 == t
    clips = sizes["dp"]
    _, valid, width = frames.shape
    rows = -(-valid // 256) * 256
    head_width = qkv_weight.shape[2]
    langs = lang_table.shape[0]
    pad = ((0, rows - valid), (0, 0))

    one_hot = (languages[:, None] == lax.broadcasted_iota(jnp.int32, (1, langs), 1)).astype(F32)
    embedding = jnp.dot(one_hot, lang_table.astype(F32), precision=lax.Precision.HIGHEST)
    lane = lax.broadcasted_iota(jnp.int32, (1, width), 1)
    once = jnp.where(s == 0, languages[:, None].astype(F32), 0.0)
    info = jnp.concatenate(
        [
            embedding,
            jnp.broadcast_to(present[:, None].astype(F32), (1, width)),
            jnp.where(lane == d, once, 0.0),
            jnp.zeros((5, width), F32),
        ]
    )
    biases = jnp.concatenate([qkv_bias.reshape(1, width), up_bias.reshape(-1, width)]).astype(F32)
    vectors = jnp.stack(
        [norm1_gain, norm2_gain, norm2_shift, out_bias, down_bias, norm1_shift, out_bias, out_bias]
    )
    b = layer(
        clips,
        valid,
        dict(
            frames_local=jnp.pad(frames[0], pad),
            grad_local=jnp.pad(grad_out[0], pad),
            info_local=info,
            bias_local=jnp.pad(biases, ((0, 8 - biases.shape[0]), (0, 0))),
            vectors=vectors.astype(F32),
            qkv_local=qkv_weight,
            up_local=up_weight,
            down_local=down_weight,
            out_local=out_weight,
        ),
    )
    v = b.pack[clips:]
    tail = jnp.where(home, v, b.pack_tail)
    down, up, qkv, out, output, grad_frames = finish(
        valid, head_width, b.down_sum, b.up_sum, b.late_sum, b.output, b.grad_frames
    )
    ids = v[9, :clips][:, None]
    hot = (ids == lax.broadcasted_iota(jnp.int32, (1, langs), 1).astype(F32)).astype(F32)
    grad_lang_table = lax.dot_general(
        hot, b.pack[:clips], (((0,), (0,)), ((), ())), precision=lax.Precision.HIGHEST
    )
    return (
        output[None],
        grad_frames[None],
        grad_lang_table,
        v[0],
        v[1],
        qkv,
        tail[6].reshape(2, head_width),
        out,
        v[2],
        v[3],
        v[4],
        up,
        tail[7:9].reshape(-1),
        down,
        v[5],
    )


def solution(mesh):
    rows = P("dp", "seq", None)
    columns, one = P(None, "tensor"), P("dp")
    placed = (
        rows,
        one,
        one,
        P(),
        P(),
        P(),
        P(None, None, "tensor"),
        columns,
        P("tensor", None),
        P(),
        P(),
        P(),
        columns,
        P("tensor"),
        P("tensor", None),
        P(),
        rows,
    )
    out = (
        rows,
        rows,
        P(),
        P(),
        P(),
        P(None, None, "tensor"),
        columns,
        P("tensor", None),
        P(),
        P(),
        P(),
        columns,
        P("tensor"),
        P("tensor", None),
        P(),
    )
    return jax.shard_map(
        functools.partial(on_device, dict(mesh.shape)),
        mesh=mesh,
        in_specs=placed,
        out_specs=out,
        check_vma=False,
    )
```

```python
import functools
import types

import jax
import jax.numpy as jnp
from jax import lax
from jax.experimental import pallas as pl
from jax.experimental.pallas import tpu as pltpu
from jax.sharding import PartitionSpec as P

HEAD = 64
EPSILON = 1e-05
QUERY_SCALE = 0.125
AXES = ("dp", "tensor", "seq")
F32 = jnp.float32
BF16 = jnp.bfloat16
NN = (((1,), (0,)), ((), ()))
NT = (((1,), (1,)), ((), ()))
TN = (((0,), (0,)), ((), ()))
VMEM = pl.BlockSpec(memory_space=pltpu.VMEM)
ANY = pl.BlockSpec(memory_space=pl.ANY)
RS = 3


ORDERS = (
    (0, 1, 2),
    (2, 1, 0),
    (2, 1, 0),
    (1, 2, 0),
    (1, 2, 0),
    (1, 2, 0),
    (1, 2, 0),
    (1, 2, 0),
    (1, 2, 0),
    (2, 1, 0),
    (1, 2, 0),
    (2, 1, 0),
    (1, 0, 2),
    (2, 1, 0),
    (1, 2, 0),
)
SCHEDULE = (
    (),
    (),
    (),
    (),
    (),
    (1, 0, 3),
    (),
    (),
    (4, 2, 3),
    (),
    (),
    (5, 4),
    (1,),
    (),
    (),
    (0, 5, 3, 2, 6, 0, 3, 7, 6),
    (8,),
    (4, 0, 7),
    (),
    (1,),
    (8,),
    (),
    (5,),
    (4, 9, 10),
    (1, 2),
    (11,),
    (0, 3, 5, 12, 6, 7, 13, 14, 10, 8, 9, 11, 3, 14, 0, 13, 4, 3, 4, 1, 2, 4),
    (5, 1, 12, 10),
    (9, 6, 11, 5, 7, 14, 8, 10, 9, 11, 14, 1, 0, 12, 13),
    (2, 5, 6, 12, 7, 13, 8, 10, 9, 11, 14),
    (6, 12, 2, 7, 13, 8, 9, 10, 11, 14, 12, 6, 7, 13, 2, 8, 9, 10, 11, 14, 13, 12),
)


def dg(left, right, dims):
    return lax.dot_general(left, right, dims, preferred_element_type=F32)


def rows_at(start, size):
    return pl.ds(pl.multiple_of(start, 16), size)


class Place:
    def __init__(self, dp):
        self.d, self.t, self.s = (lax.axis_index(name) for name in AXES)
        self.core = lax.rem(self.d, 2)
        self.home = self.core == self.t
        self.away = jnp.logical_not(self.home)
        self.clip = self.d - self.core + self.t
        self.sibling = (self.d + 1 - 2 * self.core, self.t, self.s)
        self.across = (self.d, 1 - self.t, self.s)
        self.level = [((self.d, self.t, 1 - self.s), self.s)]
        bit = 2
        while bit < dp:
            value = lax.rem(self.d // bit, 2)
            self.level.append(((self.d + bit - 2 * bit * value, self.t, self.s), value))
            bit *= 2
        self.peers = [self.sibling, self.across] + [to for to, _ in self.level]

    def enter(self):
        barrier = pltpu.get_barrier_semaphore()
        for to in self.peers:
            pl.semaphore_signal(barrier, inc=1, device_id=to, device_id_type=pl.DeviceIdType.MESH)
        pl.semaphore_wait(barrier, len(self.peers))

    def order(self, numbers):
        levels = [self.level[i] for i in numbers]
        return [to for to, _ in levels], [bit for _, bit in levels]


class Wires:
    def __init__(self, send_sems, recv_sems):
        self.send_sems, self.recv_sems, self.used = send_sems, recv_sems, 0

    def copy(self, src, dst, to):
        i = self.used
        self.used += 1
        return pltpu.make_async_remote_copy(
            src_ref=src,
            dst_ref=dst,
            send_sem=self.send_sems.at[i],
            recv_sem=self.recv_sems.at[i],
            device_id=to,
            device_id_type=pl.DeviceIdType.MESH,
        )


class Fetch:
    def __init__(self, place, wires, order, local, result):
        self.to, self.bits = place.order(order)
        self.place, self.wires, self.result = place, wires, result
        self.slice = local.shape[0] // 2**RS
        self.at = self.slice * (4 * self.bits[0] + 2 * self.bits[1] + self.bits[2])
        at = rows_at(self.at, self.slice)
        self.crossing = wires.copy(local.at[at], result.at[at], place.across)

        @pl.when(place.home)
        def _():
            self.crossing.start()

    def widen(self, j):
        size = self.slice * 2 ** (RS - 1 - j)
        ref = self.result.at[rows_at(self.at, size)]
        self.at = self.at - self.bits[j] * size
        return self.wires.copy(ref, ref, self.to[j])

    def arrive(self):
        self.moving = self.widen(RS - 1)

        @pl.when(self.place.home)
        def _():
            self.crossing.wait_send()

        @pl.when(self.place.away)
        def _():
            self.crossing.wait_recv()
            self.moving.start()

    def double(self, j):
        before = self.moving
        if j:
            self.moving = self.widen(j - 1)

        @pl.when(self.place.away)
        def _():
            before.wait()
            if j:
                self.moving.start()


class Reduction:
    def __init__(self, place, wires, order, kept, land, more, stage, result, sem):
        self.to, self.bits = place.order(order)
        self.place, self.wires, self.stage, self.result = place, wires, stage, result
        self.kept, self.land_ref = kept, land
        self.extra = list(zip(place.level[RS:], more))
        self.local = lambda src, dst: pltpu.make_async_copy(src, dst, sem)
        self.steps = [
            functools.partial(self.halve, 0),
            functools.partial(self.halve, 1),
            self.cross,
            self.land,
            functools.partial(self.double, 2),
            functools.partial(self.double, 1),
            functools.partial(self.double, 0),
        ]
        self.slice = result.shape[0] // 2**RS
        self.low = 0
        self.at = self.bits[0] * 4 * self.slice
        self.forwards = []
        sizes = [4, 2, 1, 1]
        starts = [sum(sizes[:i]) for i in range(4)]
        self.lands = [
            self.land_ref.at[pl.ds(start * self.slice, size * self.slice)]
            for start, size in zip(starts, sizes)
        ]
        self.last = stage.at[pl.ds(3 * self.slice, self.slice)]

    def start(self, total):
        half = 4 * self.slice
        bit = self.bits[0]
        self.stage[...] = total[rows_at((1 - bit) * half, half), :].astype(BF16)
        self.moving = self.wires.copy(self.stage, self.lands[0], self.to[0])
        self.moving.start()
        self.kept[...] = total[rows_at(bit * half, half), :]

    def halve(self, j):
        self.moving.wait()
        half = self.slice * 2 ** (RS - 2 - j)
        bit = self.bits[j + 1]
        away, home = (1 - bit) * half, bit * half
        stage = self.stage.at[pl.ds(0 if j == 0 else 2 * self.slice, half)]
        stage[...] = (
            self.kept[rows_at(self.low + away, half), :]
            + self.lands[j][rows_at(away, half), :].astype(F32)
        ).astype(BF16)
        self.moving = self.wires.copy(stage, self.lands[j + 1], self.to[j + 1])
        self.moving.start()
        self.kept[rows_at(self.low + home, half), :] += self.lands[j][
            rows_at(home, half), :
        ].astype(F32)
        self.low = self.low + home
        self.at = self.at + home

    def cross(self):
        self.moving.wait()
        now = rows_at(self.low, self.slice)
        self.kept[now, :] += self.lands[RS - 1][...].astype(F32)
        for (to, _), land in self.extra:
            self.last[...] = self.kept[now, :].astype(BF16)
            copy = self.wires.copy(self.last, land, to)
            copy.start()
            copy.wait()
            self.kept[now, :] = self.last[...].astype(F32) + land[...].astype(F32)
        self.crossing = self.wires.copy(self.last, self.lands[RS], self.place.across)

        @pl.when(self.place.away)
        def _():
            self.last[...] = self.kept[now, :].astype(BF16)
            self.crossing.start()

    def spread(self, src, start, size):
        ref = self.result.at[rows_at(start, size)]
        forward = self.wires.copy(ref if src is None else src, ref, self.place.sibling)
        self.forwards.append(forward)
        return forward

    def widen(self, src, j):
        ref = self.result.at[rows_at(self.at, self.slice * 2 ** (RS - 1 - j))]
        return self.wires.copy(ref if src is None else src, ref, self.to[j])

    def land(self):
        first = self.spread(self.last, self.at, self.slice)
        self.moving = self.widen(self.last, RS - 1)
        self.writing = self.local(self.last, self.result.at[rows_at(self.at, self.slice)])

        @pl.when(self.place.home)
        def _():
            self.crossing.wait_recv()
            self.last[...] = (
                self.kept[rows_at(self.low, self.slice), :] + self.lands[RS][...].astype(F32)
            ).astype(BF16)
            self.moving.start()
            first.start()
            self.writing.start()

        @pl.when(self.place.away)
        def _():
            self.crossing.wait_send()

    def double(self, j):
        size = self.slice * 2 ** (RS - 1 - j)
        bit = self.bits[j]
        came = self.at + (1 - 2 * bit) * size
        self.at = self.at - bit * size
        before, forward = self.moving, self.spread(None, came, size)
        if j:
            self.moving = self.widen(None, j - 1)

        @pl.when(self.place.home)
        def _():
            before.wait()
            if j == RS - 1:
                self.writing.wait()
            if j:
                self.moving.start()
            forward.start()

    def finish(self):
        @pl.when(self.place.home)
        def _():
            for forward in self.forwards:
                forward.wait_send()

        @pl.when(self.place.away)
        def _():
            for forward in self.forwards:
                forward.wait_recv()


def pair_lanes(rows):
    return lax.broadcasted_iota(jnp.int32, (rows, 128), 1)


def one_head(pair, e, extra=None):
    lane = pair_lanes(pair.shape[0])
    own = (lane < HEAD) if e == 0 else (lane >= HEAD)
    kept = jnp.where(own, pair, jnp.zeros_like(pair))
    if extra is not None:
        kept = jnp.where(lane == (HEAD if e == 0 else 0), extra, kept)
    return kept


def masked(r, e, part):
    return r.grad_pre.at[:, pl.ds((2 * e + part) * 128, 128)]


def mask_keys(r, columns, valid):
    rows = r.query.shape[0]
    row = lax.broadcasted_iota(jnp.int32, (rows, 128), 0)
    bias = jnp.where(row >= valid, -1e30, 0.0).astype(BF16)
    for e in range(2):
        for part in range(2):
            masked(r, e, part)[...] = one_head(r.key[pl.ds(part * rows, rows), columns], e, bias)


def centre(inputs):
    centred = inputs - jnp.mean(inputs, axis=1, keepdims=True)
    scale = lax.rsqrt(jnp.mean(centred * centred, axis=1, keepdims=True) + EPSILON)
    return centred * scale, scale


def call(kernel, name, collective, ins, outs, scratch, hbm, cost):
    names = list(ins) + list(outs) + list(scratch)

    def body(*refs):
        named = dict(zip(names, refs))
        plain = {name: ref for name, ref in named.items() if isinstance(name, str)}
        kernel(types.SimpleNamespace(table=named, **plain))

    results = pl.pallas_call(
        body,
        out_shape=[jax.ShapeDtypeStruct(*item) for item in outs.values()],
        in_specs=[ANY if item in hbm else VMEM for item in ins],
        out_specs=[ANY if item in hbm else VMEM for item in outs],
        scratch_shapes=list(scratch.values()),
        compiler_params=pltpu.CompilerParams(
            collective_id=collective,
            has_side_effects=collective is not None,
            vmem_limit_bytes=60 * 2**20,
        ),
        cost_estimate=cost,
        name=name,
    )(*ins.values())
    return types.SimpleNamespace(**dict(zip(outs, results)))


def attention_forward(place, wires, valid, r):
    rows, width = r.query.shape
    home, away = place.home, place.away
    chunk = rows // 3
    chunks = [pl.ds(c * chunk, chunk) for c in range(3)]
    gain, shift = r.vectors[0:1, :], r.vectors[5:6, :]

    def weight(j):
        return r.active.at[:, pl.ds(j * width, width)]

    light = ((1, 2, 0), (2, 1, 0), (1, 2, 0))
    turns = ((0, 1, 2), (1, 2, 0), (2, 0, 1))
    first = [Fetch(place, wires, light[j], r.qkv_local.at[j], weight(j)) for j in range(3)]
    info = wires.copy(r.info_local, r.info, place.sibling)
    bias = wires.copy(r.bias_local, r.bias, place.across)
    own = wires.copy(r.frames_local, r.frames, place.sibling)
    beside, onward = [], []
    for at in chunks:
        to = r.share_land.at[at]
        beside.append(wires.copy(r.frames_local.at[at], to, place.level[0][0]))
        onward.append(wires.copy(to, to, place.sibling))
    grads = wires.copy(r.grad_local, r.grad_rows, place.sibling)
    own_out = r.out.at[rows_at(place.core * width, width)]
    other_out = r.out.at[rows_at((1 - place.core) * width, width)]
    pairs_of = [(r.frames_local, r.frames)] + [(r.qkv_local.at[j], weight(j)) for j in range(3)]
    pairs_of += [(r.grad_local, r.grad_rows), (r.out_local, own_out)]
    pairs_of += [(r.up_local, r.up), (r.down_local, r.down)]
    keep = [
        pltpu.make_async_copy(src, dst, r.local_sems.at[i]) for i, (src, dst) in enumerate(pairs_of)
    ]
    lend = pltpu.make_async_copy(r.out_local, other_out, r.local_sems.at[len(keep)])
    lent = wires.copy(own_out, own_out, place.sibling)

    @pl.when(home)
    def _():
        own.start()
        for copy in beside:
            copy.start()
        info.start()
        bias.start()
        for copy in keep:
            copy.start()
        r.info[...] = r.info_local[...]
        r.bias[...] = r.bias_local[...]

    @pl.when(away)
    def _():
        lend.start()

    def fetch(local, result):
        size = local.shape[0] // RS
        cuts = [pl.ds(part * size, size) for part in range(RS)]
        return [
            Fetch(place, wires, turn, local.at[at], result.at[at]) for turn, at in zip(turns, cuts)
        ]

    later = fetch(r.out_local, own_out) + fetch(r.up_local, r.up) + fetch(r.down_local, r.down)

    @pl.when(home)
    def _():
        grads.start()

    for item in first:
        item.arrive()

    @pl.when(home)
    def _():
        keep[0].wait()

    @pl.when(away)
    def _():
        info.wait_recv()
        own.wait_recv()

    embedding = r.info[0:1, :]

    def norm(source, at, to):
        normal, _ = centre(source[at, :].astype(F32) + embedding)
        normed = normal * gain + shift
        to[at, :] = normed.astype(BF16)
        return normed

    for c, at in enumerate(chunks):
        r.normed_t[:, at] = norm(r.frames, at, r.normed2).T.astype(BF16)
        if c == 1:
            for item in first:
                item.double(2)

        @pl.when(home)
        def _():
            beside[c].wait()
            onward[c].start()

    for item in first:
        item.double(1)
    for c, at in enumerate(chunks):

        @pl.when(away)
        def _():
            onward[c].wait_recv()

        norm(r.share_land, at, r.stage)
    for item in first:
        item.double(0)
    for item in later:
        item.arrive()

    @pl.when(home)
    def _():
        for copy in keep[1:4]:
            copy.wait()

    @pl.when(away)
    def _():
        bias.wait_recv()

    r.query[...] = (
        (dg(r.normed2[...], weight(0)[...], NN) + r.bias[0:1, :width]) * QUERY_SCALE
    ).astype(BF16)
    for part, normed in enumerate((r.normed2, r.stage)):
        at = pl.ds(part * rows, rows)
        r.key[at, :] = dg(normed[...], weight(1)[...], NN).astype(BF16)
        r.value[at, :] = (dg(normed[...], weight(2)[...], NN) + r.bias[0:1, width:]).astype(BF16)
    for item in later:
        item.double(2)

    block = 256
    mixed_copies = []

    def one_pair(p):
        columns = pl.ds(p * 128, 128)
        whole = pl.ds(pl.multiple_of(place.core * width + p * 128, 128), 128)
        mask_keys(r, columns, valid)
        for j in range(3):
            r.qkv_pairs[p, :, j * 128 : (j + 1) * 128] = weight(j)[:, columns]

        def one_block(i, _):
            at = pl.ds(pl.multiple_of(i * block, block), block)
            parts, rests = [], []
            for e in range(2):
                queries = one_head(r.query[at, columns], e, jnp.ones((), BF16))
                scores = [dg(queries, masked(r, e, part)[...], NT) for part in range(2)]
                top = jnp.maximum(*(jnp.max(half, axis=1, keepdims=True) for half in scores))
                weights = [jnp.exp(half - top) for half in scores]
                total = sum(jnp.sum(half, axis=1, keepdims=True) for half in weights)
                scale = 1.0 / total
                near = rest = 0.0
                for part in range(2):
                    values = r.value[part * rows : (part + 1) * rows, columns]
                    exact = weights[part] * scale
                    low = exact.astype(BF16)
                    near = near + dg(low, values, NN)
                    rest = rest + dg((exact - low.astype(F32)).astype(BF16), values, NN)
                parts.append(near)
                rests.append(rest)
                r.lse[pl.ds(2 * p + e, 1), at] = (top + jnp.log(total)).reshape(1, block)
            first = pair_lanes(block) < HEAD
            mixed = jnp.where(first, parts[0], parts[1])
            low = mixed.astype(BF16)
            r.mixed[at, whole] = low
            rest = mixed - low.astype(F32) + jnp.where(first, rests[0], rests[1])
            r.mixed_rest[at, columns] = rest.astype(BF16)
            return 0

        lax.fori_loop(0, rows // block, one_block, 0)
        copy = wires.copy(r.mixed.at[:, whole], r.mixed.at[:, whole], place.sibling)
        copy.start()
        mixed_copies.append(copy)

    one_pair(0)
    for item in later:
        item.double(1)
    one_pair(1)
    for item in later[:RS]:
        item.double(0)

    @pl.when(away)
    def _():
        lent.start()
        lend.wait()
        grads.wait_recv()

    one_pair(2)
    for item in later[RS:]:
        item.double(0)

    @pl.when(away)
    def _():
        lent.wait_send()

    @pl.when(home)
    def _():
        lent.wait_recv()
        for copy in keep[4:]:
            copy.wait()
        info.wait_send()
        bias.wait_send()
        own.wait_send()
        grads.wait_send()
        for copy in onward:
            copy.wait_send()

    for at in chunks:
        r.grad_rows[at, :] = (r.grad_rows[at, :].astype(F32) * r.info[1:2, :]).astype(BF16)
    for copy in mixed_copies:
        copy.wait()


def gelu_pair(inputs):
    half = 0.5 + 0.5 * lax.erf(inputs * 0.7071067811865476)
    slope = inputs * (jnp.exp(inputs * inputs * -0.5) * 0.3989422804014327)
    return inputs * half, half + slope


def layer_kernel(dp, valid, r):
    place = Place(dp)
    place.enter()
    wires = Wires(r.send_sems, r.recv_sems)
    attention_forward(place, wires, valid, r)
    rows, width = r.query.shape
    wide = r.normed_t.shape[0]
    hidden = r.up.shape[1]
    home, away = place.home, place.away
    chunk = rows // 3
    chunks = [pl.ds(c * chunk, chunk) for c in range(3)]
    embedding, keep = r.info[0:1, :], r.info[1:2, :]
    gain_one, gain_two, shift_two, out_bias, down_bias = (r.vectors[i : i + 1, :] for i in range(5))
    zero = jnp.zeros((1, wide), F32)

    for at in chunks:
        attention = dg(r.mixed[at, :], r.out[...], NN)
        rows_in = r.frames[at, :].astype(F32) + embedding + attention + out_bias
        r.hidden[at, :] = rows_in
        normal, _ = centre(rows_in)
        r.normed2[at, :] = (normal * gain_two + shift_two).astype(BF16)

    block = 512
    up_sums = [jnp.zeros((1, block), F32) for _ in range(hidden // block)]
    for at in chunks:
        for h in range(hidden // block):
            units = pl.ds(h * block, block)
            start = h * block
            bias = r.bias[1 + start // wide : 2 + start // wide, start % wide : start % wide + block]
            if start % wide + block > wide:
                bias = jnp.concatenate(
                    [
                        r.bias[1 + start // wide : 2 + start // wide, start % wide :],
                        r.bias[2 + start // wide : 3 + start // wide, : start % wide + block - wide],
                    ],
                    axis=1,
                )
            active, slope = gelu_pair(dg(r.normed2[at, :], r.up[:, units], NN) + bias)
            r.active[at, units] = active.astype(BF16)
            grad = dg(r.grad_rows[at, :], r.down[units, :], NT)
            low = (grad * slope).astype(BF16)
            r.grad_pre[at, units] = low
            up_sums[h] = up_sums[h] + jnp.sum(low.astype(F32), axis=0, keepdims=True)
    norm_copies, feed_copies = [], []
    for at in chunks:
        r.norm_stage[at, :] = dg(r.grad_pre[at, :], r.up[...], NT)
        copy = wires.copy(r.norm_stage.at[at], r.norm_land.at[at], place.sibling)
        copy.start()
        norm_copies.append(copy)
    for at in chunks:
        r.stage[at, :] = dg(r.active[at, :], r.down[...], NN).astype(BF16)
        copy = wires.copy(r.stage.at[at], r.feed_land.at[at], place.sibling)
        copy.start()
        feed_copies.append(copy)

    parts = []

    def reduction(slot, cut, stage, result):
        number = len(parts)
        views = [ref.at[:, cut] for ref in (r.kept.at[slot], r.land.at[slot])]
        more = [r.more_land.at[slot, i].at[:, cut] for i in range(len(place.level) - RS)]
        item = Reduction(
            place,
            wires,
            ORDERS[number],
            *views,
            more,
            stage.at[:, cut],
            result.at[:, cut],
            r.part_sems.at[number],
        )
        item.start(r.total.at[:, cut])
        parts.append(item)

    groups = iter(SCHEDULE)

    def tick():
        for number in next(groups):
            parts[number].steps.pop(0)()

    every = pl.ds(0, wide)
    for p in range(RS):
        columns = pl.ds(p * block, block)
        r.total[...] = dg(r.active[:, columns], r.grad_rows[...], TN)
        reduction(p, every, r.part_stage.at[p], r.down_sum.at[p])
    for p in range(RS):
        columns = pl.ds(p * chunk, chunk)
        outer = dg(r.normed2[:, columns], r.grad_pre[...], TN)
        r.total[:chunk, :] = outer[:, :wide]
        r.total[chunk:, :] = outer[:, wide:]
        reduction(RS + p, every, r.part_stage.at[RS + p], r.up_sum.at[p])

    grad_gain_two = grad_shift_two = grad_out_bias = grad_down_bias = zero
    for c, at in enumerate(chunks):
        tick()
        norm_copies[c].wait()
        feed_copies[c].wait()
        rows_in = r.hidden[at, :]
        normal, scale = centre(rows_in)
        feed = r.stage[at, :].astype(F32) + r.feed_land[at, :].astype(F32)
        r.stage[at, :] = (keep * (rows_in + feed + down_bias)).astype(BF16)
        grad = r.norm_stage[at, :] + r.norm_land[at, :]
        grad_shift_two = grad_shift_two + jnp.sum(grad, axis=0, keepdims=True)
        grad_gain_two = grad_gain_two + jnp.sum(grad * normal, axis=0, keepdims=True)
        grad = grad * gain_two
        grad = (
            grad
            - jnp.mean(grad, axis=1, keepdims=True)
            - normal * jnp.mean(grad * normal, axis=1, keepdims=True)
        ) * scale
        grad_out = r.grad_rows[at, :].astype(F32)
        grad_down_bias = grad_down_bias + jnp.sum(grad_out, axis=0, keepdims=True)
        grad = grad + grad_out
        grad_out_bias = grad_out_bias + jnp.sum(grad, axis=0, keepdims=True)
        r.hidden[at, :] = grad
        low = grad.astype(BF16)
        r.grad_attn[at, :] = low
        r.grad_mixed[at, :] = dg(low, r.out[rows_at(place.core * width, width), :], NT).astype(BF16)
    out_copy = wires.copy(r.stage, r.output, place.across)
    out_keep = pltpu.make_async_copy(r.stage, r.output, r.local_sems.at[0])

    @pl.when(home)
    def _():
        out_copy.start()
        out_keep.start()

    def operand(i):
        return r.grad_pre.at[:, pl.ds((4 + i) * 128, 128)]

    def kv(ref, p):
        return ref.at[:, pl.ds(p * 256, 256)]

    def whole(p):
        return pl.ds(pl.multiple_of(place.core * width + p * 128, 128), 128)

    def prepare(p):
        columns = pl.ds(p * 128, 128)
        grad = r.grad_mixed[:, columns]
        product = grad.astype(F32) * (
            r.mixed[:, whole(p)].astype(F32) + r.mixed_rest[:, columns].astype(F32)
        )
        query = r.query[:, columns]
        lane = pair_lanes(rows)
        mask_keys(r, columns, valid)
        for e in range(2):
            operand(e)[...] = one_head(query, e, jnp.ones((), BF16))
            operand(2 + e)[...] = one_head(query, e)
            operand(4 + e)[...] = one_head(grad, e)
            own = (lane < HEAD) if e == 0 else (lane >= HEAD)
            r.inner[e : e + 1, :] = jnp.sum(
                jnp.where(own, product, 0.0), axis=1, keepdims=True
            ).reshape(1, rows)

    def back_half(p, part, total):
        columns = pl.ds(p * 128, 128)
        size = 384
        store = kv(r.norm_stage if part == 0 else r.normed2, p)

        def one_block(i, total):
            at = pl.ds(pl.multiple_of(i * size, size), size)
            from_all = pl.ds(pl.multiple_of(part * rows + i * size, size), size)
            grad_keys, grad_values = [], []
            for e in range(2):
                scores = dg(masked(r, e, part)[at, :], operand(e)[...], NT)
                weights = jnp.exp(scores - r.lse[2 * p + e : 2 * p + e + 1, :])
                grad_weights = dg(r.value[from_all, columns], operand(4 + e)[...], NT)
                grad_scores = (weights * (grad_weights - r.inner[e : e + 1, :])).astype(BF16)
                grad_values.append(dg(weights.astype(BF16), operand(4 + e)[...], NN))
                grad_keys.append(dg(grad_scores, operand(2 + e)[...], NN))
                total = total + dg(one_head(r.key[from_all, columns], e), grad_scores, TN)
            store[at, :128] = (grad_keys[0] + grad_keys[1]).astype(store.dtype)
            store[at, 128:] = (grad_values[0] + grad_values[1]).astype(store.dtype)
            return total

        return lax.fori_loop(0, rows // size, one_block, total)

    def send_kv(p):
        copy = wires.copy(kv(r.normed2, p), kv(r.kv_land, p), place.level[0][0])
        copy.start()
        return copy

    def stacked(p):
        return r.active.at[:, pl.ds(p * 384, 384)]

    def end_queries(p, total):
        low = total.T.astype(BF16)
        stacked(p)[:, :128] = (low.astype(F32) * QUERY_SCALE).astype(BF16)

    def after_pair(p, copy):
        copy.wait()
        mine = stacked(p)
        mine[:, 128:] = (kv(r.norm_stage, p)[...] + kv(r.kv_land, p)[...].astype(F32)).astype(BF16)
        grads = mine[...]
        share = dg(grads, r.qkv_pairs[p], NT)
        if p == 0:
            r.norm_land[...] = share
        else:
            r.norm_land[...] += share

    def weigh_pair(p):
        grads = stacked(p)[...]
        outer = dg(r.normed_t[...], grads, NN)
        half = wide // 2
        r.total[:half, :half] = outer[:half, :]
        r.total[:half, half:] = outer[half:, :]
        r.total[half:, :] = dg(r.mixed[:, whole(p)], r.grad_attn[...], TN)
        for q in range(3):
            stage = r.down.at[pl.ds(p * 256, 256)]
            reduction(2 * RS + p, pl.ds(q * 256, 256), stage, r.late_sum.at[p])
        sums = jnp.sum(grads.astype(F32), axis=0, keepdims=True)
        r.bias_row[:, p * 128 : (p + 1) * 128] = sums[:, :128]
        r.bias_row[:, width + p * 128 : width + (p + 1) * 128] = sums[:, 256:]

    none = jnp.zeros((128, rows), F32)
    kv_copies = {}

    def others(p):
        tick()
        prepare(p)
        tick()
        total = back_half(p, 1, none)
        kv_copies[p] = send_kv(p)
        return total

    def owns(p, total):
        tick()
        end_queries(p, back_half(p, 0, total))

    def end_pair(p):
        tick()
        after_pair(p, kv_copies[p])
        tick()
        weigh_pair(p)

    owns(0, others(0))
    held = others(2)
    owns(1, others(1))
    end_pair(0)
    tick()
    prepare(2)
    owns(2, held)
    end_pair(1)
    tick()
    after_pair(2, kv_copies[2])

    @pl.when(home)
    def _():
        out_copy.wait_send()
        out_keep.wait()

    @pl.when(away)
    def _():
        out_copy.wait_recv()

    share_copies = []
    for at in chunks:
        tick()
        r.stage[at, :] = r.norm_land[at, :].astype(BF16)
        copy = wires.copy(r.stage.at[at], r.share_land.at[at], place.sibling)
        copy.start()
        share_copies.append(copy)
    tick()
    weigh_pair(2)

    grad_gain = grad_shift = grad_stream_sum = zero
    frame_copies = []
    for c, at in enumerate(chunks):
        tick()
        share_copies[c].wait()
        normal, scale = centre(r.frames[at, :].astype(F32) + embedding)
        grad = r.stage[at, :].astype(F32) + r.share_land[at, :].astype(F32)
        grad_shift = grad_shift + jnp.sum(grad, axis=0, keepdims=True)
        grad_gain = grad_gain + jnp.sum(grad * normal, axis=0, keepdims=True)
        grad = grad * gain_one
        grad = (
            grad
            - jnp.mean(grad, axis=1, keepdims=True)
            - normal * jnp.mean(grad * normal, axis=1, keepdims=True)
        ) * scale + r.hidden[at, :]
        grad_stream_sum = grad_stream_sum + jnp.sum(grad, axis=0, keepdims=True)
        r.normed2[at, :] = grad.astype(BF16)
        frame_copy = wires.copy(r.normed2.at[at], r.grad_frames.at[at], place.across)
        frame_keep = pltpu.make_async_copy(
            r.normed2.at[at], r.grad_frames.at[at], r.local_sems.at[1 + c]
        )
        frame_copies.append((frame_copy, frame_keep))

        @pl.when(home)
        def _():
            frame_copy.start()
            frame_keep.start()

    tick()
    pack = r.pack
    row = lax.broadcasted_iota(jnp.int32, (dp, wide), 0)
    pack[:dp, :] = jnp.where(row == place.clip, grad_stream_sum, 0.0)
    up_sum = jnp.concatenate(up_sums, axis=1)
    items = [
        grad_gain,
        grad_shift,
        grad_out_bias,
        grad_gain_two,
        grad_shift_two,
        grad_down_bias,
        r.bias_row[...],
    ]
    items += [up_sum[:, i * wide : (i + 1) * wide] for i in range(hidden // wide)]
    items.append(r.info[2:3, :])
    row = lax.broadcasted_iota(jnp.int32, (16, wide), 0)
    table = jnp.zeros((16, wide), F32)
    for i, item in enumerate(items):
        table = table + jnp.where(row == i, item, 0.0)
    pack[dp:, :] = table
    steps = [to for to, _ in place.level] + [place.across]
    for i, to in enumerate(steps):
        r.pack_stage[...] = pack[...]
        copy = wires.copy(r.pack_stage, r.pack_land.at[i], to)
        copy.start()
        if i < 3 or i == len(steps) - 1:
            tick()
        copy.wait()
        pack[...] += r.pack_land[i]
    tail_copy = wires.copy(pack.at[pl.ds(dp, 16)], r.pack_tail, place.sibling)
    tail_copy.start()
    tick()
    tail_copy.wait()

    @pl.when(home)
    def _():
        for copy, local in frame_copies:
            copy.wait_send()
            local.wait()

    @pl.when(away)
    def _():
        for copy, _ in frame_copies:
            copy.wait_recv()

    for item in parts:
        item.finish()


def levels_of(dp):
    levels = 1
    while 2**levels < dp:
        levels += 1
    return levels


def layer(dp, valid, ins):
    rows, wide = ins["frames_local"].shape
    width = ins["qkv_local"].shape[2]
    hidden = ins["up_local"].shape[1]
    levels = levels_of(dp)
    extra = levels - RS
    part = (2 * wide * hidden // (2 * RS * wide), wide)
    half = (part[0] // 2, wide)
    outs = dict(
        output=((rows, wide), BF16),
        grad_frames=((rows, wide), BF16),
        down_sum=((RS,) + part, BF16),
        up_sum=((RS,) + part, BF16),
        late_sum=((RS,) + part, BF16),
        pack=((dp + 16, wide), F32),
        pack_tail=((16, wide), F32),
    )
    wires = 4 * RS * (1 + RS) + 3 + 6 + 1 + 1 + 3
    wires += 15 * (2 * RS + 2 + RS + extra) + 3 + 3 + 1 + 3 + 3 + 3 + levels + 1 + 1
    square = (rows, wide)
    scratch = dict(
        frames=pltpu.VMEM(square, BF16),
        grad_rows=pltpu.VMEM(square, BF16),
        info=pltpu.VMEM((8, wide), F32),
        bias=pltpu.VMEM((8, wide), F32),
        normed_t=pltpu.VMEM((wide, rows), BF16),
        query=pltpu.VMEM((rows, width), BF16),
        key=pltpu.VMEM((2 * rows, width), BF16),
        value=pltpu.VMEM((2 * rows, width), BF16),
        lse=pltpu.VMEM((8, rows), F32),
        mixed=pltpu.VMEM(square, BF16),
        mixed_rest=pltpu.VMEM((rows, width), BF16),
        qkv_pairs=pltpu.VMEM((width // 128, wide, 384), BF16),
        out=pltpu.VMEM((wide, wide), BF16),
        up=pltpu.VMEM((wide, hidden), BF16),
        down=pltpu.VMEM((hidden, wide), BF16),
        hidden=pltpu.VMEM(square, F32),
        normed2=pltpu.VMEM(square, BF16),
        active=pltpu.VMEM((rows, hidden), BF16),
        grad_pre=pltpu.VMEM((rows, hidden), BF16),
        grad_attn=pltpu.VMEM(square, BF16),
        grad_mixed=pltpu.VMEM((rows, width), BF16),
        inner=pltpu.VMEM((8, rows), F32),
        norm_stage=pltpu.VMEM(square, F32),
        norm_land=pltpu.VMEM(square, F32),
        stage=pltpu.VMEM(square, BF16),
        feed_land=pltpu.VMEM(square, BF16),
        share_land=pltpu.VMEM(square, BF16),
        kv_land=pltpu.VMEM(square, BF16),
        total=pltpu.VMEM(part, F32),
        kept=pltpu.VMEM((9,) + half, F32),
        land=pltpu.VMEM((9,) + part, BF16),
        part_stage=pltpu.VMEM((6,) + half, BF16),
        bias_row=pltpu.VMEM((1, 2 * width), F32),
        pack_stage=pltpu.VMEM((dp + 16, wide), F32),
        pack_land=pltpu.VMEM((levels + 1, dp + 16, wide), F32),
        send_sems=pltpu.SemaphoreType.DMA((wires,)),
        recv_sems=pltpu.SemaphoreType.DMA((wires,)),
        part_sems=pltpu.SemaphoreType.DMA((15,)),
        local_sems=pltpu.SemaphoreType.DMA((9,)),
    )
    if extra:
        scratch.update(more_land=pltpu.VMEM((9, extra, part[0] // 8, wide), BF16))
    cost = pl.CostEstimate(flops=3 * 10**10, bytes_accessed=10**8, transcendentals=2 * 10**7)
    kernel = functools.partial(layer_kernel, dp, valid)
    hbm = ("frames_local", "grad_local", "qkv_local", "up_local", "down_local", "out_local")
    hbm += ("output", "grad_frames", "down_sum", "up_sum", "late_sum")
    return call(kernel, "layer", 1, ins, outs, scratch, hbm, cost)


def finish_kernel(down_sum, up_sum, late_sum, rows_a, rows_b, down, up, qkv, out, out_a, out_b):
    wide = down.shape[1]
    half = wide // 2
    chunk = up.shape[0]
    down[...] = down_sum[0].astype(F32)
    for i in range(up.shape[1] // wide):
        up[:, i * wide : (i + 1) * wide] = up_sum[0, i * chunk : (i + 1) * chunk, :].astype(F32)
    for j in range(3):
        for i in range(2):
            columns = pl.ds(i * half + j * 128, 128)
            qkv[j, i * half : (i + 1) * half, :] = late_sum[0, :half, columns].astype(F32)
    out[...] = late_sum[0, half:, :].astype(F32)
    out_a[...] = rows_a[...]
    out_b[...] = rows_b[...]


def finish(valid, width, down_sum, up_sum, late_sum, output, grad_frames):
    rows, wide = output.shape
    hidden = down_sum.shape[1] * RS
    part = pl.BlockSpec((1,) + down_sum.shape[1:], lambda p: (p, 0, 0))
    block = pl.BlockSpec((rows // RS, wide), lambda p: (p, 0))

    def by_rows(height, columns):
        return pl.BlockSpec((height // RS, columns), lambda p: (p, 0))

    return pl.pallas_call(
        finish_kernel,
        grid=(RS,),
        out_shape=[
            jax.ShapeDtypeStruct((hidden, wide), F32),
            jax.ShapeDtypeStruct((wide, hidden), F32),
            jax.ShapeDtypeStruct((3, wide, width), F32),
            jax.ShapeDtypeStruct((width, wide), F32),
            jax.ShapeDtypeStruct((valid, wide), BF16),
            jax.ShapeDtypeStruct((valid, wide), BF16),
        ],
        in_specs=[part] * 3 + [block] * 2,
        out_specs=[
            by_rows(hidden, wide),
            by_rows(wide, hidden),
            pl.BlockSpec((3, wide, width // RS), lambda p: (0, 0, p)),
            by_rows(width, wide),
            block,
            block,
        ],
        compiler_params=pltpu.CompilerParams(vmem_limit_bytes=60 * 2**20),
        name="finish",
    )(down_sum, up_sum, late_sum, output, grad_frames)


def on_device(
    sizes,
    frames,
    languages,
    present,
    lang_table,
    norm1_gain,
    norm1_shift,
    qkv_weight,
    qkv_bias,
    out_weight,
    out_bias,
    norm2_gain,
    norm2_shift,
    up_weight,
    up_bias,
    down_weight,
    down_bias,
    grad_out,
):
    d, t, s = (lax.axis_index(name) for name in AXES)
    home = d % 2 == t
    clips = sizes["dp"]
    _, valid, width = frames.shape
    rows = -(-valid // 256) * 256
    head_width = qkv_weight.shape[2]
    langs = lang_table.shape[0]
    pad = ((0, rows - valid), (0, 0))

    one_hot = (languages[:, None] == lax.broadcasted_iota(jnp.int32, (1, langs), 1)).astype(F32)
    embedding = jnp.dot(one_hot, lang_table.astype(F32), precision=lax.Precision.HIGHEST)
    lane = lax.broadcasted_iota(jnp.int32, (1, width), 1)
    once = jnp.where(s == 0, languages[:, None].astype(F32), 0.0)
    info = jnp.concatenate(
        [
            embedding,
            jnp.broadcast_to(present[:, None].astype(F32), (1, width)),
            jnp.where(lane == d, once, 0.0),
            jnp.zeros((5, width), F32),
        ]
    )
    biases = jnp.concatenate([qkv_bias.reshape(1, width), up_bias.reshape(-1, width)]).astype(F32)
    vectors = jnp.stack(
        [norm1_gain, norm2_gain, norm2_shift, out_bias, down_bias, norm1_shift, out_bias, out_bias]
    )
    b = layer(
        clips,
        valid,
        dict(
            frames_local=jnp.pad(frames[0], pad),
            grad_local=jnp.pad(grad_out[0], pad),
            info_local=info,
            bias_local=jnp.pad(biases, ((0, 8 - biases.shape[0]), (0, 0))),
            vectors=vectors.astype(F32),
            qkv_local=qkv_weight,
            up_local=up_weight,
            down_local=down_weight,
            out_local=out_weight,
        ),
    )
    v = b.pack[clips:]
    tail = jnp.where(home, v, b.pack_tail)
    down, up, qkv, out, output, grad_frames = finish(
        valid, head_width, b.down_sum, b.up_sum, b.late_sum, b.output, b.grad_frames
    )
    ids = v[9, :clips][:, None]
    hot = (ids == lax.broadcasted_iota(jnp.int32, (1, langs), 1).astype(F32)).astype(F32)
    grad_lang_table = lax.dot_general(
        hot, b.pack[:clips], (((0,), (0,)), ((), ())), precision=lax.Precision.HIGHEST
    )
    return (
        output[None],
        grad_frames[None],
        grad_lang_table,
        v[0],
        v[1],
        qkv,
        tail[6].reshape(2, head_width),
        out,
        v[2],
        v[3],
        v[4],
        up,
        tail[7:9].reshape(-1),
        down,
        v[5],
    )


def solution(mesh):
    rows = P("dp", "seq", None)
    columns, one = P(None, "tensor"), P("dp")
    placed = (
        rows,
        one,
        one,
        P(),
        P(),
        P(),
        P(None, None, "tensor"),
        columns,
        P("tensor", None),
        P(),
        P(),
        P(),
        columns,
        P("tensor"),
        P("tensor", None),
        P(),
        rows,
    )
    out = (
        rows,
        rows,
        P(),
        P(),
        P(),
        P(None, None, "tensor"),
        columns,
        P("tensor", None),
        P(),
        P(),
        P(),
        columns,
        P("tensor"),
        P("tensor", None),
        P(),
    )
    return jax.shard_map(
        functools.partial(on_device, dict(mesh.shape)),
        mesh=mesh,
        in_specs=placed,
        out_specs=out,
        check_vma=False,
    )
```
